128 devices in a mesh: dp: 32 (over x, z, y_lo), seq: 4 (over y_hi, core).
Axes of the slice: x: 4, y: 4 (y_hi: 2, y_lo: 2; y = y_hi * 2 + y_lo), z: 4, core: 2. Of those that a mesh axis runs over, the one named last changes fastest.
Arguments:
- tokens: bfloat16 [32, 1024, 1024], P('dp', 'seq'), may hold values from -6 to 6
- memory: bfloat16 [32, 1024, 1024], P('dp', 'seq'), may hold values from -6 to 6
- cotangent: bfloat16 [32, 1024, 1024], P('dp', 'seq'), may hold values from -12 to 12
- mem_len: int32 [32], P('dp'), may hold values from 0 to 1024, as said below
- value_route: int32 [32, 2, 1024, 4, 2], P('dp', None, 'seq'), may hold values from 0 to 4, all different within a row
- output_route: int32 [32, 1024, 4, 2], P('dp', 'seq'), may hold values from 0 to 4, all different within a row
- attn_norm_gain: bfloat16 [1024], replicated, may hold values from 0.5 to 1.5
- attn_norm_bias: bfloat16 [1024], replicated, may hold values from -1.25 to 1.25
- query_weight: bfloat16 [1024, 448], replicated, may hold values from -0.1875 to 0.1875
- key_weight: bfloat16 [1024, 448], replicated, may hold values from -0.1875 to 0.1875
- rel_weight: bfloat16 [1024, 448], replicated, may hold values from -0.1875 to 0.1875
- bias_u: bfloat16 [448], replicated, may hold values from -3 to 3
- bias_v: bfloat16 [448], replicated, may hold values from -3 to 3
- value_router: bfloat16 [1024, 20], replicated, may hold values from -0.09375 to 0.09375
- value_weight: bfloat16 [1024, 2240], replicated, may hold values from -0.1875 to 0.1875
- out_router: bfloat16 [1024, 20], replicated, may hold values from -0.09375 to 0.09375
- out_weight: bfloat16 [2240, 1024], replicated, may hold values from -3 to 3
- ffn_norm_gain: bfloat16 [1024], replicated, may hold values from 0.5 to 1.5
- ffn_norm_bias: bfloat16 [1024], replicated, may hold values from -1.25 to 1.25
- up_weight: bfloat16 [1024, 4096], replicated, may hold values from -0.1875 to 0.1875
- up_bias: bfloat16 [4096], replicated, may hold values from -1.25 to 1.25
- down_weight: bfloat16 [4096, 1024], replicated, may hold values from -0.09375 to 0.09375
- down_bias: bfloat16 [1024], replicated, may hold values from -1.25 to 1.25
Outputs:
- result: bfloat16 [32, 1024, 1024], P('dp', 'seq')
- grad_tokens: float32 [32, 1024, 1024], P('dp', 'seq')
- grad_attn_norm_gain: float32 [1024], P(('dp', 'seq'))
- grad_attn_norm_bias: float32 [1024], P(('dp', 'seq'))
- grad_query_weight: float32 [1024, 448], P(('dp', 'seq'))
- grad_key_weight: float32 [1024, 448], P(('dp', 'seq'))
- grad_rel_weight: float32 [1024, 448], P(('dp', 'seq'))
- grad_bias_u: float32 [448], replicated
- grad_bias_v: float32 [448], replicated
- grad_value_router: float32 [1024, 20], P(('dp', 'seq'))
- grad_value_weight: float32 [1024, 2240], P(('dp', 'seq'))
- grad_out_router: float32 [1024, 20], P(('dp', 'seq'))
- grad_out_weight: float32 [2240, 1024], P(None, ('dp', 'seq'))
- grad_ffn_norm_gain: float32 [1024], P(('dp', 'seq'))
- grad_ffn_norm_bias: float32 [1024], P(('dp', 'seq'))
- grad_up_weight: float32 [1024, 4096], P(('dp', 'seq'))
- grad_up_bias: float32 [4096], P(('dp', 'seq'))
- grad_down_weight: float32 [4096, 1024], P(('dp', 'seq'))
- grad_down_bias: float32 [1024], P(('dp', 'seq'))
- expert_counts: int32 [2, 4, 5], replicated
The draws below stay inside these ranges and needn't reach their ends.
Inputs may be any that keep to these rules, and one draw needn't show every extreme that they name: `mem_len`: some item sees no memory row and some item sees all 1024. `value_route`: 2 different experts for each row and head. `output_route`: 2 different experts for each token and head.
All inputs are finite; a program needn't handle non-finite values.
Results may differ from the reference program's by a relative error of at most 0.02.
Values may be sent and summed in bfloat16 or wider, within the bound.
A program may use at most 384 MiB of HBM per device.

```python
import math
import jax
import jax.numpy as jnp
from jax import lax

D = 1024
H = 4
DH = 112
E = 5
TOP = 2
FF = 4096
LEN = 1024
ITEMS = 32


def draw_mem_len(key, part):
    key = jax.random.fold_in(key, 11)
    key_lengths, key_order = jax.random.split(key)
    lengths = jax.random.randint(key_lengths, (ITEMS,), 0, LEN + 1)
    shuffled = jax.random.permutation(key_order, ITEMS)
    lengths = lengths.at[shuffled[0]].set(LEN)
    return lengths.at[shuffled[1]].set(0).astype(jnp.int32)


def strengthened(entries, stream_key, source, target, blocks, factor):
    owner, partner = [(jnp.arange(entries.shape[dim]) // (entries.shape[dim] // blocks)).reshape([-1 if axis == dim else 1 for axis in range(entries.ndim)]) for dim in (source, target)]
    chosen = jax.random.permutation(stream_key, blocks)[partner]
    strong = (owner == chosen) | (owner == (partner + blocks // 2) % blocks)
    return jnp.where(strong, factor * entries, entries)


def steps_of(key, dims, shards, least, top_value):
    def one(axis_at, parts):
        steps = jax.random.uniform(jax.random.fold_in(jax.random.fold_in(key, 6), axis_at), (parts,), jnp.float32, least / len(shards), top_value / len(shards))
        return jnp.repeat(jnp.exp(steps), dims[axis_at] // parts).reshape((-1,) + (1,) * (len(dims) - axis_at - 1))

    loudness = one(*shards[0])
    for cut in shards[1:]:
        loudness = loudness * one(*cut)
    return loudness


def distinct(own_key, rows, count, top, lift):
    order = jax.random.permutation(jax.random.fold_in(own_key, 1), count)
    boost = order
    for power in range(3):
        boost = boost * boost // count
    boost = boost * lift // count
    lots = jax.random.randint(jax.random.fold_in(own_key, 2), (rows, count), 0, 4096) + boost
    fixed_rows = jax.random.permutation(jax.random.fold_in(own_key, 3), rows)[jnp.arange(count) % rows]
    lots = jnp.where(jnp.arange(rows)[:, None] == fixed_rows[None, :], 1 << 14, lots)
    merit = lots * count + jnp.arange(count)
    return lax.top_k(merit.astype(jnp.int32), top)[1].astype(jnp.int32)


def gaussian(stream_key, extent, width, reach, shards=(), kind=jnp.bfloat16):
    entries = width * jax.random.normal(stream_key, extent, jnp.float32)
    if shards:
        entries = entries * steps_of(stream_key, extent, shards, -0.22, 0.18)
    return jnp.clip(entries, -reach, reach).astype(kind)


def noise_with(rng, shape, scale, limit, pieces, heavy, kind=jnp.bfloat16):
    values = scale * jax.random.normal(rng, shape, jnp.float32)
    if pieces:
        values = values * steps_of(rng, shape, pieces, -0.22, 0.18)
    return jnp.clip(strengthened(values, jax.random.fold_in(rng, 3), *heavy), -limit, limit).astype(kind)


def setup_inputs(seed: int = 0) -> dict:
    arg_keys = jax.random.split(jax.random.key(seed), 24)
    tokens = gaussian(arg_keys[0], (ITEMS, LEN, D), 1.0, 6.0, ((0, 32), (1, 4)))
    memory = gaussian(arg_keys[1], (ITEMS, LEN, D), 1.0, 6.0, ((0, 32), (1, 4)))
    cotangent = noise_with(arg_keys[2], (ITEMS, LEN, D), 1.0, 12.0, ((0, 32), (1, 4)), (0, 2, 32, 2.75))
    mem_len = draw_mem_len(jax.random.fold_in(arg_keys[23], 71), 0)
    value_route = distinct(arg_keys[4], ITEMS * 2 * LEN * H, E, TOP, 3276).reshape((ITEMS, 2, LEN, H, TOP))
    output_route = distinct(arg_keys[5], ITEMS * LEN * H, E, TOP, 3276).reshape((ITEMS, LEN, H, TOP))
    attn_norm_gain = jnp.clip(1.0 + 0.1 * jax.random.normal(arg_keys[6], (D,), jnp.float32), 0.5, 1.5).astype(jnp.bfloat16)
    attn_norm_bias = gaussian(arg_keys[7], (D,), 0.2, 1.25)
    query_weight = gaussian(arg_keys[8], (D, H * DH), D ** -0.5, 0.1875)
    key_weight = gaussian(arg_keys[9], (D, H * DH), D ** -0.5, 0.1875)
    rel_weight = gaussian(arg_keys[10], (D, H * DH), D ** -0.5, 0.1875)
    bias_u = gaussian(arg_keys[11], (H * DH,), 0.5, 3.0)
    bias_v = gaussian(arg_keys[12], (H * DH,), 0.5, 3.0)
    value_router = gaussian(arg_keys[13], (D, H * E), (4 * D) ** -0.5, 0.09375)
    value_weight = gaussian(arg_keys[14], (D, H * E * DH), D ** -0.5, 0.1875)
    out_router = gaussian(arg_keys[15], (D, H * E), (4 * D) ** -0.5, 0.09375)
    out_weight = gaussian(arg_keys[16], (H * E * DH, D), 4 ** -0.5, 3.0)
    ffn_norm_gain = jnp.clip(1.0 + 0.1 * jax.random.normal(arg_keys[17], (D,), jnp.float32), 0.5, 1.5).astype(jnp.bfloat16)
    ffn_norm_bias = gaussian(arg_keys[18], (D,), 0.2, 1.25)
    up_weight = gaussian(arg_keys[19], (D, FF), D ** -0.5, 0.1875)
    up_bias = gaussian(arg_keys[20], (FF,), 0.2, 1.25)
    down_weight = gaussian(arg_keys[21], (FF, D), FF ** -0.5, 0.09375)
    down_bias = gaussian(arg_keys[22], (D,), 0.2, 1.25)
    return dict(tokens=tokens, memory=memory, cotangent=cotangent, mem_len=mem_len, value_route=value_route, output_route=output_route, attn_norm_gain=attn_norm_gain, attn_norm_bias=attn_norm_bias, query_weight=query_weight, key_weight=key_weight, rel_weight=rel_weight, bias_u=bias_u, bias_v=bias_v, value_router=value_router, value_weight=value_weight, out_router=out_router, out_weight=out_weight, ffn_norm_gain=ffn_norm_gain, ffn_norm_bias=ffn_norm_bias, up_weight=up_weight, up_bias=up_bias, down_weight=down_weight, down_bias=down_bias)


eps = 1e-05
masked_fill = -1e+30

@jax.custom_vjp
def low(v):
    return lax.optimization_barrier(v.astype(jnp.bfloat16)).astype(jnp.float32)

@jax.custom_vjp
def low_back(v):
    return v

def low_keep(v):
    return (low(v), None)

def low_pass(kept, grad):
    return (grad,)

def back_keep(v):
    return (v, None)

def back_low(kept, grad):
    return (low(grad),)
low.defvjp(low_keep, low_pass)
low_back.defvjp(back_keep, back_low)

def matmul(left, right):
    return jnp.dot(left, right, precision=lax.Precision.HIGHEST, preferred_element_type=jnp.float32)

def layer_norm(values, norm_gain, norm_shift):
    center = values - lax.optimization_barrier(jnp.mean(values, axis=-1, keepdims=True))
    spread = lax.optimization_barrier(jnp.mean(center * center, axis=-1, keepdims=True))
    return center * lax.rsqrt(spread + eps) * norm_gain + norm_shift

def sinus_table(first_row, row_count, feat_count):
    places = (first_row + jnp.arange(row_count, dtype=jnp.int32)).astype(jnp.float32)
    frequency = jnp.exp(jnp.arange(feat_count // 2, dtype=jnp.int32).astype(jnp.float32) * (-2.0 * math.log(10000.0) / feat_count))
    angles = places[:, None] * frequency[None, :]
    return jnp.concatenate([jnp.sin(angles), jnp.cos(angles)], axis=1)

def one_item(param_set, tokens, memory, value_route, output_route, mem_len):
    attn_norm_gain, attn_norm_bias, query_weight, key_weight, rel_weight, bias_u, bias_v, value_router, value_weight, out_router, out_weight, ffn_norm_gain, ffn_norm_bias, up_weight, up_bias, down_weight, down_bias = param_set
    key_span = 2 * LEN
    all_rows = jnp.concatenate([memory, tokens], axis=0)
    normed = low(layer_norm(all_rows, attn_norm_gain, attn_norm_bias))
    tok_normed = normed[LEN:]
    query = low_back(matmul(tok_normed, query_weight))
    query_u = low(query + bias_u).reshape(LEN, H, DH)
    query_v = low(query + bias_v).reshape(LEN, H, DH)
    keys = low(low_back(matmul(normed, key_weight))).reshape(key_span, H, DH)
    picks = jnp.arange(E, dtype=jnp.int32)
    value_pick = lax.optimization_barrier(jnp.sum((value_route.reshape(key_span, H, TOP)[..., None] == picks).astype(jnp.float32), axis=2))
    value_logit = low_back(matmul(normed, value_router)).reshape(key_span, H, E)
    value_gate = jax.nn.sigmoid(value_logit) * value_pick
    value_experts = low_back(matmul(normed, value_weight)).reshape(key_span, H, E, DH)
    values = low(low_back(lax.optimization_barrier(jnp.sum(value_gate[..., None] * value_experts, axis=2))))
    sinus = low(sinus_table(0, key_span, D))
    relative = low(low_back(matmul(sinus, rel_weight))).reshape(key_span, H, DH)
    content = low_back(jnp.einsum('ihd,jhd->hij', query_u, keys, precision=lax.Precision.HIGHEST))
    position = low_back(jnp.einsum('ihd,rhd->hir', query_v, relative, precision=lax.Precision.HIGHEST))
    query_at = jnp.arange(LEN, dtype=jnp.int32)[:, None]
    key_at = jnp.arange(key_span, dtype=jnp.int32)[None, :]
    distance = jnp.clip(LEN + query_at - key_at, 0, key_span - 1)
    shifted = jnp.take_along_axis(position, jnp.broadcast_to(distance[None], (H, LEN, key_span)), axis=2)
    visible = (key_at <= LEN + query_at) & (key_at >= LEN - mem_len)
    scores = jnp.where(visible[None], (content + shifted) * DH ** (-0.5), masked_fill)
    highest = lax.optimization_barrier(jnp.max(scores, axis=-1, keepdims=True))
    weights = jnp.exp(scores - highest)
    probs = weights / lax.optimization_barrier(jnp.sum(weights, axis=-1, keepdims=True))
    attended = low_back(jnp.einsum('hij,jhd->ihd', low(probs), values, precision=lax.Precision.HIGHEST))
    out_pick = lax.optimization_barrier(jnp.sum((output_route[..., None] == picks).astype(jnp.float32), axis=2))
    out_logit = low_back(matmul(tok_normed, out_router)).reshape(LEN, H, E)
    out_gate = jax.nn.sigmoid(out_logit) * out_pick
    mixed = low(out_gate[..., None] * attended[:, :, None, :]).reshape(LEN, H * E * DH)
    attn_out = low_back(matmul(mixed, out_weight))
    resid = tokens + attn_out
    normed_two = low(layer_norm(resid, ffn_norm_gain, ffn_norm_bias))
    before = low_back(matmul(normed_two, up_weight) + up_bias)
    hidden = low(jax.nn.gelu(before, approximate=False))
    return resid + matmul(hidden, down_weight) + down_bias

def reference(tokens, memory, cotangent, mem_len, value_route, output_route, attn_norm_gain, attn_norm_bias, query_weight, key_weight, rel_weight, bias_u, bias_v, value_router, value_weight, out_router, out_weight, ffn_norm_gain, ffn_norm_bias, up_weight, up_bias, down_weight, down_bias):
    param_set = jax.tree.map(lambda leaf_value: leaf_value.astype(jnp.float32), (attn_norm_gain, attn_norm_bias, query_weight, key_weight, rel_weight, bias_u, bias_v, value_router, value_weight, out_router, out_weight, ffn_norm_gain, ffn_norm_bias, up_weight, up_bias, down_weight, down_bias))
    tokens_full = tokens.astype(jnp.float32)
    memory_full = memory.astype(jnp.float32)

    def forward(params_in, tokens_in):

        def scan_step(running, item_data):
            return (running, jax.checkpoint(one_item)(params_in, *item_data))
        _, outputs = lax.scan(scan_step, jnp.float32(0.0), (tokens_in, memory_full, value_route, output_route, mem_len))
        return outputs
    outputs, pullback = jax.vjp(forward, param_set, tokens_full)
    param_grads, token_grad = pullback(cotangent.astype(jnp.float32))
    picks = jnp.arange(E, dtype=jnp.int32)
    value_count = lax.optimization_barrier(jnp.sum((value_route[..., None] == picks).astype(jnp.int32), axis=(0, 1, 2, 4)))
    out_count = lax.optimization_barrier(jnp.sum((output_route[..., None] == picks).astype(jnp.int32), axis=(0, 1, 3)))
    counts = jnp.stack([value_count, out_count])
    return (outputs.astype(jnp.bfloat16), token_grad, param_grads[0], param_grads[1], param_grads[2], param_grads[3], param_grads[4], param_grads[5], param_grads[6], param_grads[7], param_grads[8], param_grads[9], param_grads[10], param_grads[11], param_grads[12], param_grads[13], param_grads[14], param_grads[15], param_grads[16], counts)
```

```python
from functools import partial
import math

import jax
import jax.numpy as jnp
from jax import lax
from jax.experimental import pallas as pl
from jax.experimental.pallas import tpu as pltpu
from jax.sharding import PartitionSpec as P

D = 1024
H = 4
DH = 112
E = 5
FF = 4096
LEN = 1024
SLOT = 128
BLOCK = 256
EXPERTS = 2 * E * SLOT
KEY_AT = EXPERTS
QUERY_AT = KEY_AT + 2 * SLOT
ROUTER_AT = QUERY_AT + 2 * SLOT
WIDE = ROUTER_AT + SLOT
SCALE = DH ** (-0.5)
MASKED = -1e30
EPS = 1e-05
BF16 = jnp.bfloat16
F32 = jnp.float32
VMEM_BYTES = 58 * 1024 * 1024
IN_VMEM = pl.BlockSpec(memory_space=pltpu.VMEM)
IN_SMEM = pl.BlockSpec(memory_space=pltpu.SMEM)
MESH = pl.DeviceIdType.MESH


def dot(left, right, left_dim=1, right_dim=0):
    return lax.dot_general(
        left, right, (((left_dim,), (right_dim,)), ((), ())), preferred_element_type=F32
    )


def struct(shape, kind=BF16):
    return jax.ShapeDtypeStruct(shape, kind)


def local_call(kernel, out_shape, scratch_shapes=(), smem=0, vmem=0, **kw):
    return pl.pallas_call(
        kernel,
        out_shape=out_shape,
        in_specs=[IN_SMEM] * smem + [IN_VMEM] * vmem,
        out_specs=[IN_VMEM] * len(out_shape),
        scratch_shapes=scratch_shapes,
        compiler_params=pltpu.CompilerParams(vmem_limit_bytes=VMEM_BYTES),
        **kw,
    )


def centered(rows):
    center = rows - jnp.mean(rows, axis=1, keepdims=True)
    inverse = lax.rsqrt(jnp.mean(center * center, axis=1, keepdims=True) + EPS)
    return center * inverse, inverse


def norm_back(grad, scaled, inverse, gain):
    through = grad * gain
    return inverse * (
        through
        - jnp.mean(through, axis=1, keepdims=True)
        - scaled * jnp.mean(through * scaled, axis=1, keepdims=True)
    )


def picked(route, head, expert):
    return (route[:, 2 * head : 2 * head + 1] == expert) | (
        route[:, 2 * head + 1 : 2 * head + 2] == expert
    )


def pick_of(route, core, pair, expert):
    one = picked(route, 2 * pair, expert)
    two = picked(route, 2 * pair + 1, expert)
    return jnp.where(core == 0, one.astype(F32), two.astype(F32))


def prepare_kernel(spot, value_weight, key_weight, query_weight, rel_weight, value_router, out_router, out_weight, wide, rel, out_wide):
    core = spot[0]
    blank = jnp.zeros((SLOT - DH, D), BF16)

    def fill(target, slot, source, start):
        target[slot : slot + DH, :] = source[pl.ds(pl.multiple_of(start, DH), DH), :]
        target[slot + DH : slot + SLOT, :] = blank

    for pair in range(2):
        head = 2 * pair + core
        for expert in range(E):
            slot = (pair * E + expert) * SLOT
            fill(wide, slot, value_weight, (head * E + expert) * DH)
            fill(out_wide, slot, out_weight, (head * E + expert) * DH)
        fill(wide, KEY_AT + pair * SLOT, key_weight, head * DH)
        fill(wide, QUERY_AT + pair * SLOT, query_weight, head * DH)
    fill(rel, 0, rel_weight, (2 * spot[1] + core) * DH)
    routers = []
    for router in (value_router, out_router):
        for pair in range(2):
            one = router[2 * pair * E : (2 * pair + 1) * E, :].astype(F32)
            two = router[(2 * pair + 1) * E : (2 * pair + 2) * E, :].astype(F32)
            routers.append(jnp.where(core == 0, one, two))
    routers.append(jnp.zeros((SLOT - 4 * E, D), F32))
    wide[ROUTER_AT:, :] = jnp.concatenate(routers, axis=0).astype(BF16)


def prepare(spot, value_weight, key_weight, query_weight, rel_weight, value_router, out_router, out_weight):
    return local_call(
        prepare_kernel, [struct((WIDE, D)), struct((SLOT, D)), struct((EXPERTS, D))], smem=1, vmem=7
    )(spot, value_weight.T, key_weight.T, query_weight.T, rel_weight.T, value_router.T, out_router.T, out_weight)


def project_kernel(spot, rows, gain, shift, wide, route, normed, experts, logits, pay, full):
    step = pl.program_id(0)
    scaled, _ = centered(rows[...].astype(F32))
    low = (scaled * gain[...].astype(F32) + shift[...].astype(F32)).astype(BF16)
    normed[...] = low
    full[...] = dot(low, wide[...], 1, 1)
    experts[...] = full[:, :EXPERTS].astype(BF16)
    logit = full[:, ROUTER_AT:WIDE]
    logits[...] = logit
    gate = jax.nn.sigmoid(logit)
    routes = route[...]
    for pair in range(2):
        total = jnp.zeros((BLOCK, SLOT), F32)
        for expert in range(E):
            slot = pair * E + expert
            weight = gate[:, slot : slot + 1] * pick_of(routes, spot[0], pair, expert)
            total += weight * full[:, slot * SLOT : (slot + 1) * SLOT]
        pay[pair, step] = full[:, KEY_AT + pair * SLOT : KEY_AT + (pair + 1) * SLOT].astype(BF16)
        pay[pair, 4 + step] = total.astype(BF16)

        def keep_query(pair=pair):
            pay[pair, 6 + step] = full[:, QUERY_AT + pair * SLOT : QUERY_AT + (pair + 1) * SLOT].astype(BF16)

        pl.when(step >= 2)(keep_query)


def project(spot, rows, gain, shift, wide, route):
    block = lambda width: pl.BlockSpec((BLOCK, width), lambda step: (step, 0))
    fixed = lambda *shape: pl.BlockSpec(shape, lambda step: (0,) * len(shape))
    return pl.pallas_call(
        project_kernel,
        grid=(4,),
        out_shape=[struct((4 * BLOCK, D)), struct((4 * BLOCK, EXPERTS)), struct((4 * BLOCK, SLOT), F32), struct((2, 10, BLOCK, SLOT))],
        in_specs=[IN_SMEM, block(D), fixed(1, D), fixed(1, D), fixed(WIDE, D), block(2 * H)],
        out_specs=[block(D), block(EXPERTS), block(SLOT), fixed(2, 10, BLOCK, SLOT)],
        scratch_shapes=[pltpu.VMEM((BLOCK, WIDE), F32)],
        compiler_params=pltpu.CompilerParams(vmem_limit_bytes=VMEM_BYTES),
    )(spot, rows, gain, shift, wide, route)


def spots_of(core, chip):
    return [
        chip * 512 + core * BLOCK,
        chip * 512 + (1 - core) * BLOCK,
        (1 - chip) * 512 + core * BLOCK,
        (1 - chip) * 512 + (1 - core) * BLOCK,
    ]


def rows_at(start):
    return pl.ds(pl.multiple_of(start, BLOCK), BLOCK)


def attention_kernel(spot, own, peer, bias_u, bias_v, far_rel, attended, probs, keys, values, qu, qv, back):
    shown = spot[2]
    places = spots_of(spot[0], spot[1])
    for chip, pay in ((0, own), (1, peer)):
        for side in range(2):
            start = places[2 * chip + side]
            keys[rows_at(start), :] = pay[side]
            keys[rows_at(start + LEN), :] = pay[2 + side]
            values[rows_at(start), :] = pay[4 + side]
            values[rows_at(start + LEN), :] = pay[6 + side]
            query = pay[8 + side].astype(F32)
            qu[rows_at(start), :] = (query + bias_u[...]).astype(BF16)
            qv[rows_at(start), :] = (query + bias_v[...]).astype(BF16)
    for block in range(LEN // BLOCK):
        rows = pl.ds(block * BLOCK, BLOCK)
        width = LEN + (block + 1) * BLOCK
        first_far = 2 * LEN - width
        content = dot(qu[rows, :], keys[:width, :], 1, 1)
        far = dot(qv[rows, :], far_rel[first_far:, :], 1, 1)
        near = pltpu.roll(far, width - BLOCK + 1, 1, stride=1, stride_axis=0)
        row_at = lax.broadcasted_iota(jnp.int32, (BLOCK, width), 0) + (LEN + block * BLOCK)
        key_at = lax.broadcasted_iota(jnp.int32, (BLOCK, width), 1)
        visible = (key_at <= row_at) & (key_at >= LEN - shown)
        scores = jnp.where(visible, (content + near) * SCALE, MASKED)
        highest = jnp.max(scores, axis=1, keepdims=True)
        weights = jnp.exp(scores - highest)
        total = jnp.sum(weights, axis=1, keepdims=True)
        low = (weights * (1.0 / total)).astype(BF16)
        probs[rows, :width] = low
        attended[rows, :] = dot(low, values[:width, :], 1, 0)
    for number, start in enumerate(places):
        back[number] = attended[rows_at(start), :].astype(BF16)


def attention(spot, own, peer, bias_u, bias_v, far_rel):
    return local_call(
        attention_kernel,
        [
            struct((LEN, SLOT), F32),
            struct((LEN, 2 * LEN)),
            struct((2 * LEN, SLOT)),
            struct((2 * LEN, SLOT)),
            struct((LEN, SLOT)),
            struct((LEN, SLOT)),
            struct((4, BLOCK, SLOT)),
        ],
        smem=1,
        vmem=5,
    )(spot, own, peer, bias_u, bias_v, far_rel)


def two_heads(chip, own, peer):
    first = jnp.where(chip == 0, own.astype(F32), peer.astype(F32))
    second = jnp.where(chip == 0, peer.astype(F32), own.astype(F32))
    return first, second


def mix_kernel(spot, own, peer, logits, route, out_wide, mixed, partial_out):
    heads = two_heads(spot[1], own[...].reshape(2 * BLOCK, SLOT), peer[...].reshape(2 * BLOCK, SLOT))
    gate = jax.nn.sigmoid(logits[2 * BLOCK :, :])
    routes = route[...]
    for pair in range(2):
        for expert in range(E):
            slot = pair * E + expert
            weight = gate[:, 2 * E + slot : 2 * E + slot + 1] * pick_of(routes, spot[0], pair, expert)
            mixed[:, slot * SLOT : (slot + 1) * SLOT] = (weight * heads[pair]).astype(BF16)
    partial_out[...] = dot(mixed[...], out_wide[...]).astype(BF16)


def mix(spot, own, peer, logits, route, out_wide):
    return local_call(
        mix_kernel, [struct((2 * BLOCK, EXPERTS)), struct((2 * BLOCK, D))], smem=1, vmem=5
    )(spot, own, peer, logits, route, out_wide)


def feed_kernel(
    spot,
    rows,
    part_mine,
    part_theirs,
    cot,
    gain,
    shift,
    up,
    up_bias,
    down,
    down_bias,
    resid,
    final_mine,
    final_theirs,
    grad_part,
    grad_up,
    grad_up_bias,
    grad_down,
    low,
    low_turned,
    sum_out,
    sum_grad,
):
    step = pl.program_id(0)

    def first():
        for side in range(2):
            here = slice(side * BLOCK, (side + 1) * BLOCK)
            there = slice((1 - side) * BLOCK, (2 - side) * BLOCK)
            total = rows[here, :].astype(F32) + (part_mine[here, :].astype(F32) + part_theirs[there, :].astype(F32))
            resid[here, :] = total
            scaled, _ = centered(total)
            low[here, :] = (scaled * gain[...].astype(F32) + shift[...].astype(F32)).astype(BF16)
        low_turned[...] = low[...].T
        sum_out[...] = jnp.zeros_like(sum_out)
        sum_grad[...] = jnp.zeros_like(sum_grad)

    pl.when(step == 0)(first)
    before = dot(low[...], up[...]) + up_bias[...].astype(F32)
    below = 0.5 * (1.0 + lax.erf(before * (0.5**0.5)))
    hidden = (before * below).astype(BF16)
    slope = below + before * (jnp.exp(-0.5 * before * before) * ((2.0 * math.pi) ** -0.5))
    grad_before = dot(cot[...], down[...], 1, 1) * slope
    grad_low = grad_before.astype(BF16)
    grad_up_bias[...] = jnp.sum(grad_low.astype(F32), axis=0, keepdims=True)
    sum_out[...] += dot(hidden, down[...])
    sum_grad[...] += dot(grad_low, up[...], 1, 1)
    grad_up[...] = dot(low_turned[...], grad_low).astype(BF16)
    grad_down[...] = dot(hidden, cot[...], 0, 0).astype(BF16)

    def last():
        final_mine[...] = resid[:BLOCK, :] + sum_out[:BLOCK, :] + down_bias[...].astype(F32)
        final_theirs[...] = sum_out[BLOCK:, :].astype(BF16)
        grad_part[...] = sum_grad[...].astype(BF16)

    pl.when(step == pl.num_programs(0) - 1)(last)


def feed(spot, rows, part_mine, part_theirs, cot, gain, shift, up, up_bias, down, down_bias):
    fixed = lambda *shape: pl.BlockSpec(shape, lambda step, spot: (0,) * len(shape))
    steps = FF // 2 // BLOCK
    columns = lambda count: pl.BlockSpec((count, BLOCK), lambda step, spot: (0, spot[0] * steps + step))
    return pl.pallas_call(
        feed_kernel,
        grid_spec=pltpu.PrefetchScalarGridSpec(
            num_scalar_prefetch=1,
            grid=(steps,),
            in_specs=[
                pl.BlockSpec((2 * BLOCK, D), lambda step, spot: (1, 0)),
                fixed(2 * BLOCK, D),
                fixed(2 * BLOCK, D),
                fixed(2 * BLOCK, D),
                fixed(1, D),
                fixed(1, D),
                columns(D),
                columns(1),
                pl.BlockSpec((BLOCK, D), lambda step, spot: (spot[0] * steps + step, 0)),
                fixed(1, D),
            ],
            out_specs=[
                fixed(2 * BLOCK, D),
                fixed(BLOCK, D),
                fixed(BLOCK, D),
                fixed(2 * BLOCK, D),
                pl.BlockSpec((D, BLOCK), lambda step, spot: (0, step)),
                pl.BlockSpec((1, BLOCK), lambda step, spot: (0, step)),
                pl.BlockSpec((BLOCK, D), lambda step, spot: (step, 0)),
            ],
            scratch_shapes=[
                pltpu.VMEM((2 * BLOCK, D), BF16),
                pltpu.VMEM((D, 2 * BLOCK), BF16),
                pltpu.VMEM((2 * BLOCK, D), F32),
                pltpu.VMEM((2 * BLOCK, D), F32),
            ],
        ),
        out_shape=[
            struct((2 * BLOCK, D), F32),
            struct((BLOCK, D), F32),
            struct((BLOCK, D)),
            struct((2 * BLOCK, D)),
            struct((D, FF // 2)),
            struct((1, FF // 2), F32),
            struct((FF // 2, D)),
        ],
        compiler_params=pltpu.CompilerParams(vmem_limit_bytes=VMEM_BYTES),
    )(spot, rows, part_mine, part_theirs, cot, gain, shift, up, up_bias, down, down_bias)


def unmix_kernel(
    spot,
    resid,
    grad_mine,
    grad_theirs,
    cot,
    gain,
    own,
    peer,
    mixed,
    logits,
    route,
    out_wide,
    final_mine,
    final_theirs,
    grad_resid,
    pay,
    grad_logit,
    grad_out,
    sums,
    result,
    grad_low,
    grad_mixed,
):
    result[...] = (final_mine[...] + final_theirs[...].astype(F32)).astype(BF16)
    for side in range(2):
        here = slice(side * BLOCK, (side + 1) * BLOCK)
        there = slice((1 - side) * BLOCK, (2 - side) * BLOCK)
        scaled, inverse = centered(resid[here, :])
        grad = grad_mine[here, :].astype(F32) + grad_theirs[there, :].astype(F32)
        above = cot[here, :].astype(F32)
        total = above + norm_back(grad, scaled, inverse, gain[...].astype(F32))
        grad_low[here, :] = total.astype(BF16)
        if side == 0:
            grad_resid[...] = total
            sums[0:1, :] = jnp.sum(grad * scaled, axis=0, keepdims=True)
            sums[1:2, :] = jnp.sum(grad, axis=0, keepdims=True)
            sums[2:3, :] = jnp.sum(above, axis=0, keepdims=True)
    grad_mixed[...] = dot(grad_low[...], out_wide[...], 1, 1)
    heads = two_heads(spot[1], own[...].reshape(2 * BLOCK, SLOT), peer[...].reshape(2 * BLOCK, SLOT))
    gate = jax.nn.sigmoid(logits[2 * BLOCK :, :])
    routes = route[...]
    lane = lax.broadcasted_iota(jnp.int32, (2 * BLOCK, SLOT), 1)
    logit_sum = jnp.zeros((2 * BLOCK, SLOT), F32)
    totals = []
    for pair in range(2):
        total = jnp.zeros((2 * BLOCK, SLOT), F32)
        for expert in range(E):
            slot = pair * E + expert
            sig = gate[:, 2 * E + slot : 2 * E + slot + 1]
            pick = pick_of(routes, spot[0], pair, expert)
            part = grad_mixed[:, slot * SLOT : (slot + 1) * SLOT]
            total += part * (sig * pick)
            grad_gate = jnp.sum(part * heads[pair], axis=1, keepdims=True)
            logit_sum += jnp.where(lane == 2 * E + slot, grad_gate * pick * sig * (1.0 - sig), 0.0)
        totals.append(total)
    grad_logit[...] = logit_sum.astype(BF16)
    mine = jnp.where(spot[1] == 0, totals[0], totals[1]).astype(BF16)
    other = jnp.where(spot[1] == 0, totals[1], totals[0]).astype(BF16)
    pay[0, 0], pay[0, 1] = mine[:BLOCK], mine[BLOCK:]
    pay[1, 0], pay[1, 1] = other[:BLOCK], other[BLOCK:]
    grad_out[...] = dot(grad_low[...], mixed[...], 0, 0).astype(BF16)


def unmix(spot, resid, grad_mine, grad_theirs, cot, gain, own, peer, mixed, logits, route, out_wide, final_mine, final_theirs):
    return local_call(
        unmix_kernel,
        [
            struct((BLOCK, D), F32),
            struct((2, 2, BLOCK, SLOT)),
            struct((2 * BLOCK, SLOT)),
            struct((D, EXPERTS)),
            struct((8, D), F32),
            struct((BLOCK, D)),
        ],
        [pltpu.VMEM((2 * BLOCK, D), BF16), pltpu.VMEM((2 * BLOCK, EXPERTS), F32)],
        smem=1,
        vmem=13,
    )(spot, resid, grad_mine, grad_theirs, cot, gain, own, peer, mixed, logits, route, out_wide, final_mine, final_theirs)


def attention_back_kernel(
    spot,
    own,
    peer,
    qu,
    qv,
    keys,
    values,
    far_rel,
    probs,
    attended,
    pay,
    sums,
    grad_far,
    grad_out,
    grad_query,
    key_sum,
    value_sum,
    far_sum,
):
    places = spots_of(spot[0], spot[1])
    for chip, given in ((0, own), (1, peer)):
        for side in range(2):
            grad_out[rows_at(places[2 * chip + side]), :] = given[side]
    key_sum[...] = jnp.zeros_like(key_sum)
    value_sum[...] = jnp.zeros_like(value_sum)
    far_sum[...] = jnp.zeros_like(far_sum)
    sum_u = jnp.zeros((1, SLOT), F32)
    sum_v = jnp.zeros((1, SLOT), F32)
    down = lax.broadcasted_iota(jnp.int32, (BLOCK, BLOCK), 0)
    across = lax.broadcasted_iota(jnp.int32, (BLOCK, BLOCK), 1)
    flip = (down + across == BLOCK - 1).astype(F32).astype(BF16)
    for block in range(LEN // BLOCK):
        rows = pl.ds(block * BLOCK, BLOCK)
        width = LEN + (block + 1) * BLOCK
        first_far = 2 * LEN - width
        above = grad_out[rows, :]
        low = probs[rows, :width]
        grad_probs = dot(above, values[:width, :], 1, 1)
        inner = jnp.sum(above.astype(F32) * attended[rows, :], axis=1, keepdims=True)
        grad_scores = (low.astype(F32) * ((grad_probs - inner) * SCALE)).astype(BF16)
        grad_u = dot(grad_scores, keys[:width, :], 1, 0)
        key_sum[:width, :] += dot(grad_scores, qu[rows, :], 0, 0)
        value_sum[:width, :] += dot(low, above, 0, 0)
        far = pltpu.roll(dot(flip, grad_scores), 0, 1, stride=1, stride_axis=0).astype(BF16)
        turned = dot(flip, far).astype(BF16)
        grad_v = dot(turned, far_rel[first_far:, :], 1, 0)
        far_sum[first_far:, :] += dot(turned, qv[rows, :], 0, 0)
        grad_query[rows, :] = (grad_u + grad_v).astype(BF16)
        sum_u += jnp.sum(grad_u, axis=0, keepdims=True)
        sum_v += jnp.sum(grad_v, axis=0, keepdims=True)
    sums[0:1, :] = sum_u
    sums[1:2, :] = sum_v
    grad_far[...] = far_sum[...].astype(BF16)
    for chip in range(2):
        for side in range(2):
            start = places[2 * chip + side]
            pay[chip, side] = key_sum[rows_at(start), :].astype(BF16)
            pay[chip, 2 + side] = key_sum[rows_at(start + LEN), :].astype(BF16)
            pay[chip, 4 + side] = value_sum[rows_at(start), :].astype(BF16)
            pay[chip, 6 + side] = value_sum[rows_at(start + LEN), :].astype(BF16)
            pay[chip, 8 + side] = grad_query[rows_at(start), :]


def attention_back(spot, own, peer, qu, qv, keys, values, far_rel, probs, attended):
    return local_call(
        attention_back_kernel,
        [struct((2, 10, BLOCK, SLOT)), struct((2, SLOT), F32), struct((2 * LEN, SLOT))],
        [pltpu.VMEM((LEN, SLOT), BF16)] * 2 + [pltpu.VMEM((2 * LEN, SLOT), F32)] * 3,
        smem=1,
        vmem=9,
    )(spot, own, peer, qu, qv, keys, values, far_rel, probs, attended)


def unproject_kernel(spot, own, peer, normed, experts, logits, route, grad_logit, wide, grad_part, grad_wide, grad_all, turned):
    step = pl.program_id(0)
    flat = [own[step], own[4 + step], peer[step], peer[4 + step]]
    key_heads = two_heads(spot[1], flat[0], flat[2])
    value_heads = two_heads(spot[1], flat[1], flat[3])
    token = step >= 2
    query_at = jnp.where(token, 6 + step, 8)
    query_heads = two_heads(spot[1], own[query_at], peer[query_at])
    keep = jnp.where(token, 1.0, 0.0)
    gate = jax.nn.sigmoid(logits[...])
    routes = route[...]
    rows = rows_at(step * BLOCK)
    lane = lax.broadcasted_iota(jnp.int32, (BLOCK, SLOT), 1)
    logit_sum = grad_logit[rows_at(jnp.where(token, step - 2, 0) * BLOCK), :].astype(F32) * keep
    for pair in range(2):
        for expert in range(E):
            slot = pair * E + expert
            cols = slice(slot * SLOT, (slot + 1) * SLOT)
            sig = gate[:, slot : slot + 1]
            pick = pick_of(routes, spot[0], pair, expert)
            grad_all[rows, cols] = ((sig * pick) * value_heads[pair]).astype(BF16)
            grad_gate = jnp.sum(value_heads[pair] * experts[:, cols].astype(F32), axis=1, keepdims=True)
            logit_sum += jnp.where(lane == slot, grad_gate * pick * sig * (1.0 - sig), 0.0)
        grad_all[rows, KEY_AT + pair * SLOT : KEY_AT + (pair + 1) * SLOT] = key_heads[pair].astype(BF16)
        grad_all[rows, QUERY_AT + pair * SLOT : QUERY_AT + (pair + 1) * SLOT] = (keep * query_heads[pair]).astype(BF16)
    grad_all[rows, ROUTER_AT:WIDE] = logit_sum.astype(BF16)
    grad_part[...] = dot(grad_all[rows, :], wide[...]).astype(BF16)
    turned[:, rows] = normed[...].T

    def last():
        for part in range(5):
            cols = slice(part * 384, (part + 1) * 384)
            grad_wide[:, cols] = dot(turned[...], grad_all[:, cols]).astype(BF16)

    pl.when(step == 3)(last)


def unproject(spot, own, peer, normed, experts, logits, route, grad_logit, wide):
    block = lambda width: pl.BlockSpec((BLOCK, width), lambda step: (step, 0))
    fixed = lambda *shape: pl.BlockSpec(shape, lambda step: (0,) * len(shape))
    return pl.pallas_call(
        unproject_kernel,
        grid=(4,),
        out_shape=[struct((4 * BLOCK, D)), struct((D, WIDE))],
        in_specs=[
            IN_SMEM,
            fixed(10, BLOCK, SLOT),
            fixed(10, BLOCK, SLOT),
            block(D),
            block(EXPERTS),
            block(SLOT),
            block(2 * H),
            fixed(2 * BLOCK, SLOT),
            fixed(WIDE, D),
        ],
        out_specs=[block(D), fixed(D, WIDE)],
        scratch_shapes=[pltpu.VMEM((4 * BLOCK, WIDE), BF16), pltpu.VMEM((D, 4 * BLOCK), BF16)],
        compiler_params=pltpu.CompilerParams(vmem_limit_bytes=VMEM_BYTES),
    )(spot, own, peer, normed, experts, logits, route, grad_logit, wide)


def finish_kernel(rows, grad_mine, grad_theirs, gain, grad_resid, grad_tokens, sums):
    gain_sum = jnp.zeros((1, D), F32)
    bias_sum = jnp.zeros((1, D), F32)
    for part in range(2):
        here = slice(2 * part * BLOCK, (2 * part + 1) * BLOCK)
        scaled, inverse = centered(rows[here, :].astype(F32))
        grad = grad_mine[here, :].astype(F32) + grad_theirs[part].astype(F32)
        gain_sum += jnp.sum(grad * scaled, axis=0, keepdims=True)
        bias_sum += jnp.sum(grad, axis=0, keepdims=True)
        if part == 1:
            grad_tokens[...] = grad_resid[...] + norm_back(grad, scaled, inverse, gain[...].astype(F32))
    sums[0:1, :] = gain_sum
    sums[1:2, :] = bias_sum


def finish(rows, grad_mine, grad_theirs, gain, grad_resid):
    return local_call(finish_kernel, [struct((BLOCK, D), F32), struct((8, D), F32)], vmem=5)(
        rows, grad_mine, grad_theirs, gain, grad_resid
    )


def place():
    dp = lax.axis_index("dp")
    sq = lax.axis_index("seq")
    return dict(x=dp // 8, z=(dp // 2) % 4, y=(sq // 2) * 2 + dp % 2, core=sq % 2)


def device_of(at):
    return (at["x"] * 8 + at["z"] * 2 + at["y"] % 2, (at["y"] // 2) * 2 + at["core"])


def moved(at, axis, steps):
    other = dict(at)
    other[axis] = (at[axis] + steps) % 4
    return device_of(other)


PLAIN = (("x", 4), ("z", 4), ("ylo", 2), ("yhi", 2))
SPLIT = (("xhi", 2), ("z", 4), ("ylo", 2), ("yhi", 2), ("xlo", 2))


def part_of(name, where):
    return {"hi": where // 2, "lo": where % 2}.get(name[1:], where)


def chunk_of(ref, dims, axis, where):
    return ref.at[tuple(part_of(name, where) if name[0] == axis else slice(None) for name, _ in dims)]


def without(dims, axes):
    return tuple(dim for dim in dims if dim[0][0] not in axes)


def lead_shape(dims):
    return tuple(size for _, size in dims)


def halves(width):
    one = (width // 2 + 127) // 128 * 128
    return (0, one), (one, width - one)


def each_block(lead, step):
    count = math.prod(lead)
    if not lead:
        step(Ellipsis)
        return

    def run(flat, carry):
        index = []
        for size in reversed(lead):
            index.insert(0, flat % size)
            flat = flat // size
        step(tuple(index))
        return carry

    lax.fori_loop(0, count, run, 0)


def reduce_kernel(layouts, pieces, *refs):
    count = len(layouts)
    refs = list(refs)
    take = lambda number: [refs.pop(0) for _ in range(number)]
    sources = take(count)
    (small_in,) = take(1)
    mine = take(count)
    theirs = take(sum(dims is PLAIN for dims in layouts))
    (small_out,) = take(1)
    send_sem, recv_sem, own_sem = take(3)
    totals = take(count)
    small_slots = take(4)
    at = place()
    sibling = dict(at)
    sibling["core"] = 1 - at["core"]
    sibling = device_of(sibling)
    high, low, core = at["x"] // 2, at["x"] % 2, at["core"]
    stays = (high == low) & (low == core)
    ahead, behind = dict(at), dict(at)
    ahead["x"], ahead["core"] = 2 * core + high, low
    behind["x"], behind["core"] = 2 * low + core, high
    ahead, behind = device_of(ahead), device_of(behind)
    barrier = pltpu.get_barrier_semaphore()
    greeted = [moved(at, axis, steps) for axis in "xyz" for steps in (1, 2, 3)] + [sibling]

    def greet(device):
        pl.semaphore_signal(barrier, inc=1, device_id=device, device_id_type=pl.DeviceIdType.MESH)

    for device in greeted:
        greet(device)

    def greet_far():
        greet(ahead)
        greet(behind)
        pl.semaphore_wait(barrier, len(greeted) + 2)

    pl.when(jnp.logical_not(stays))(greet_far)
    pl.when(stays)(lambda: pl.semaphore_wait(barrier, len(greeted)))
    used = [0]

    def prepared(src, dst, device):
        slot = used[0]
        used[0] += 1
        return pltpu.make_async_remote_copy(
            src_ref=src,
            dst_ref=dst,
            send_sem=send_sem.at[slot],
            recv_sem=recv_sem.at[slot],
            device_id=device,
            device_id_type=pl.DeviceIdType.MESH,
        )

    def send(src, dst, device):
        copy = prepared(src, dst, device)
        copy.start()
        return copy

    def added(target, *terms):
        def add(index):
            total = terms[0][index].astype(F32)
            for term in terms[1:]:
                total += term[index].astype(F32)
            target[index] = total.astype(target.dtype)

        return add

    current = [sources[array].at[..., pl.ds(start, width)] for array, start, width, order in pieces]
    small_now = small_in
    open_sends = []
    for phase in range(3):
        plans = []
        for number, (array, start, width, order) in enumerate(pieces):
            axis = order[phase]
            dims = without(layouts[array], order[:phase])
            left = lead_shape(without(dims, axis))
            cols = [pl.ds(*half) for half in halves(width)]
            bufs = take(6)
            after = take(1)[0] if phase < 2 else totals[array].at[:, pl.ds(start, width)]
            near = [chunk_of(current[number], dims, axis, (at[axis] + steps) % 4) for steps in range(4)]
            plans.append((axis, left, cols, bufs, after, near, []))
        for axis, left, cols, bufs, after, near, made in plans:
            for side, steps in ((0, 1), (1, 3)):
                made.append(send(near[2].at[..., cols[side]], bufs[side], moved(at, axis, steps)))
        small_axis = "xyz"[phase]
        slots = small_slots[phase]
        small_copies = []
        slots[at[small_axis]] = small_now[...]
        for steps in (1, 2, 3):
            small_copies.append(
                send(slots.at[at[small_axis]], slots.at[at[small_axis]], moved(at, small_axis, steps))
            )
        for axis, left, cols, bufs, after, near, made in plans:
            for side, steps in ((0, 1), (1, 3)):
                made.append(
                    send(near[steps].at[..., cols[1 - side]], bufs[2 + side], moved(at, axis, steps))
                )
        for axis, left, cols, bufs, after, near, made in plans:
            for side, steps in ((0, 1), (1, 3)):
                made[side].wait_recv()
                each_block(left, added(bufs[side], bufs[side], near[steps].at[..., cols[side]]))
                made.append(send(bufs[side], bufs[4 + side], moved(at, axis, steps)))
        for copy in small_copies:
            copy.wait_recv()
        small_total = (slots[0] + slots[1]) + (slots[2] + slots[3])
        small_now = small_slots[3].at[core] if phase == 2 else small_out
        small_now[...] = small_total
        open_sends += small_copies
        current = []
        for axis, left, cols, bufs, after, near, made in plans:
            for copy in made[2:]:
                copy.wait_recv()
            for side in (0, 1):
                each_block(
                    left,
                    added(
                        after.at[..., cols[side]],
                        near[0].at[..., cols[side]],
                        bufs[4 + side],
                        bufs[3 - side],
                    ),
                )
            open_sends += made
            current.append(after)
    last = []
    pair = small_slots[3]
    last.append(send(pair.at[core], pair.at[core], sibling))
    spare = list(theirs)
    for array, dims in enumerate(layouts):
        if dims is PLAIN:
            half = totals[array].shape[0] // 2
            other = pl.ds(pl.multiple_of((1 - core) * half, 8), half)
            last.append(send(totals[array].at[other], spare.pop(0), sibling))
            mine[array][...] = totals[array][pl.ds(pl.multiple_of(core * half, 8), half), :]
            continue
        away = prepared(totals[array], mine[array], ahead)
        here = pltpu.make_async_copy(totals[array], mine[array], own_sem)
        pl.when(jnp.logical_not(stays))(away.start)
        pl.when(stays)(here.start)
        pl.when(jnp.logical_not(stays))(away.wait)
        pl.when(stays)(here.wait)
    for copy in last:
        copy.wait_recv()
    small_out[...] = pair[0] + pair[1]
    for copy in open_sends + last:
        copy.wait_send()


def reduce_all(arrays, layouts, pieces, small):
    shapes = [array.shape[1:] for array in arrays]
    arrays = [
        array.reshape(lead_shape(dims) + shape) for array, dims, shape in zip(arrays, layouts, shapes)
    ]
    scratch = []
    copies = 0
    for phase in range(3):
        for array, start, width, order in pieces:
            left = lead_shape(without(layouts[array], order[: phase + 1]))
            rows = shapes[array][0]
            (_, one), (_, two) = halves(width)
            for size in (one, two, two, one, one, two):
                scratch.append(pltpu.VMEM(left + (rows, size), BF16))
            if phase < 2:
                scratch.append(pltpu.VMEM(left + (rows, width), BF16))
            copies += 6
    copies += 9 + len(arrays) + 1
    head = [pltpu.SemaphoreType.DMA((copies,)), pltpu.SemaphoreType.DMA((copies,)), pltpu.SemaphoreType.DMA]
    head += [pltpu.VMEM(shape, F32) for shape in shapes]
    head += [pltpu.VMEM((4,) + small.shape, F32)] * 3 + [pltpu.VMEM((2,) + small.shape, F32)]
    outs = []
    for shape, dims in zip(shapes, layouts):
        outs.append(struct((shape[0] // 2 if dims is PLAIN else shape[0], shape[1]), F32))
    outs += [out for out, dims in zip(outs, layouts) if dims is PLAIN]
    outs.append(struct(small.shape, F32))
    return pl.pallas_call(
        partial(reduce_kernel, layouts, pieces),
        out_shape=outs,
        in_specs=[IN_VMEM] * (len(arrays) + 1),
        out_specs=[IN_VMEM] * len(outs),
        scratch_shapes=head + scratch,
        compiler_params=pltpu.CompilerParams(
            collective_id=0, has_side_effects=True, vmem_limit_bytes=VMEM_BYTES
        ),
    )(*arrays, small)


def sinus_far():
    frequency = jnp.exp(jnp.arange(D // 2, dtype=jnp.int32).astype(F32) * (-2.0 * math.log(10000.0) / D))
    coarse = (64 * (31 - jnp.arange(32, dtype=jnp.int32))).astype(F32)[:, None] * frequency
    fine = (63 - jnp.arange(64, dtype=jnp.int32)).astype(F32)[:, None] * frequency
    sin_a, cos_a = jnp.sin(coarse)[:, None], jnp.cos(coarse)[:, None]
    sin_b, cos_b = jnp.sin(fine)[None], jnp.cos(fine)[None]
    sines = sin_a * cos_b + cos_a * sin_b
    cosines = cos_a * cos_b - sin_a * sin_b
    return jnp.concatenate([sines, cosines], axis=2).reshape(2 * LEN, D).astype(BF16)


def swap(value):
    return lax.ppermute(value, "seq", [(0, 1), (1, 0), (2, 3), (3, 2)])


def cross(value):
    return lax.ppermute(value, "seq", [(0, 2), (2, 0), (1, 3), (3, 1)])


def body(
    tokens,
    memory,
    cotangent,
    mem_len,
    value_route,
    output_route,
    attn_norm_gain,
    attn_norm_bias,
    query_weight,
    key_weight,
    rel_weight,
    bias_u,
    bias_v,
    value_router,
    value_weight,
    out_router,
    out_weight,
    ffn_norm_gain,
    ffn_norm_bias,
    up_weight,
    up_bias,
    down_weight,
    down_bias,
):
    seq_index = lax.axis_index("seq")
    core, chip = seq_index % 2, seq_index // 2
    spot = jnp.stack([core, chip, mem_len[0]]).astype(jnp.int32)
    row = lambda vector: vector.reshape(1, -1)
    tokens, memory, cotangent = tokens[0], memory[0], cotangent[0]
    routes = jnp.concatenate(
        [value_route[0].reshape(2 * BLOCK, 2 * H), output_route[0].reshape(BLOCK, 2 * H)], axis=0
    )
    memory_theirs, tokens_theirs, routes_theirs = swap(memory), swap(tokens), swap(routes)
    cot = jnp.concatenate([cotangent, swap(cotangent)], axis=0)
    rows = jnp.concatenate([memory, memory_theirs, tokens, tokens_theirs], axis=0)
    value_routes = jnp.stack(
        [routes[: 2 * BLOCK].reshape(2, BLOCK, 2 * H), routes_theirs[: 2 * BLOCK].reshape(2, BLOCK, 2 * H)], axis=1
    ).reshape(4 * BLOCK, 2 * H)
    out_routes = jnp.concatenate([routes[2 * BLOCK :], routes_theirs[2 * BLOCK :]], axis=0)
    wide, rel, out_wide = prepare(
        spot, value_weight, key_weight, query_weight, rel_weight, value_router, out_router, out_weight
    )
    head_bias = lambda bias: jnp.pad(
        lax.dynamic_slice_in_dim(bias.astype(F32), seq_index * DH, DH, 0), (0, SLOT - DH)
    ).reshape(1, SLOT)
    sinus = sinus_far()
    far_rel = dot(sinus, rel, 1, 1).astype(BF16)
    attn_gain = row(attn_norm_gain)
    normed, experts, logits, pay = project(spot, rows, attn_gain, row(attn_norm_bias), wide, value_routes)
    pay_own = jnp.where(chip == 0, pay[0], pay[1])
    pay_peer = cross(jnp.where(chip == 0, pay[1], pay[0]))
    attended, probs, keys, values, qu, qv, back = attention(
        spot, pay_own, pay_peer, head_bias(bias_u), head_bias(bias_v), far_rel
    )
    att_own, att_peer = back[:2], cross(back[2:])
    mixed, out_part = mix(spot, att_own, att_peer, logits, out_routes, out_wide)
    resid, final_mine, final_theirs, norm_part, grad_up, grad_up_bias, grad_down = feed(
        spot,
        rows,
        out_part,
        swap(out_part),
        cot,
        row(ffn_norm_gain),
        row(ffn_norm_bias),
        up_weight,
        row(up_bias),
        down_weight,
        row(down_bias),
    )
    grad_resid, grad_att, grad_out_logit, grad_out, feed_sums, result = unmix(
        spot,
        resid,
        norm_part,
        swap(norm_part),
        cot,
        row(ffn_norm_gain),
        att_own,
        att_peer,
        mixed,
        logits,
        out_routes,
        out_wide,
        final_mine,
        swap(final_theirs),
    )
    pay_back, bias_sums, grad_far = attention_back(
        spot, grad_att[0], cross(grad_att[1]), qu, qv, keys, values, far_rel, probs, attended
    )
    grad_rel = dot(sinus, grad_far, 0, 0).astype(BF16)
    part, grad_wide = unproject(
        spot, pay_back[0], cross(pay_back[1]), normed, experts, logits, value_routes, grad_out_logit, wide
    )
    part_theirs = swap(part.reshape(2, 2, BLOCK, D)[:, 1])
    grad_tokens, attn_sums = finish(rows, part, part_theirs, attn_gain, grad_resid)
    nothing = jnp.zeros((), F32)
    up_bias_full = jnp.concatenate(
        [jnp.where(core == 0, grad_up_bias[0], nothing), jnp.where(core == 1, grad_up_bias[0], nothing)]
    )
    narrow = jnp.concatenate(
        [attn_sums[:2].T, feed_sums[:3].T, up_bias_full.reshape(D, 4), jnp.zeros((D, SLOT - 9), F32)], axis=1
    ).astype(BF16)
    blank = jnp.zeros((), BF16)
    rest = jnp.concatenate(
        [jnp.where(chip == 0, grad_rel, blank), jnp.where(chip == 1, grad_rel, blank), narrow], axis=1
    )
    picks = jnp.arange(E, dtype=jnp.int32)
    chosen = (routes.reshape(3 * BLOCK, H, 2)[..., None] == picks).astype(F32).sum(axis=2)
    counts = jnp.concatenate(
        [chosen[: 2 * BLOCK].sum(axis=0).reshape(-1), chosen[2 * BLOCK :].sum(axis=0).reshape(-1)]
    )
    head_at = (jnp.arange(H) == seq_index).astype(F32)[:, None]
    small = jnp.concatenate(
        [
            head_at * bias_sums[0:1],
            head_at * bias_sums[1:2],
            jnp.pad(counts, (0, SLOT - 40)).reshape(1, SLOT),
            jnp.zeros((7, SLOT), F32),
        ],
        axis=0,
    )
    pieces = (
        (0, 0, 2048, "xyz"),
        (1, 0, 1024, "yzx"),
        (2, 0, 1408, "zxy"),
        (3, 0, 768, "zxy"),
        (4, 0, 384, "zxy"),
        (2, 1408, 512, "xyz"),
        (3, 768, 512, "yzx"),
    )
    layouts = (PLAIN, SPLIT, PLAIN, PLAIN, PLAIN)
    up_mine, down_mine, wide_mine, out_mine, rest_mine, up_their, wide_their, out_their, rest_their, small_sum = (
        reduce_all(
            [
                grad_up.reshape(64, 16, FF // 2),
                grad_down.reshape(64, 32, D),
                grad_wide.reshape(64, 16, WIDE),
                grad_out.reshape(64, 16, EXPERTS),
                rest.reshape(64, 16, 3 * SLOT),
            ],
            layouts,
            pieces,
            small,
        )
    )
    first = core == 0

    def cores(mine, theirs):
        return jnp.stack([jnp.where(first, mine, theirs), jnp.where(first, theirs, mine)])

    def by_head(both, parts, width):
        shaped = both.reshape(2, 8, 2, parts, -1)[..., :width]
        return shaped.transpose(1, 2, 0, 3, 4).reshape(8, H * parts * width)

    wide_both = cores(wide_mine, wide_their)
    out_both = cores(out_mine, out_their)
    rest_both = cores(rest_mine, rest_their)
    narrow_sum = rest_mine[:, 2 * SLOT :] + rest_their[:, 2 * SLOT :]
    up_both = cores(up_mine, up_their)
    per_head = lambda rows: rows[:, :DH].reshape(H * DH)
    return (
        result[None],
        grad_tokens[None],
        narrow_sum[:, 0],
        narrow_sum[:, 1],
        by_head(wide_both[..., QUERY_AT:ROUTER_AT], 1, DH),
        by_head(wide_both[..., KEY_AT:QUERY_AT], 1, DH),
        by_head(rest_both[..., : 2 * SLOT], 1, DH),
        per_head(small_sum[:4]),
        per_head(small_sum[4:8]),
        by_head(wide_both[..., ROUTER_AT : ROUTER_AT + 10], E, 1),
        by_head(wide_both[..., :EXPERTS], E, DH),
        by_head(wide_both[..., ROUTER_AT + 10 : ROUTER_AT + 20], E, 1),
        by_head(out_both, E, DH).T,
        narrow_sum[:, 2],
        narrow_sum[:, 3],
        jnp.concatenate([up_both[0], up_both[1]], axis=1),
        narrow_sum[:, 5:9].reshape(-1),
        down_mine,
        narrow_sum[:, 4],
        jnp.round(small_sum[8, :40]).astype(jnp.int32).reshape(2, H, E),
    )


def solution(mesh):
    in_specs = (
        P("dp", "seq", None),
        P("dp", "seq", None),
        P("dp", "seq", None),
        P("dp"),
        P("dp", None, "seq", None, None),
        P("dp", "seq", None, None),
        P(),
        P(),
        P(),
        P(),
        P(),
        P(),
        P(),
        P(),
        P(),
        P(),
        P(),
        P(),
        P(),
        P(),
        P(),
        P(),
        P(),
    )
    out_specs = (
        P("dp", "seq", None),
        P("dp", "seq", None),
        P(("dp", "seq")),
        P(("dp", "seq")),
        P(("dp", "seq"), None),
        P(("dp", "seq"), None),
        P(("dp", "seq"), None),
        P(),
        P(),
        P(("dp", "seq"), None),
        P(("dp", "seq"), None),
        P(("dp", "seq"), None),
        P(None, ("dp", "seq")),
        P(("dp", "seq")),
        P(("dp", "seq")),
        P(("dp", "seq"), None),
        P(("dp", "seq")),
        P(("dp", "seq"), None),
        P(("dp", "seq")),
        P(),
    )
    return jax.shard_map(body, mesh=mesh, in_specs=in_specs, out_specs=out_specs, check_vma=False)
```

```python
from functools import partial
import math

import jax
import jax.numpy as jnp
from jax import lax
from jax.experimental import pallas as pl
from jax.experimental.pallas import tpu as pltpu
from jax.sharding import PartitionSpec as P

D = 1024
H = 4
DH = 112
E = 5
FF = 4096
LEN = 1024
SLOT = 128
BLOCK = 256
EXPERTS = 2 * E * SLOT
KEY_AT = EXPERTS
QUERY_AT = KEY_AT + 2 * SLOT
ROUTER_AT = QUERY_AT + 2 * SLOT
WIDE = ROUTER_AT + SLOT
SCALE = DH ** (-0.5)
MASKED = -1e30
EPS = 1e-05
BF16 = jnp.bfloat16
F32 = jnp.float32
VMEM_BYTES = 58 * 1024 * 1024
IN_VMEM = pl.BlockSpec(memory_space=pltpu.VMEM)
IN_SMEM = pl.BlockSpec(memory_space=pltpu.SMEM)
MESH = pl.DeviceIdType.MESH


def dot(left, right, left_dim=1, right_dim=0):
    return lax.dot_general(
        left, right, (((left_dim,), (right_dim,)), ((), ())), preferred_element_type=F32
    )


def struct(shape, kind=BF16):
    return jax.ShapeDtypeStruct(shape, kind)


def local_call(kernel, out_shape, scratch_shapes=(), smem=0, vmem=0, **kw):
    return pl.pallas_call(
        kernel,
        out_shape=out_shape,
        in_specs=[IN_SMEM] * smem + [IN_VMEM] * vmem,
        out_specs=[IN_VMEM] * len(out_shape),
        scratch_shapes=scratch_shapes,
        compiler_params=pltpu.CompilerParams(vmem_limit_bytes=VMEM_BYTES),
        **kw,
    )


def centered(rows):
    center = rows - jnp.mean(rows, axis=1, keepdims=True)
    inverse = lax.rsqrt(jnp.mean(center * center, axis=1, keepdims=True) + EPS)
    return center * inverse, inverse


def norm_back(grad, scaled, inverse, gain):
    through = grad * gain
    return inverse * (
        through
        - jnp.mean(through, axis=1, keepdims=True)
        - scaled * jnp.mean(through * scaled, axis=1, keepdims=True)
    )


def picked(route, head, expert):
    return (route[:, 2 * head : 2 * head + 1] == expert) | (
        route[:, 2 * head + 1 : 2 * head + 2] == expert
    )


def pick_of(route, core, pair, expert):
    one = picked(route, 2 * pair, expert)
    two = picked(route, 2 * pair + 1, expert)
    return jnp.where(core == 0, one.astype(F32), two.astype(F32))


def prepare_kernel(spot, value_weight, key_weight, query_weight, rel_weight, value_router, out_router, out_weight, wide, rel, out_wide):
    core = spot[0]
    blank = jnp.zeros((SLOT - DH, D), BF16)

    def fill(target, slot, source, start):
        target[slot : slot + DH, :] = source[pl.ds(pl.multiple_of(start, DH), DH), :]
        target[slot + DH : slot + SLOT, :] = blank

    for pair in range(2):
        head = 2 * pair + core
        for expert in range(E):
            slot = (pair * E + expert) * SLOT
            fill(wide, slot, value_weight, (head * E + expert) * DH)
            fill(out_wide, slot, out_weight, (head * E + expert) * DH)
        fill(wide, KEY_AT + pair * SLOT, key_weight, head * DH)
        fill(wide, QUERY_AT + pair * SLOT, query_weight, head * DH)
    fill(rel, 0, rel_weight, (2 * spot[1] + core) * DH)
    routers = []
    for router in (value_router, out_router):
        for pair in range(2):
            one = router[2 * pair * E : (2 * pair + 1) * E, :].astype(F32)
            two = router[(2 * pair + 1) * E : (2 * pair + 2) * E, :].astype(F32)
            routers.append(jnp.where(core == 0, one, two))
    routers.append(jnp.zeros((SLOT - 4 * E, D), F32))
    wide[ROUTER_AT:, :] = jnp.concatenate(routers, axis=0).astype(BF16)


def prepare(spot, value_weight, key_weight, query_weight, rel_weight, value_router, out_router, out_weight):
    return local_call(
        prepare_kernel, [struct((WIDE, D)), struct((SLOT, D)), struct((EXPERTS, D))], smem=1, vmem=7
    )(spot, value_weight.T, key_weight.T, query_weight.T, rel_weight.T, value_router.T, out_router.T, out_weight)


def project_kernel(spot, rows, gain, shift, wide, route, normed, experts, logits, pay, full):
    step = pl.program_id(0)
    scaled, _ = centered(rows[...].astype(F32))
    low = (scaled * gain[...].astype(F32) + shift[...].astype(F32)).astype(BF16)
    normed[...] = low
    full[...] = dot(low, wide[...], 1, 1)
    experts[...] = full[:, :EXPERTS].astype(BF16)
    logit = full[:, ROUTER_AT:WIDE]
    logits[...] = logit
    gate = jax.nn.sigmoid(logit)
    routes = route[...]
    for pair in range(2):
        total = jnp.zeros((BLOCK, SLOT), F32)
        for expert in range(E):
            slot = pair * E + expert
            weight = gate[:, slot : slot + 1] * pick_of(routes, spot[0], pair, expert)
            total += weight * full[:, slot * SLOT : (slot + 1) * SLOT]
        pay[pair, step] = full[:, KEY_AT + pair * SLOT : KEY_AT + (pair + 1) * SLOT].astype(BF16)
        pay[pair, 4 + step] = total.astype(BF16)

        def keep_query(pair=pair):
            pay[pair, 6 + step] = full[:, QUERY_AT + pair * SLOT : QUERY_AT + (pair + 1) * SLOT].astype(BF16)

        pl.when(step >= 2)(keep_query)


def project(spot, rows, gain, shift, wide, route):
    block = lambda width: pl.BlockSpec((BLOCK, width), lambda step: (step, 0))
    fixed = lambda *shape: pl.BlockSpec(shape, lambda step: (0,) * len(shape))
    return pl.pallas_call(
        project_kernel,
        grid=(4,),
        out_shape=[struct((4 * BLOCK, D)), struct((4 * BLOCK, EXPERTS)), struct((4 * BLOCK, SLOT), F32), struct((2, 10, BLOCK, SLOT))],
        in_specs=[IN_SMEM, block(D), fixed(1, D), fixed(1, D), fixed(WIDE, D), block(2 * H)],
        out_specs=[block(D), block(EXPERTS), block(SLOT), fixed(2, 10, BLOCK, SLOT)],
        scratch_shapes=[pltpu.VMEM((BLOCK, WIDE), F32)],
        compiler_params=pltpu.CompilerParams(vmem_limit_bytes=VMEM_BYTES),
    )(spot, rows, gain, shift, wide, route)


def spots_of(core, chip):
    return [
        chip * 512 + core * BLOCK,
        chip * 512 + (1 - core) * BLOCK,
        (1 - chip) * 512 + core * BLOCK,
        (1 - chip) * 512 + (1 - core) * BLOCK,
    ]


def rows_at(start):
    return pl.ds(pl.multiple_of(start, BLOCK), BLOCK)


def attention_kernel(spot, own, peer, bias_u, bias_v, far_rel, attended, probs, keys, values, qu, qv, back):
    shown = spot[2]
    places = spots_of(spot[0], spot[1])
    for chip, pay in ((0, own), (1, peer)):
        for side in range(2):
            start = places[2 * chip + side]
            keys[rows_at(start), :] = pay[side]
            keys[rows_at(start + LEN), :] = pay[2 + side]
            values[rows_at(start), :] = pay[4 + side]
            values[rows_at(start + LEN), :] = pay[6 + side]
            query = pay[8 + side].astype(F32)
            qu[rows_at(start), :] = (query + bias_u[...]).astype(BF16)
            qv[rows_at(start), :] = (query + bias_v[...]).astype(BF16)
    for block in range(LEN // BLOCK):
        rows = pl.ds(block * BLOCK, BLOCK)
        width = LEN + (block + 1) * BLOCK
        first_far = 2 * LEN - width
        content = dot(qu[rows, :], keys[:width, :], 1, 1)
        far = dot(qv[rows, :], far_rel[first_far:, :], 1, 1)
        near = pltpu.roll(far, width - BLOCK + 1, 1, stride=1, stride_axis=0)
        row_at = lax.broadcasted_iota(jnp.int32, (BLOCK, width), 0) + (LEN + block * BLOCK)
        key_at = lax.broadcasted_iota(jnp.int32, (BLOCK, width), 1)
        visible = (key_at <= row_at) & (key_at >= LEN - shown)
        scores = jnp.where(visible, (content + near) * SCALE, MASKED)
        highest = jnp.max(scores, axis=1, keepdims=True)
        weights = jnp.exp(scores - highest)
        total = jnp.sum(weights, axis=1, keepdims=True)
        low = (weights * (1.0 / total)).astype(BF16)
        probs[rows, :width] = low
        attended[rows, :] = dot(low, values[:width, :], 1, 0)
    for number, start in enumerate(places):
        back[number] = attended[rows_at(start), :].astype(BF16)


def attention(spot, own, peer, bias_u, bias_v, far_rel):
    return local_call(
        attention_kernel,
        [
            struct((LEN, SLOT), F32),
            struct((LEN, 2 * LEN)),
            struct((2 * LEN, SLOT)),
            struct((2 * LEN, SLOT)),
            struct((LEN, SLOT)),
            struct((LEN, SLOT)),
            struct((4, BLOCK, SLOT)),
        ],
        smem=1,
        vmem=5,
    )(spot, own, peer, bias_u, bias_v, far_rel)


def two_heads(chip, own, peer):
    first = jnp.where(chip == 0, own.astype(F32), peer.astype(F32))
    second = jnp.where(chip == 0, peer.astype(F32), own.astype(F32))
    return first, second


def mix_kernel(spot, own, peer, logits, route, out_wide, mixed, partial_out):
    heads = two_heads(spot[1], own[...].reshape(2 * BLOCK, SLOT), peer[...].reshape(2 * BLOCK, SLOT))
    gate = jax.nn.sigmoid(logits[2 * BLOCK :, :])
    routes = route[...]
    for pair in range(2):
        for expert in range(E):
            slot = pair * E + expert
            weight = gate[:, 2 * E + slot : 2 * E + slot + 1] * pick_of(routes, spot[0], pair, expert)
            mixed[:, slot * SLOT : (slot + 1) * SLOT] = (weight * heads[pair]).astype(BF16)
    partial_out[...] = dot(mixed[...], out_wide[...]).astype(BF16)


def mix(spot, own, peer, logits, route, out_wide):
    return local_call(
        mix_kernel, [struct((2 * BLOCK, EXPERTS)), struct((2 * BLOCK, D))], smem=1, vmem=5
    )(spot, own, peer, logits, route, out_wide)


def feed_kernel(
    spot,
    rows,
    part_mine,
    part_theirs,
    cot,
    gain,
    shift,
    up,
    up_bias,
    down,
    down_bias,
    resid,
    final_mine,
    final_theirs,
    grad_part,
    grad_up,
    grad_up_bias,
    grad_down,
    low,
    low_turned,
    sum_out,
    sum_grad,
):
    step = pl.program_id(0)

    def first():
        for side in range(2):
            here = slice(side * BLOCK, (side + 1) * BLOCK)
            there = slice((1 - side) * BLOCK, (2 - side) * BLOCK)
            total = rows[here, :].astype(F32) + (part_mine[here, :].astype(F32) + part_theirs[there, :].astype(F32))
            resid[here, :] = total
            scaled, _ = centered(total)
            low[here, :] = (scaled * gain[...].astype(F32) + shift[...].astype(F32)).astype(BF16)
        low_turned[...] = low[...].T
        sum_out[...] = jnp.zeros_like(sum_out)
        sum_grad[...] = jnp.zeros_like(sum_grad)

    pl.when(step == 0)(first)
    before = dot(low[...], up[...]) + up_bias[...].astype(F32)
    below = 0.5 * (1.0 + lax.erf(before * (0.5**0.5)))
    hidden = (before * below).astype(BF16)
    slope = below + before * (jnp.exp(-0.5 * before * before) * ((2.0 * math.pi) ** -0.5))
    grad_before = dot(cot[...], down[...], 1, 1) * slope
    grad_low = grad_before.astype(BF16)
    grad_up_bias[...] = jnp.sum(grad_low.astype(F32), axis=0, keepdims=True)
    sum_out[...] += dot(hidden, down[...])
    sum_grad[...] += dot(grad_low, up[...], 1, 1)
    grad_up[...] = dot(low_turned[...], grad_low).astype(BF16)
    grad_down[...] = dot(hidden, cot[...], 0, 0).astype(BF16)

    def last():
        final_mine[...] = resid[:BLOCK, :] + sum_out[:BLOCK, :] + down_bias[...].astype(F32)
        final_theirs[...] = sum_out[BLOCK:, :].astype(BF16)
        grad_part[...] = sum_grad[...].astype(BF16)

    pl.when(step == pl.num_programs(0) - 1)(last)


def feed(spot, rows, part_mine, part_theirs, cot, gain, shift, up, up_bias, down, down_bias):
    fixed = lambda *shape: pl.BlockSpec(shape, lambda step, spot: (0,) * len(shape))
    steps = FF // 2 // BLOCK
    columns = lambda count: pl.BlockSpec((count, BLOCK), lambda step, spot: (0, spot[0] * steps + step))
    return pl.pallas_call(
        feed_kernel,
        grid_spec=pltpu.PrefetchScalarGridSpec(
            num_scalar_prefetch=1,
            grid=(steps,),
            in_specs=[
                pl.BlockSpec((2 * BLOCK, D), lambda step, spot: (1, 0)),
                fixed(2 * BLOCK, D),
                fixed(2 * BLOCK, D),
                fixed(2 * BLOCK, D),
                fixed(1, D),
                fixed(1, D),
                columns(D),
                columns(1),
                pl.BlockSpec((BLOCK, D), lambda step, spot: (spot[0] * steps + step, 0)),
                fixed(1, D),
            ],
            out_specs=[
                fixed(2 * BLOCK, D),
                fixed(BLOCK, D),
                fixed(BLOCK, D),
                fixed(2 * BLOCK, D),
                pl.BlockSpec((D, BLOCK), lambda step, spot: (0, step)),
                pl.BlockSpec((1, BLOCK), lambda step, spot: (0, step)),
                pl.BlockSpec((BLOCK, D), lambda step, spot: (step, 0)),
            ],
            scratch_shapes=[
                pltpu.VMEM((2 * BLOCK, D), BF16),
                pltpu.VMEM((D, 2 * BLOCK), BF16),
                pltpu.VMEM((2 * BLOCK, D), F32),
                pltpu.VMEM((2 * BLOCK, D), F32),
            ],
        ),
        out_shape=[
            struct((2 * BLOCK, D), F32),
            struct((BLOCK, D), F32),
            struct((BLOCK, D)),
            struct((2 * BLOCK, D)),
            struct((D, FF // 2)),
            struct((1, FF // 2), F32),
            struct((FF // 2, D)),
        ],
        compiler_params=pltpu.CompilerParams(vmem_limit_bytes=VMEM_BYTES),
    )(spot, rows, part_mine, part_theirs, cot, gain, shift, up, up_bias, down, down_bias)


def unmix_kernel(
    spot,
    resid,
    grad_mine,
    grad_theirs,
    cot,
    gain,
    own,
    peer,
    mixed,
    logits,
    route,
    out_wide,
    final_mine,
    final_theirs,
    grad_resid,
    pay,
    grad_logit,
    grad_out,
    sums,
    result,
    grad_low,
    grad_mixed,
):
    result[...] = (final_mine[...] + final_theirs[...].astype(F32)).astype(BF16)
    for side in range(2):
        here = slice(side * BLOCK, (side + 1) * BLOCK)
        there = slice((1 - side) * BLOCK, (2 - side) * BLOCK)
        scaled, inverse = centered(resid[here, :])
        grad = grad_mine[here, :].astype(F32) + grad_theirs[there, :].astype(F32)
        above = cot[here, :].astype(F32)
        total = above + norm_back(grad, scaled, inverse, gain[...].astype(F32))
        grad_low[here, :] = total.astype(BF16)
        if side == 0:
            grad_resid[...] = total
            sums[0:1, :] = jnp.sum(grad * scaled, axis=0, keepdims=True)
            sums[1:2, :] = jnp.sum(grad, axis=0, keepdims=True)
            sums[2:3, :] = jnp.sum(above, axis=0, keepdims=True)
    grad_mixed[...] = dot(grad_low[...], out_wide[...], 1, 1)
    heads = two_heads(spot[1], own[...].reshape(2 * BLOCK, SLOT), peer[...].reshape(2 * BLOCK, SLOT))
    gate = jax.nn.sigmoid(logits[2 * BLOCK :, :])
    routes = route[...]
    lane = lax.broadcasted_iota(jnp.int32, (2 * BLOCK, SLOT), 1)
    logit_sum = jnp.zeros((2 * BLOCK, SLOT), F32)
    totals = []
    for pair in range(2):
        total = jnp.zeros((2 * BLOCK, SLOT), F32)
        for expert in range(E):
            slot = pair * E + expert
            sig = gate[:, 2 * E + slot : 2 * E + slot + 1]
            pick = pick_of(routes, spot[0], pair, expert)
            part = grad_mixed[:, slot * SLOT : (slot + 1) * SLOT]
            total += part * (sig * pick)
            grad_gate = jnp.sum(part * heads[pair], axis=1, keepdims=True)
            logit_sum += jnp.where(lane == 2 * E + slot, grad_gate * pick * sig * (1.0 - sig), 0.0)
        totals.append(total)
    grad_logit[...] = logit_sum.astype(BF16)
    mine = jnp.where(spot[1] == 0, totals[0], totals[1]).astype(BF16)
    other = jnp.where(spot[1] == 0, totals[1], totals[0]).astype(BF16)
    pay[0, 0], pay[0, 1] = mine[:BLOCK], mine[BLOCK:]
    pay[1, 0], pay[1, 1] = other[:BLOCK], other[BLOCK:]
    grad_out[...] = dot(grad_low[...], mixed[...], 0, 0).astype(BF16)


def unmix(spot, resid, grad_mine, grad_theirs, cot, gain, own, peer, mixed, logits, route, out_wide, final_mine, final_theirs):
    return local_call(
        unmix_kernel,
        [
            struct((BLOCK, D), F32),
            struct((2, 2, BLOCK, SLOT)),
            struct((2 * BLOCK, SLOT)),
            struct((D, EXPERTS)),
            struct((8, D), F32),
            struct((BLOCK, D)),
        ],
        [pltpu.VMEM((2 * BLOCK, D), BF16), pltpu.VMEM((2 * BLOCK, EXPERTS), F32)],
        smem=1,
        vmem=13,
    )(spot, resid, grad_mine, grad_theirs, cot, gain, own, peer, mixed, logits, route, out_wide, final_mine, final_theirs)


def unproject_kernel(spot, own, peer, normed, experts, logits, route, grad_logit, wide, grad_part, grad_wide, grad_all, turned):
    step = pl.program_id(0)
    flat = [own[step], own[4 + step], peer[step], peer[4 + step]]
    key_heads = two_heads(spot[1], flat[0], flat[2])
    value_heads = two_heads(spot[1], flat[1], flat[3])
    token = step >= 2
    query_at = jnp.where(token, 6 + step, 8)
    query_heads = two_heads(spot[1], own[query_at], peer[query_at])
    keep = jnp.where(token, 1.0, 0.0)
    gate = jax.nn.sigmoid(logits[...])
    routes = route[...]
    rows = rows_at(step * BLOCK)
    lane = lax.broadcasted_iota(jnp.int32, (BLOCK, SLOT), 1)
    logit_sum = grad_logit[rows_at(jnp.where(token, step - 2, 0) * BLOCK), :].astype(F32) * keep
    for pair in range(2):
        for expert in range(E):
            slot = pair * E + expert
            cols = slice(slot * SLOT, (slot + 1) * SLOT)
            sig = gate[:, slot : slot + 1]
            pick = pick_of(routes, spot[0], pair, expert)
            grad_all[rows, cols] = ((sig * pick) * value_heads[pair]).astype(BF16)
            grad_gate = jnp.sum(value_heads[pair] * experts[:, cols].astype(F32), axis=1, keepdims=True)
            logit_sum += jnp.where(lane == slot, grad_gate * pick * sig * (1.0 - sig), 0.0)
        grad_all[rows, KEY_AT + pair * SLOT : KEY_AT + (pair + 1) * SLOT] = key_heads[pair].astype(BF16)
        grad_all[rows, QUERY_AT + pair * SLOT : QUERY_AT + (pair + 1) * SLOT] = (keep * query_heads[pair]).astype(BF16)
    grad_all[rows, ROUTER_AT:WIDE] = logit_sum.astype(BF16)
    grad_part[...] = dot(grad_all[rows, :], wide[...]).astype(BF16)
    turned[:, rows] = normed[...].T

    def last():
        for part in range(5):
            cols = slice(part * 384, (part + 1) * 384)
            grad_wide[:, cols] = dot(turned[...], grad_all[:, cols]).astype(BF16)

    pl.when(step == 3)(last)


def unproject(spot, own, peer, normed, experts, logits, route, grad_logit, wide):
    block = lambda width: pl.BlockSpec((BLOCK, width), lambda step: (step, 0))
    fixed = lambda *shape: pl.BlockSpec(shape, lambda step: (0,) * len(shape))
    return pl.pallas_call(
        unproject_kernel,
        grid=(4,),
        out_shape=[struct((4 * BLOCK, D)), struct((D, WIDE))],
        in_specs=[
            IN_SMEM,
            fixed(10, BLOCK, SLOT),
            fixed(10, BLOCK, SLOT),
            block(D),
            block(EXPERTS),
            block(SLOT),
            block(2 * H),
            fixed(2 * BLOCK, SLOT),
            fixed(WIDE, D),
        ],
        out_specs=[block(D), fixed(D, WIDE)],
        scratch_shapes=[pltpu.VMEM((4 * BLOCK, WIDE), BF16), pltpu.VMEM((D, 4 * BLOCK), BF16)],
        compiler_params=pltpu.CompilerParams(vmem_limit_bytes=VMEM_BYTES),
    )(spot, own, peer, normed, experts, logits, route, grad_logit, wide)


def place():
    dp = lax.axis_index("dp")
    sq = lax.axis_index("seq")
    return dict(x=dp // 8, z=(dp // 2) % 4, y=(sq // 2) * 2 + dp % 2, core=sq % 2)


def device_of(at):
    return (at["x"] * 8 + at["z"] * 2 + at["y"] % 2, (at["y"] // 2) * 2 + at["core"])


def moved(at, axis, steps):
    other = dict(at)
    other[axis] = (at[axis] + steps) % 4
    return device_of(other)


PLAIN = (("x", 4), ("z", 4), ("ylo", 2), ("yhi", 2))
SPLIT = (("xhi", 2), ("z", 4), ("ylo", 2), ("yhi", 2), ("xlo", 2))


def part_of(name, where):
    return {"hi": where // 2, "lo": where % 2}.get(name[1:], where)


def chunk_of(ref, dims, axis, where):
    return ref.at[tuple(part_of(name, where) if name[0] == axis else slice(None) for name, _ in dims)]


def without(dims, axes):
    return tuple(dim for dim in dims if dim[0][0] not in axes)


def lead_shape(dims):
    return tuple(size for _, size in dims)


def halves(width):
    one = (width // 2 + 127) // 128 * 128
    return (0, one), (one, width - one)


def each_block(lead, step):
    count = math.prod(lead)
    if not lead:
        step(Ellipsis)
        return

    def run(flat, carry):
        index = []
        for size in reversed(lead):
            index.insert(0, flat % size)
            flat = flat // size
        step(tuple(index))
        return carry

    lax.fori_loop(0, count, run, 0)


class Links:
    def __init__(self, send_sem, recv_sem):
        self.send_sem, self.recv_sem, self.made = send_sem, recv_sem, []

    def prepared(self, src, dst, device):
        slot = len(self.made)
        copy = pltpu.make_async_remote_copy(
            src_ref=src,
            dst_ref=dst,
            send_sem=self.send_sem.at[slot],
            recv_sem=self.recv_sem.at[slot],
            device_id=device,
            device_id_type=MESH,
        )
        self.made.append(copy)
        return copy

    def send(self, src, dst, device):
        copy = self.prepared(src, dst, device)
        copy.start()
        return copy


def added(target, *terms):
    def add(index):
        total = terms[0][index].astype(F32)
        for term in terms[1:]:
            total += term[index].astype(F32)
        target[index] = total.astype(target.dtype)

    return add


class Stage:
    def __init__(self, links, at, ref, dims, axis, width, bufs, after):
        self.links, self.at, self.axis, self.bufs, self.after = links, at, axis, bufs, after
        self.left = lead_shape(without(dims, axis))
        self.cols = [pl.ds(*half) for half in halves(width)]
        self.near = [chunk_of(ref, dims, axis, (at[axis] + steps) % 4) for steps in range(4)]
        self.made = []

    def launch_far(self):
        for side, steps in ((0, 1), (1, 3)):
            src = self.near[2].at[..., self.cols[side]]
            self.made.append(self.links.send(src, self.bufs[side], moved(self.at, self.axis, steps)))

    def launch_near(self):
        for side, steps in ((0, 1), (1, 3)):
            src = self.near[steps].at[..., self.cols[1 - side]]
            self.made.append(self.links.send(src, self.bufs[2 + side], moved(self.at, self.axis, steps)))

    def forward(self):
        for side, steps in ((0, 1), (1, 3)):
            self.made[side].wait_recv()
            held = self.bufs[side]
            each_block(self.left, added(held, held, self.near[steps].at[..., self.cols[side]]))
            self.made.append(self.links.send(held, self.bufs[4 + side], moved(self.at, self.axis, steps)))

    def collect(self):
        for copy in self.made[2:]:
            copy.wait_recv()
        for side in (0, 1):
            cols = self.cols[side]
            terms = self.near[0].at[..., cols], self.bufs[4 + side], self.bufs[3 - side]
            each_block(self.left, added(self.after.at[..., cols], *terms))


def stage_scratch(dims, axis, rows, width):
    left = lead_shape(without(dims, axis))
    (_, one), (_, two) = halves(width)
    return [pltpu.VMEM(left + (rows, size), BF16) for size in (one, two, two, one, one, two)]


def launch(stages):
    for stage in stages:
        stage.launch_far()
    for stage in stages:
        stage.launch_near()


def greet(devices):
    barrier = pltpu.get_barrier_semaphore()
    for device in devices:
        pl.semaphore_signal(barrier, inc=1, device_id=device, device_id_type=MESH)


UP, DOWN, OUT, WIDE_GRAD, REST = range(5)
LAYOUTS = (PLAIN, SPLIT, PLAIN, PLAIN, PLAIN)
SHAPES = ((16, FF // 2), (32, D), (16, EXPERTS), (16, WIDE), (16, 2 * SLOT))
EARLY = (
    (UP, 0, 1792, "xyz"),
    (DOWN, 0, 768, "yzx"),
    (OUT, 0, 256, "yzx"),
    (OUT, 256, 1024, "zxy"),
    (UP, 1792, 256, "zxy"),
    (DOWN, 768, 256, "zxy"),
)
LATE = (
    (WIDE_GRAD, 0, 768, "xyz"),
    (WIDE_GRAD, 768, 768, "yzx"),
    (WIDE_GRAD, 1536, 384, "zxy"),
    (REST, 0, 256, "zxy"),
)


def dims_after(piece, phases):
    return without(LAYOUTS[piece[0]], piece[3][:phases])


def after_shape(piece, phases):
    return lead_shape(dims_after(piece, phases)) + (SHAPES[piece[0]][0], piece[2])


def phase_scratch(piece, phase):
    return stage_scratch(dims_after(piece, phase), piece[3][phase], SHAPES[piece[0]][0], piece[2])


def stage_for(links, at, piece, phase, ref, bufs, after):
    return Stage(links, at, ref, dims_after(piece, phase), piece[3][phase], piece[2], bufs, after)


KEY_BLOCKS = 2 * LEN // BLOCK


def attention_back_kernel(*refs):
    refs = list(refs)
    take = lambda count: [refs.pop(0) for _ in range(count)]
    given, qu, qv, keys, values, far_rel, probs, attended = take(8)
    grads = take(3)
    pay, pay_in, sums, grad_far = take(4)
    afters = take(len(EARLY))
    send_sem, recv_sem = take(2)
    given_in, grad_out, grad_scores, grad_u, grad_query, grad_keys, grad_values, far_sum = take(8)
    links = Links(send_sem, recv_sem)
    at = place()
    peer = moved(at, "y", 2)
    devices = [moved(at, axis, steps) for axis in "xyz" for steps in (1, 3)] + [peer]
    greet(devices)
    pl.semaphore_wait(pltpu.get_barrier_semaphore(), len(devices))
    arrived = links.send(given.at[1], given_in, peer)
    stages = []
    for piece, after in zip(EARLY, afters):
        source = grads[piece[0]].at[..., pl.ds(piece[1], piece[2])]
        stages.append(stage_for(links, at, piece, 0, source, take(6), after))
    launch(stages)
    places = spots_of(at["core"], at["y"] // 2)
    for side in range(2):
        grad_out[rows_at(places[side]), :] = given[0, side]
    arrived.wait_recv()
    for side in range(2):
        grad_out[rows_at(places[2 + side]), :] = given_in[side]
    moving = []

    def give(first, held, base):
        for side in range(2):
            pay[first + side] = held[rows_at(places[side] + base), :]
            src = held.at[rows_at(places[2 + side] + base)]
            moving.append(links.send(src, pay_in.at[first + side], peer))

    def rows_seeing(block):
        return pl.ds(max(0, block - 4) * BLOCK, LEN - max(0, block - 4) * BLOCK)

    for block in range(KEY_BLOCKS):
        cols, rows = pl.ds(block * BLOCK, BLOCK), rows_seeing(block)
        grad_values[cols, :] = dot(probs[rows, cols], grad_out[rows, :], 0, 0).astype(BF16)
    give(4, grad_values, 0)
    give(6, grad_values, LEN)
    blocks = LEN // BLOCK
    sum_u = jnp.zeros((1, SLOT), F32)
    for block in range(blocks):
        rows = pl.ds(block * BLOCK, BLOCK)
        width = LEN + (block + 1) * BLOCK
        above = grad_out[rows, :]
        grad_probs = dot(above, values[:width, :], 1, 1)
        inner = jnp.sum(above.astype(F32) * attended[rows, :], axis=1, keepdims=True)
        scores = (probs[rows, :width].astype(F32) * ((grad_probs - inner) * SCALE)).astype(BF16)
        grad_scores[rows, :width] = scores
        part = dot(scores, keys[:width, :])
        grad_u[rows, :] = part
        sum_u += jnp.sum(part, axis=0, keepdims=True)
    for stage in stages:
        stage.forward()
    for block in range(KEY_BLOCKS):
        cols, rows = pl.ds(block * BLOCK, BLOCK), rows_seeing(block)
        grad_keys[cols, :] = dot(grad_scores[rows, cols], qu[rows, :], 0, 0).astype(BF16)
    give(0, grad_keys, 0)
    give(2, grad_keys, LEN)
    far_sum[...] = jnp.zeros_like(far_sum)
    down = lax.broadcasted_iota(jnp.int32, (BLOCK, BLOCK), 0)
    across = lax.broadcasted_iota(jnp.int32, (BLOCK, BLOCK), 1)
    flip = (down + across == BLOCK - 1).astype(F32).astype(BF16)
    sum_v = jnp.zeros((1, SLOT), F32)
    for block in range(blocks):
        rows = pl.ds(block * BLOCK, BLOCK)
        width = LEN + (block + 1) * BLOCK
        first_far = 2 * LEN - width
        far = pltpu.roll(dot(flip, grad_scores[rows, :width]), 0, 1, stride=1, stride_axis=0).astype(BF16)
        turned = dot(flip, far).astype(BF16)
        part = dot(turned, far_rel[first_far:, :])
        far_sum[first_far:, :] += dot(turned, qv[rows, :], 0, 0)
        grad_query[rows, :] = (grad_u[rows, :] + part).astype(BF16)
        sum_v += jnp.sum(part, axis=0, keepdims=True)
    give(8, grad_query, 0)
    sums[0:1, :] = sum_u
    sums[1:2, :] = sum_v
    grad_far[...] = far_sum[...].astype(BF16)
    for stage in stages:
        stage.collect()
    for copy in moving:
        copy.wait_recv()
    for copy in links.made:
        copy.wait_send()


def attention_back(given, qu, qv, keys, values, far_rel, probs, attended, grads):
    scratch = []
    for piece in EARLY:
        scratch += phase_scratch(piece, 0)
    copies = 1 + 10 + 6 * len(EARLY)
    seq = (2 * LEN, SLOT)
    outs = [struct((10, BLOCK, SLOT)), struct((10, BLOCK, SLOT)), struct((2, SLOT), F32), struct(seq)]
    outs += [struct(after_shape(piece, 1)) for piece in EARLY]
    return pl.pallas_call(
        attention_back_kernel,
        out_shape=outs,
        in_specs=[IN_VMEM] * 11,
        out_specs=[IN_VMEM] * len(outs),
        scratch_shapes=[
            pltpu.SemaphoreType.DMA((copies,)),
            pltpu.SemaphoreType.DMA((copies,)),
            pltpu.VMEM((2, BLOCK, SLOT), BF16),
            pltpu.VMEM((LEN, SLOT), BF16),
            pltpu.VMEM((LEN, 2 * LEN), BF16),
            pltpu.VMEM((LEN, SLOT), F32),
            pltpu.VMEM((LEN, SLOT), BF16),
            pltpu.VMEM(seq, BF16),
            pltpu.VMEM(seq, BF16),
            pltpu.VMEM(seq, F32),
        ]
        + scratch,
        compiler_params=pltpu.CompilerParams(
            collective_id=1, has_side_effects=True, vmem_limit_bytes=VMEM_BYTES
        ),
    )(given, qu, qv, keys, values, far_rel, probs, attended, *grads)


COUNT_ROW = 2 * H
VECTOR_ROW = 16
UP_BIAS_ROW = VECTOR_ROW + 5 * 8
SMALL_ROWS = UP_BIAS_ROW + FF // SLOT


def lay(target, first, vector):
    for row in range(vector.shape[1] // SLOT):
        target[first + row : first + row + 1, :] = vector[:, row * SLOT : (row + 1) * SLOT]


def final_kernel(*refs):
    refs = list(refs)
    take = lambda count: [refs.pop(0) for _ in range(count)]
    rows, part, gain, grad_resid, feed_sums, grad_up_bias, small_in = take(7)
    early = take(len(EARLY))
    late = dict(zip((WIDE_GRAD, REST), take(2)))
    grad_tokens, small_out, down_out = take(3)
    both = dict(zip((UP, OUT, WIDE_GRAD, REST), take(4)))
    send_sem, recv_sem, own_sem, part_in, half_bias = take(5)
    totals = take(5)
    slots = take(4)
    links = Links(send_sem, recv_sem)
    at = place()
    core = at["core"]
    sibling = dict(at)
    sibling["core"] = 1 - core
    sibling = device_of(sibling)
    high, low = at["x"] // 2, at["x"] % 2
    stays = (high == low) & (low == core)
    ahead, behind = dict(at), dict(at)
    ahead["x"], ahead["core"] = 2 * core + high, low
    behind["x"], behind["core"] = 2 * low + core, high
    ahead, behind = device_of(ahead), device_of(behind)
    devices = [moved(at, axis, steps) for axis in "xyz" for steps in (1, 2, 3)] + [sibling]
    greet(devices)

    def greet_more():
        greet([ahead, behind])
        pl.semaphore_wait(pltpu.get_barrier_semaphore(), len(devices) + 2)

    pl.when(jnp.logical_not(stays))(greet_more)
    pl.when(stays)(lambda: pl.semaphore_wait(pltpu.get_barrier_semaphore(), len(devices)))
    halves_in = [links.send(part.at[2 * side + 1], part_in.at[side], sibling) for side in range(2)]

    jobs = []
    for piece in LATE:
        jobs.append([piece, 0, late[piece[0]].at[..., pl.ds(piece[1], piece[2])]])
    for piece, ref in zip(EARLY, early):
        jobs.append([piece, 1, ref])

    def begin():
        stages = []
        for job in jobs:
            piece, phase, ref = job
            bufs = take(6)
            after = take(1)[0] if phase < 2 else totals[piece[0]].at[:, pl.ds(piece[1], piece[2])]
            stages.append(stage_for(links, at, piece, phase, ref, bufs, after))
            job[1:] = [phase + 1, after]
        launch(stages)
        jobs[:] = [job for job in jobs if job[1] < 3]
        return stages

    def spread(number, value):
        axis = "xyz"[number]
        here = slots[number].at[at[axis]]
        here[...] = value
        return [links.send(here, here, moved(at, axis, steps)) for steps in (1, 2, 3)]

    def gathered(number, copies):
        for copy in copies:
            copy.wait_recv()
        one = slots[number]
        return (one[0] + one[1]) + (one[2] + one[3])

    stages = begin()
    for copy in halves_in:
        copy.wait_recv()
    gain_sum = jnp.zeros((1, D), F32)
    bias_sum = jnp.zeros((1, D), F32)
    for side in range(2):
        scaled, inverse = centered(rows[side].astype(F32))
        grad = part[2 * side].astype(F32) + part_in[side].astype(F32)
        gain_sum += jnp.sum(grad * scaled, axis=0, keepdims=True)
        bias_sum += jnp.sum(grad, axis=0, keepdims=True)
        if side == 1:
            grad_tokens[...] = grad_resid[...] + norm_back(grad, scaled, inverse, gain[...].astype(F32))
    small = small_out
    small[:VECTOR_ROW, :] = small_in[...]
    lay(small, VECTOR_ROW, gain_sum)
    lay(small, VECTOR_ROW + 8, bias_sum)
    for number in range(3):
        lay(small, VECTOR_ROW + 16 + 8 * number, feed_sums[number : number + 1, :])
    small[UP_BIAS_ROW:, :] = jnp.zeros((FF // SLOT, SLOT), F32)
    lay(half_bias, 0, grad_up_bias[...])
    half = FF // 2 // SLOT
    small[pl.ds(pl.multiple_of(UP_BIAS_ROW + core * half, 8), half), :] = half_bias[...]
    copies = spread(0, small[...])
    for stage in stages:
        stage.forward()
    for stage in stages:
        stage.collect()
    stages = begin()
    copies = spread(1, gathered(0, copies))
    for stage in stages:
        stage.forward()
    for stage in stages:
        stage.collect()
    stages = begin()
    copies = spread(2, gathered(1, copies))
    for stage in stages:
        stage.forward()
    for stage in stages:
        stage.collect()
    last = []
    pair = slots[3]
    pair[core] = gathered(2, copies)
    last.append(links.send(pair.at[core], pair.at[core], sibling))
    away = links.prepared(totals[DOWN], down_out, ahead)
    here = pltpu.make_async_copy(totals[DOWN], down_out, own_sem)
    pl.when(jnp.logical_not(stays))(away.start)
    pl.when(stays)(here.start)
    for array, out in both.items():
        other = pl.ds(pl.multiple_of((1 - core) * 8, 8), 8)
        last.append(links.send(totals[array].at[other], out.at[core], sibling))
        out[core] = totals[array][pl.ds(pl.multiple_of(core * 8, 8), 8), :]
    for copy in last:
        copy.wait_recv()
    small_out[...] = pair[0] + pair[1]
    pl.when(jnp.logical_not(stays))(away.wait)
    pl.when(stays)(here.wait)
    for copy in links.made:
        if copy is not away:
            copy.wait_send()


def final(rows, part, gain, grad_resid, feed_sums, grad_up_bias, small, early, late):
    jobs = [(piece, 0) for piece in LATE] + [(piece, 1) for piece in EARLY]
    scratch = []
    copies = 2 + 9 + 1 + 1 + 4
    while jobs:
        for piece, phase in jobs:
            scratch += phase_scratch(piece, phase)
            copies += 6
            if phase < 2:
                scratch.append(pltpu.VMEM(after_shape(piece, phase + 1), BF16))
        jobs = [(piece, phase + 1) for piece, phase in jobs if phase < 2]
    outs = [struct((BLOCK, D), F32), struct((SMALL_ROWS, SLOT), F32), struct(SHAPES[DOWN], F32)]
    outs += [struct((2, 8, SHAPES[array][1]), F32) for array in (UP, OUT, WIDE_GRAD, REST)]
    return pl.pallas_call(
        final_kernel,
        out_shape=outs,
        in_specs=[IN_VMEM] * (7 + len(EARLY) + 2),
        out_specs=[IN_VMEM] * len(outs),
        scratch_shapes=[
            pltpu.SemaphoreType.DMA((copies,)),
            pltpu.SemaphoreType.DMA((copies,)),
            pltpu.SemaphoreType.DMA,
            pltpu.VMEM((2, BLOCK, D), BF16),
            pltpu.VMEM((FF // 2 // SLOT, SLOT), F32),
        ]
        + [pltpu.VMEM(shape, F32) for shape in SHAPES]
        + [pltpu.VMEM((4, SMALL_ROWS, SLOT), F32)] * 3
        + [pltpu.VMEM((2, SMALL_ROWS, SLOT), F32)]
        + scratch,
        compiler_params=pltpu.CompilerParams(
            collective_id=2, has_side_effects=True, vmem_limit_bytes=VMEM_BYTES
        ),
    )(rows, part, gain, grad_resid, feed_sums, grad_up_bias, small, *early, *late)


def arrange_kernel(up, out, wide, rest, grad_up, grad_out, grad_value, grad_key, grad_query, grad_rel, grad_routers):
    grad_up[:, : FF // 2] = up[0]
    grad_up[:, FF // 2 :] = up[1]
    for head in range(H):
        core, pair = head % 2, head // 2
        for expert in range(E):
            slot = (pair * E + expert) * SLOT
            start = (head * E + expert) * DH
            grad_out[:, start : start + DH] = out[core, :, slot : slot + DH]
            grad_value[:, start : start + DH] = wide[core, :, slot : slot + DH]
        start = head * DH
        for target, source, slot in (
            (grad_key, wide, KEY_AT),
            (grad_query, wide, QUERY_AT),
            (grad_rel, rest, 0),
        ):
            slot += pair * SLOT
            target[:, start : start + DH] = source[core, :, slot : slot + DH]
    for kind in range(2):
        for head in range(H):
            at = ROUTER_AT + (2 * kind + head // 2) * E
            start = (kind * H + head) * E
            grad_routers[:, start : start + E] = wide[head % 2, :, at : at + E]


def arrange(up, out, wide, rest):
    widths = (FF, H * E * DH, H * E * DH, H * DH, H * DH, H * DH, 2 * H * E)
    return local_call(arrange_kernel, [struct((8, width), F32) for width in widths], vmem=4)(up, out, wide, rest)


def sinus_far():
    frequency = jnp.exp(jnp.arange(D // 2, dtype=jnp.int32).astype(F32) * (-2.0 * math.log(10000.0) / D))
    coarse = (64 * (31 - jnp.arange(32, dtype=jnp.int32))).astype(F32)[:, None] * frequency
    fine = (63 - jnp.arange(64, dtype=jnp.int32)).astype(F32)[:, None] * frequency
    sin_a, cos_a = jnp.sin(coarse)[:, None], jnp.cos(coarse)[:, None]
    sin_b, cos_b = jnp.sin(fine)[None], jnp.cos(fine)[None]
    sines = sin_a * cos_b + cos_a * sin_b
    cosines = cos_a * cos_b - sin_a * sin_b
    return jnp.concatenate([sines, cosines], axis=2).reshape(2 * LEN, D).astype(BF16)


def swap(value):
    return lax.ppermute(value, "seq", [(0, 1), (1, 0), (2, 3), (3, 2)])


def cross(value):
    return lax.ppermute(value, "seq", [(0, 2), (2, 0), (1, 3), (3, 1)])


def body(
    tokens,
    memory,
    cotangent,
    mem_len,
    value_route,
    output_route,
    attn_norm_gain,
    attn_norm_bias,
    query_weight,
    key_weight,
    rel_weight,
    bias_u,
    bias_v,
    value_router,
    value_weight,
    out_router,
    out_weight,
    ffn_norm_gain,
    ffn_norm_bias,
    up_weight,
    up_bias,
    down_weight,
    down_bias,
):
    seq_index = lax.axis_index("seq")
    core, chip = seq_index % 2, seq_index // 2
    spot = jnp.stack([core, chip, mem_len[0]]).astype(jnp.int32)
    row = lambda vector: vector.reshape(1, -1)
    tokens, memory, cotangent = tokens[0], memory[0], cotangent[0]
    routes = jnp.concatenate(
        [value_route[0].reshape(2 * BLOCK, 2 * H), output_route[0].reshape(BLOCK, 2 * H)], axis=0
    )
    memory_theirs, tokens_theirs, routes_theirs = swap(memory), swap(tokens), swap(routes)
    cot = jnp.concatenate([cotangent, swap(cotangent)], axis=0)
    rows = jnp.concatenate([memory, memory_theirs, tokens, tokens_theirs], axis=0)
    value_routes = jnp.stack(
        [routes[: 2 * BLOCK].reshape(2, BLOCK, 2 * H), routes_theirs[: 2 * BLOCK].reshape(2, BLOCK, 2 * H)], axis=1
    ).reshape(4 * BLOCK, 2 * H)
    out_routes = jnp.concatenate([routes[2 * BLOCK :], routes_theirs[2 * BLOCK :]], axis=0)
    wide, rel, out_wide = prepare(
        spot, value_weight, key_weight, query_weight, rel_weight, value_router, out_router, out_weight
    )
    head_bias = lambda bias: jnp.pad(
        lax.dynamic_slice_in_dim(bias.astype(F32), seq_index * DH, DH, 0), (0, SLOT - DH)
    ).reshape(1, SLOT)
    sinus = sinus_far()
    far_rel = dot(sinus, rel, 1, 1).astype(BF16)
    attn_gain = row(attn_norm_gain)
    normed, experts, logits, pay = project(spot, rows, attn_gain, row(attn_norm_bias), wide, value_routes)
    pay_own = jnp.where(chip == 0, pay[0], pay[1])
    pay_peer = cross(jnp.where(chip == 0, pay[1], pay[0]))
    attended, probs, keys, values, qu, qv, back = attention(
        spot, pay_own, pay_peer, head_bias(bias_u), head_bias(bias_v), far_rel
    )
    att_own, att_peer = back[:2], cross(back[2:])
    mixed, out_part = mix(spot, att_own, att_peer, logits, out_routes, out_wide)
    resid, final_mine, final_theirs, norm_part, grad_up, grad_up_bias, grad_down = feed(
        spot,
        rows,
        out_part,
        swap(out_part),
        cot,
        row(ffn_norm_gain),
        row(ffn_norm_bias),
        up_weight,
        row(up_bias),
        down_weight,
        row(down_bias),
    )
    grad_resid, grad_att, grad_out_logit, grad_out, feed_sums, result = unmix(
        spot,
        resid,
        norm_part,
        swap(norm_part),
        cot,
        row(ffn_norm_gain),
        att_own,
        att_peer,
        mixed,
        logits,
        out_routes,
        out_wide,
        final_mine,
        swap(final_theirs),
    )
    pay_back, pay_in, bias_sums, grad_far, *early = attention_back(
        grad_att,
        qu,
        qv,
        keys,
        values,
        far_rel,
        probs,
        attended,
        [
            grad_up.reshape(lead_shape(PLAIN) + SHAPES[UP]),
            grad_down.reshape(lead_shape(SPLIT) + SHAPES[DOWN]),
            grad_out.reshape(lead_shape(PLAIN) + SHAPES[OUT]),
        ],
    )
    grad_rel = dot(sinus, grad_far, 0, 0).astype(BF16)
    part, grad_wide = unproject(
        spot, pay_back, pay_in, normed, experts, logits, value_routes, grad_out_logit, wide
    )
    blank = jnp.zeros((), BF16)
    rest = jnp.concatenate([jnp.where(chip == 0, grad_rel, blank), jnp.where(chip == 1, grad_rel, blank)], axis=1)
    picks = jnp.arange(E, dtype=jnp.int32)
    chosen = (routes.reshape(3 * BLOCK, H, 2)[..., None] == picks).astype(F32).sum(axis=2)
    counts = jnp.concatenate(
        [chosen[: 2 * BLOCK].sum(axis=0).reshape(-1), chosen[2 * BLOCK :].sum(axis=0).reshape(-1)]
    )
    head_at = (jnp.arange(H) == seq_index).astype(F32)[:, None]
    small = jnp.concatenate(
        [
            head_at * bias_sums[0:1],
            head_at * bias_sums[1:2],
            jnp.pad(counts, (0, SLOT - 40)).reshape(1, SLOT),
            jnp.zeros((VECTOR_ROW - COUNT_ROW - 1, SLOT), F32),
        ],
        axis=0,
    )
    grad_tokens, small_sum, grad_down_own, up_both, out_both, wide_both, rest_both = final(
        jnp.stack([memory, tokens]),
        part.reshape(4, BLOCK, D),
        attn_gain,
        grad_resid,
        feed_sums,
        grad_up_bias,
        small,
        early,
        [
            grad_wide.reshape(lead_shape(PLAIN) + SHAPES[WIDE_GRAD]),
            rest.reshape(lead_shape(PLAIN) + SHAPES[REST]),
        ],
    )
    grad_up_own, grad_out_own, grad_value, grad_key, grad_query, grad_relative, grad_routers = arrange(
        up_both, out_both, wide_both, rest_both
    )
    device = lax.axis_index("dp") * 4 + seq_index
    vectors = lax.dynamic_slice_in_dim(small_sum[VECTOR_ROW:UP_BIAS_ROW].reshape(5, D), device * 8, 8, 1)
    grad_up_bias_own = lax.dynamic_slice_in_dim(small_sum[UP_BIAS_ROW:].reshape(FF), device * 32, 32, 0)
    per_head = lambda rows: rows[:, :DH].reshape(H * DH)
    return (
        result[None],
        grad_tokens[None],
        vectors[0],
        vectors[1],
        grad_query,
        grad_key,
        grad_relative,
        per_head(small_sum[:H]),
        per_head(small_sum[H : 2 * H]),
        grad_routers[:, : H * E],
        grad_value,
        grad_routers[:, H * E :],
        grad_out_own.T,
        vectors[2],
        vectors[3],
        grad_up_own,
        grad_up_bias_own,
        grad_down_own,
        vectors[4],
        jnp.round(small_sum[COUNT_ROW, :40]).astype(jnp.int32).reshape(2, H, E),
    )


def solution(mesh):
    in_specs = (
        P("dp", "seq", None),
        P("dp", "seq", None),
        P("dp", "seq", None),
        P("dp"),
        P("dp", None, "seq", None, None),
        P("dp", "seq", None, None),
        P(),
        P(),
        P(),
        P(),
        P(),
        P(),
        P(),
        P(),
        P(),
        P(),
        P(),
        P(),
        P(),
        P(),
        P(),
        P(),
        P(),
    )
    out_specs = (
        P("dp", "seq", None),
        P("dp", "seq", None),
        P(("dp", "seq")),
        P(("dp", "seq")),
        P(("dp", "seq"), None),
        P(("dp", "seq"), None),
        P(("dp", "seq"), None),
        P(),
        P(),
        P(("dp", "seq"), None),
        P(("dp", "seq"), None),
        P(("dp", "seq"), None),
        P(None, ("dp", "seq")),
        P(("dp", "seq")),
        P(("dp", "seq")),
        P(("dp", "seq"), None),
        P(("dp", "seq")),
        P(("dp", "seq"), None),
        P(("dp", "seq")),
        P(),
    )
    return jax.shard_map(body, mesh=mesh, in_specs=in_specs, out_specs=out_specs, check_vma=False)
```

```python
from functools import partial
import math

import jax
import jax.numpy as jnp
from jax import lax
from jax.experimental import pallas as pl
from jax.experimental.pallas import tpu as pltpu
from jax.sharding import PartitionSpec as P

D = 1024
H = 4
DH = 112
E = 5
FF = 4096
LEN = 1024
SLOT = 128
BLOCK = 256
EXPERTS = 2 * E * SLOT
KEY_AT = EXPERTS
QUERY_AT = KEY_AT + 2 * SLOT
ROUTER_AT = QUERY_AT + 2 * SLOT
WIDE = ROUTER_AT + SLOT
SCALE = DH ** (-0.5)
MASKED = -1e30
EPS = 1e-05
BF16 = jnp.bfloat16
F32 = jnp.float32
VMEM_BYTES = 60 * 1024 * 1024
IN_VMEM = pl.BlockSpec(memory_space=pltpu.VMEM)
IN_SMEM = pl.BlockSpec(memory_space=pltpu.SMEM)
ANYWHERE = pl.BlockSpec(memory_space=pl.ANY)
MESH = pl.DeviceIdType.MESH


def dot(left, right, left_dim=1, right_dim=0):
    return lax.dot_general(
        left, right, (((left_dim,), (right_dim,)), ((), ())), preferred_element_type=F32
    )


def struct(shape, kind=BF16):
    return jax.ShapeDtypeStruct(shape, kind)


def local_call(kernel, out_shape, scratch_shapes=(), smem=0, vmem=0, **kw):
    return pl.pallas_call(
        kernel,
        out_shape=out_shape,
        in_specs=[IN_SMEM] * smem + [IN_VMEM] * vmem,
        out_specs=[IN_VMEM] * len(out_shape),
        scratch_shapes=scratch_shapes,
        compiler_params=pltpu.CompilerParams(vmem_limit_bytes=VMEM_BYTES),
        **kw,
    )


def centered(rows):
    center = rows - jnp.mean(rows, axis=1, keepdims=True)
    inverse = lax.rsqrt(jnp.mean(center * center, axis=1, keepdims=True) + EPS)
    return center * inverse, inverse


def norm_back(grad, scaled, inverse, gain):
    through = grad * gain
    return inverse * (
        through
        - jnp.mean(through, axis=1, keepdims=True)
        - scaled * jnp.mean(through * scaled, axis=1, keepdims=True)
    )


def as_row(vector):
    return vector[...].astype(F32).reshape(1, vector.shape[0])


def chosen_lanes(route, first, core, lane, start):
    chosen = None
    for pair in range(2):
        for number in range(2):
            column = first + 4 * pair + number
            one = jnp.where(core == 0, route[:, column : column + 1], route[:, column + 2 : column + 3])
            hit = lane == one + (start + E * pair)
            chosen = hit if chosen is None else chosen | hit
    return chosen


def spots_of(core, chip):
    return [
        chip * 512 + core * BLOCK,
        chip * 512 + (1 - core) * BLOCK,
        (1 - chip) * 512 + core * BLOCK,
        (1 - chip) * 512 + (1 - core) * BLOCK,
    ]


def rows_at(start):
    return pl.ds(pl.multiple_of(start, BLOCK), BLOCK)


def attend(block, shown, qu, qv, keys, values, far_rel, attended, probs):
    rows = pl.ds(block * BLOCK, BLOCK)
    width = LEN + (block + 1) * BLOCK
    first_far = 2 * LEN - width
    content = dot(qu[rows, :], keys[:width, :], 1, 1)
    far = dot(qv[rows, :], far_rel[first_far:, :], 1, 1)
    near = pltpu.roll(far, width - BLOCK + 1, 1, stride=1, stride_axis=0)
    row_at = lax.broadcasted_iota(jnp.int32, (BLOCK, width), 0) + (LEN + block * BLOCK)
    key_at = lax.broadcasted_iota(jnp.int32, (BLOCK, width), 1)
    visible = (key_at <= row_at) & (key_at >= LEN - shown)
    scores = jnp.where(visible, (content + near) * SCALE, MASKED)
    highest = jnp.max(scores, axis=1, keepdims=True)
    weights = jnp.exp(scores - highest)
    total = jnp.sum(weights, axis=1, keepdims=True)
    low = (weights * (1.0 / total)).astype(BF16)
    probs[rows, :width] = low
    attended[rows, :] = dot(low, values[:width, :], 1, 0)


def two_heads(chip, own, peer):
    first = jnp.where(chip == 0, own.astype(F32), peer.astype(F32))
    second = jnp.where(chip == 0, peer.astype(F32), own.astype(F32))
    return first, second


def feed_kernel(
    spot,
    rows,
    part_mine,
    part_theirs,
    cot,
    gain,
    shift,
    up,
    up_bias,
    down,
    down_bias,
    resid,
    final_mine,
    final_theirs,
    grad_part,
    low,
    hidden_out,
    grad_before,
    grad_up_bias,
    sum_out,
    sum_grad,
):
    step = pl.program_id(0)

    def first():
        for side in range(2):
            here = slice(side * BLOCK, (side + 1) * BLOCK)
            total = rows[here, :].astype(F32) + (part_mine[here, :].astype(F32) + part_theirs[here, :].astype(F32))
            resid[here, :] = total
            scaled, _ = centered(total)
            low[here, :] = (scaled * as_row(gain) + as_row(shift)).astype(BF16)
        sum_out[...] = jnp.zeros_like(sum_out)
        sum_grad[...] = jnp.zeros_like(sum_grad)

    pl.when(step == 0)(first)
    before = dot(low[...], up[...]) + as_row(up_bias)
    below = 0.5 * (1.0 + lax.erf(before * (0.5**0.5)))
    hidden = (before * below).astype(BF16)
    hidden_out[...] = hidden
    slope = below + before * (jnp.exp(-0.5 * before * before) * ((2.0 * math.pi) ** -0.5))
    grad_low = (dot(cot[...], down[...], 1, 1) * slope).astype(BF16)
    grad_before[...] = grad_low
    grad_up_bias[...] = jnp.sum(grad_low.astype(F32), axis=0, keepdims=True)
    sum_out[...] += dot(hidden, down[...])
    sum_grad[...] += dot(grad_low, up[...], 1, 1)

    def last():
        final_mine[...] = resid[:BLOCK, :] + sum_out[:BLOCK, :] + as_row(down_bias)
        final_theirs[...] = sum_out[BLOCK:, :].astype(BF16)
        grad_part[...] = sum_grad[...].astype(BF16)

    pl.when(step == pl.num_programs(0) - 1)(last)


FEED_BLOCK = 512


def feed(spot, rows, part_mine, part_theirs, cot, gain, shift, up, up_bias, down, down_bias):
    fixed = lambda *shape: pl.BlockSpec(shape, lambda step, spot: (0,) * len(shape))
    steps = FF // 2 // FEED_BLOCK
    columns = lambda count: pl.BlockSpec((count, FEED_BLOCK), lambda step, spot: (0, spot[0] * steps + step))
    own = lambda count: pl.BlockSpec((count, FEED_BLOCK), lambda step, spot: (0, step))
    return pl.pallas_call(
        feed_kernel,
        grid_spec=pltpu.PrefetchScalarGridSpec(
            num_scalar_prefetch=1,
            grid=(steps,),
            in_specs=[
                fixed(2 * BLOCK, D),
                fixed(2 * BLOCK, D),
                fixed(2 * BLOCK, D),
                fixed(2 * BLOCK, D),
                fixed(D),
                fixed(D),
                columns(D),
                pl.BlockSpec((FEED_BLOCK,), lambda step, spot: (spot[0] * steps + step,)),
                pl.BlockSpec((FEED_BLOCK, D), lambda step, spot: (spot[0] * steps + step, 0)),
                fixed(D),
            ],
            out_specs=[
                fixed(2 * BLOCK, D),
                fixed(BLOCK, D),
                fixed(BLOCK, D),
                fixed(2 * BLOCK, D),
                fixed(2 * BLOCK, D),
                own(2 * BLOCK),
                own(2 * BLOCK),
                own(1),
            ],
            scratch_shapes=[
                pltpu.VMEM((2 * BLOCK, D), F32),
                pltpu.VMEM((2 * BLOCK, D), F32),
            ],
        ),
        out_shape=[
            struct((2 * BLOCK, D), F32),
            struct((BLOCK, D), F32),
            struct((BLOCK, D)),
            struct((2 * BLOCK, D)),
            struct((2 * BLOCK, D)),
            struct((2 * BLOCK, FF // 2)),
            struct((2 * BLOCK, FF // 2)),
            struct((1, FF // 2), F32),
        ],
        compiler_params=pltpu.CompilerParams(vmem_limit_bytes=VMEM_BYTES),
    )(spot, rows, part_mine, part_theirs, cot, gain, shift, up, up_bias, down, down_bias)


def place():
    dp = lax.axis_index("dp")
    sq = lax.axis_index("seq")
    return dict(x=dp // 8, z=(dp // 2) % 4, y=(sq // 2) * 2 + dp % 2, core=sq % 2)


def device_of(at):
    return (at["x"] * 8 + at["z"] * 2 + at["y"] % 2, (at["y"] // 2) * 2 + at["core"])


def moved(at, axis, steps):
    other = dict(at)
    other[axis] = (at[axis] + steps) % 4
    return device_of(other)


PLAIN = (("x", 4), ("z", 4), ("ylo", 2), ("yhi", 2))
SPLIT = (("xhi", 2), ("z", 4), ("ylo", 2), ("yhi", 2), ("xlo", 2))


def part_of(name, where):
    return {"hi": where // 2, "lo": where % 2}.get(name[1:], where)


def chunk_of(ref, dims, axis, where):
    return ref.at[tuple(part_of(name, where) if name[0] == axis else slice(None) for name, _ in dims)]


def without(dims, axes):
    return tuple(dim for dim in dims if dim[0][0] not in axes)


def lead_shape(dims):
    return tuple(size for _, size in dims)


def halves(width):
    one = (width // 2 + 127) // 128 * 128
    return (0, one), (one, width - one)


def each_block(lead, step):
    count = math.prod(lead)
    if not lead:
        step(Ellipsis)
        return

    def run(flat, carry):
        index = []
        for size in reversed(lead):
            index.insert(0, flat % size)
            flat = flat // size
        step(tuple(index))
        return carry

    lax.fori_loop(0, count, run, 0)


class Links:
    def __init__(self, send_sem, recv_sem):
        self.send_sem, self.recv_sem, self.made = send_sem, recv_sem, []

    def prepared(self, src, dst, device):
        slot = len(self.made)
        copy = pltpu.make_async_remote_copy(
            src_ref=src,
            dst_ref=dst,
            send_sem=self.send_sem.at[slot],
            recv_sem=self.recv_sem.at[slot],
            device_id=device,
            device_id_type=MESH,
        )
        self.made.append(copy)
        return copy

    def send(self, src, dst, device):
        copy = self.prepared(src, dst, device)
        copy.start()
        return copy


def added(target, *terms):
    def add(index):
        total = terms[0][index].astype(F32)
        for term in terms[1:]:
            total += term[index].astype(F32)
        target[index] = total.astype(target.dtype)

    return add


class Stage:
    def __init__(self, links, at, ref, dims, axis, width, bufs, after):
        self.links, self.at, self.axis, self.bufs, self.after = links, at, axis, bufs, after
        self.left = lead_shape(without(dims, axis))
        self.cols = [pl.ds(*half) for half in halves(width)]
        self.near = [chunk_of(ref, dims, axis, (at[axis] + steps) % 4) for steps in range(4)]
        self.made = []

    def launch_far(self):
        for side, steps in ((0, 1), (1, 3)):
            src = self.near[2].at[..., self.cols[side]]
            self.made.append(self.links.send(src, self.bufs[side], moved(self.at, self.axis, steps)))

    def launch_near(self):
        for side, steps in ((0, 1), (1, 3)):
            src = self.near[steps].at[..., self.cols[1 - side]]
            self.made.append(self.links.send(src, self.bufs[2 + side], moved(self.at, self.axis, steps)))

    def forward(self):
        for side, steps in ((0, 1), (1, 3)):
            self.made[side].wait_recv()
            held = self.bufs[side]
            each_block(self.left, added(held, held, self.near[steps].at[..., self.cols[side]]))
            self.made.append(self.links.send(held, self.bufs[4 + side], moved(self.at, self.axis, steps)))

    def collect(self):
        for copy in self.made[2:]:
            copy.wait_recv()
        for side in (0, 1):
            cols = self.cols[side]
            terms = self.near[0].at[..., cols], self.bufs[4 + side], self.bufs[3 - side]
            each_block(self.left, added(self.after.at[..., cols], *terms))


def stage_scratch(dims, axis, rows, width):
    left = lead_shape(without(dims, axis))
    (_, one), (_, two) = halves(width)
    return [pltpu.VMEM(left + (rows, size), BF16) for size in (one, two, two, one, one, two)]


def launch(stages):
    for stage in stages:
        stage.launch_far()
    for stage in stages:
        stage.launch_near()


def greet(devices):
    barrier = pltpu.get_barrier_semaphore()
    for device in devices:
        pl.semaphore_signal(barrier, inc=1, device_id=device, device_id_type=MESH)


UP, DOWN, OUT, WIDE_GRAD, REST = range(5)
LAYOUTS = (PLAIN, SPLIT, PLAIN, PLAIN, PLAIN)
SHAPES = ((16, FF // 2), (32, D), (16, EXPERTS), (16, WIDE), (16, 2 * SLOT))
FEED_PIECES = (
    (UP, 0, 1536, "xyz"),
    (DOWN, 0, 768, "zxy"),
    (UP, 1536, 512, "yzx"),
    (DOWN, 768, 256, "yzx"),
)
OUT_PIECES = (
    (OUT, 0, 512, "xyz"),
    (OUT, 512, 512, "zxy"),
    (OUT, 1024, 256, "yzx"),
)
EARLY = FEED_PIECES + OUT_PIECES
LATE = (
    (WIDE_GRAD, 0, 768, "xyz"),
    (WIDE_GRAD, 768, 768, "zxy"),
    (WIDE_GRAD, 1536, 384, "yzx"),
    (REST, 0, 256, "yzx"),
)


def dims_after(piece, phases):
    return without(LAYOUTS[piece[0]], piece[3][:phases])


def after_shape(piece, phases):
    return lead_shape(dims_after(piece, phases)) + (SHAPES[piece[0]][0], piece[2])


def phase_scratch(piece, phase):
    return stage_scratch(dims_after(piece, phase), piece[3][phase], SHAPES[piece[0]][0], piece[2])


def stage_for(links, at, piece, phase, ref, bufs, after):
    return Stage(links, at, ref, dims_after(piece, phase), piece[3][phase], piece[2], bufs, after)


def full_shape(array):
    return lead_shape(LAYOUTS[array]) + SHAPES[array]


def columns_of(ref, piece):
    return ref.at[..., pl.ds(piece[1], piece[2])]


class Fetches:
    def __init__(self, sems):
        self.sems, self.copies = sems, []

    def start(self, src, dst):
        copy = pltpu.make_async_copy(src, dst, self.sems.at[len(self.copies)])
        copy.start()
        self.copies.append(copy)
        return copy


def wait_for(*copies):
    for copy in copies:
        copy.wait()


KEY_BLOCKS = 2 * LEN // BLOCK


def rows_seeing(block):
    return pl.ds(max(0, block - 4) * BLOCK, LEN - max(0, block - 4) * BLOCK)


def back_kernel(*refs):
    refs = list(refs)
    take = lambda count: [refs.pop(0) for _ in range(count)]
    grad_part, final_theirs, gain = take(3)
    far_away = take(16)
    pay, pay_in, sums, grad_far, grad_resid, result, grad_logit, feed_sums = take(8)
    afters = take(len(EARLY))
    send_sem, recv_sem, fetch_sem = take(3)
    local = take(16)
    low, hidden, grad_before, cot, resid, out_wide, heads_own, heads_peer, gates, final_mine, mixed, values, probs, attended, keys, small_refs = local
    qu, qv, far_rel = (small_refs.at[pl.ds(start, size)] for start, size in ((0, LEN), (LEN, LEN), (2 * LEN, 2 * LEN)))
    part_in, final_in, given, given_in, grad_low, grad_mixed = take(6)
    grad_out, grad_u, grad_query, grad_keys, grad_values, far_sum = take(6)
    grads = take(3)
    links, fetches = Links(send_sem, recv_sem), Fetches(fetch_sem)
    loads = [fetches.start(src, dst) for src, dst in zip(far_away, local)]
    at = place()
    core, chip = at["core"], at["y"] // 2
    peer = moved(at, "y", 2)
    sibling = dict(at)
    sibling["core"] = 1 - core
    sibling = device_of(sibling)
    devices = [moved(at, axis, steps) for axis in "xyz" for steps in (1, 3)] + [peer, sibling]
    greet(devices)
    pl.semaphore_wait(pltpu.get_barrier_semaphore(), len(devices))
    parts = [
        links.send(grad_part.at[pl.ds((1 - side) * BLOCK, BLOCK)], part_in.at[pl.ds(side * BLOCK, BLOCK)], sibling)
        for side in range(2)
    ]
    final_copy = links.send(final_theirs, final_in, sibling)
    stages = []

    def go(pieces):
        new = []
        for piece in pieces:
            new.append(
                stage_for(links, at, piece, 0, columns_of(grads[piece[0]], piece), take(6), afters[len(stages)])
            )
            stages.append(new[-1])
        launch(new)

    def fill(array, left, right, start, width):
        cols = pl.ds(start, width)
        block = dot(left[...], right[:, start : start + width], 0, 0).astype(BF16)
        grads[array][..., cols] = block.reshape(lead_shape(LAYOUTS[array]) + (SHAPES[array][0], width))

    wait_for(*loads[:2 + 1])
    for start in range(0, 1536, 512):
        fill(UP, low, grad_before, start, 512)
    go(FEED_PIECES[:1])
    wait_for(loads[3])
    fill(DOWN, hidden, cot, 0, 512)
    fill(DOWN, hidden, cot, 512, 256)
    go(FEED_PIECES[1:2])
    wait_for(loads[4])
    for copy in parts:
        copy.wait_recv()
    for side in range(2):
        here = slice(side * BLOCK, (side + 1) * BLOCK)
        scaled, inverse = centered(resid[here, :])
        grad = grad_part[here, :].astype(F32) + part_in[here, :].astype(F32)
        above = cot[here, :].astype(F32)
        total = above + norm_back(grad, scaled, inverse, as_row(gain))
        grad_low[here, :] = total.astype(BF16)
        if side == 0:
            grad_resid[...] = total
            feed_sums[0:1, :] = jnp.sum(grad * scaled, axis=0, keepdims=True)
            feed_sums[1:2, :] = jnp.sum(grad, axis=0, keepdims=True)
            feed_sums[2:3, :] = jnp.sum(above, axis=0, keepdims=True)
    wait_for(*loads[5:9])
    grad_mixed[...] = dot(grad_low[...], out_wide[...], 1, 1)
    for side in range(2):
        here = slice(side * BLOCK, (side + 1) * BLOCK)
        gate = gates[(2 + side) * BLOCK : (3 + side) * BLOCK, :]
        totals = []
        for pair in range(2):
            total = jnp.zeros((BLOCK, SLOT), F32)
            for expert in range(E):
                slot = pair * E + expert
                weight = gate[:, 2 * E + slot : 2 * E + slot + 1]
                total += weight * grad_mixed[here, slot * SLOT : (slot + 1) * SLOT]
            totals.append(total)
        given[0, side] = jnp.where(chip == 0, totals[0], totals[1]).astype(BF16)
        given[1, side] = jnp.where(chip == 0, totals[1], totals[0]).astype(BF16)
    arrived = links.send(given.at[1], given_in, peer)
    wait_for(loads[10])
    fill(OUT, grad_low, mixed, 0, 512)
    fill(OUT, grad_low, mixed, 512, 512)
    fill(OUT, grad_low, mixed, 1024, 256)
    fill(UP, low, grad_before, 1536, 512)
    fill(DOWN, hidden, cot, 768, 256)
    go(FEED_PIECES[2:] + OUT_PIECES)
    lane = lax.broadcasted_iota(jnp.int32, (BLOCK, SLOT), 1)
    for side in range(2):
        here = slice(side * BLOCK, (side + 1) * BLOCK)
        gate = gates[(2 + side) * BLOCK : (3 + side) * BLOCK, :]
        heads = two_heads(chip, heads_own[side], heads_peer[side])
        total = jnp.zeros((BLOCK, SLOT), F32)
        for slot in range(2 * E):
            part = grad_mixed[here, slot * SLOT : (slot + 1) * SLOT] * heads[slot // E]
            total += jnp.where(lane == 2 * E + slot, jnp.sum(part, axis=1, keepdims=True), 0.0)
        grad_logit[here, :] = (total * gate * (1.0 - gate)).astype(BF16)
    places = spots_of(core, chip)
    for side in range(2):
        grad_out[rows_at(places[side]), :] = given[0, side]
    wait_for(*loads[11:])
    arrived.wait_recv()
    for side in range(2):
        grad_out[rows_at(places[2 + side]), :] = given_in[side]
    moving = []

    def give(first, held, base):
        for side in range(2):
            pay[first + side] = held[rows_at(places[side] + base), :]
            src = held.at[rows_at(places[2 + side] + base)]
            moving.append(links.send(src, pay_in.at[first + side], peer))

    for block in range(KEY_BLOCKS):
        cols, rows = pl.ds(block * BLOCK, BLOCK), rows_seeing(block)
        grad_values[cols, :] = dot(probs[rows, cols], grad_out[rows, :], 0, 0).astype(BF16)
    give(4, grad_values, 0)
    give(6, grad_values, LEN)
    stages[0].forward()
    stages[1].forward()
    blocks = LEN // BLOCK
    sum_u = jnp.zeros((1, SLOT), F32)
    for block in range(blocks):
        rows = pl.ds(block * BLOCK, BLOCK)
        width = LEN + (block + 1) * BLOCK
        above = grad_out[rows, :]
        grad_probs = dot(above, values[:width, :], 1, 1)
        inner = jnp.sum(above.astype(F32) * attended[rows, :], axis=1, keepdims=True)
        scores = (probs[rows, :width].astype(F32) * ((grad_probs - inner) * SCALE)).astype(BF16)
        probs[rows, :width] = scores
        part = dot(scores, keys[:width, :])
        grad_u[rows, :] = part
        sum_u += jnp.sum(part, axis=0, keepdims=True)
    for block in range(KEY_BLOCKS):
        cols, rows = pl.ds(block * BLOCK, BLOCK), rows_seeing(block)
        grad_keys[cols, :] = dot(probs[rows, cols], qu[rows, :], 0, 0).astype(BF16)
    give(0, grad_keys, 0)
    give(2, grad_keys, LEN)
    for stage in stages[2:]:
        stage.forward()
    far_sum[...] = jnp.zeros_like(far_sum)
    down = lax.broadcasted_iota(jnp.int32, (BLOCK, BLOCK), 0)
    across = lax.broadcasted_iota(jnp.int32, (BLOCK, BLOCK), 1)
    flip = (down + across == BLOCK - 1).astype(F32).astype(BF16)
    sum_v = jnp.zeros((1, SLOT), F32)
    for block in range(blocks):
        rows = pl.ds(block * BLOCK, BLOCK)
        width = LEN + (block + 1) * BLOCK
        first_far = 2 * LEN - width
        far = pltpu.roll(dot(flip, probs[rows, :width]), 0, 1, stride=1, stride_axis=0).astype(BF16)
        turned = dot(flip, far).astype(BF16)
        part = dot(turned, far_rel[first_far:, :])
        far_sum[first_far:, :] += dot(turned, qv[rows, :], 0, 0)
        grad_query[rows, :] = (grad_u[rows, :] + part).astype(BF16)
        sum_v += jnp.sum(part, axis=0, keepdims=True)
    give(8, grad_query, 0)
    sums[0:1, :] = sum_u
    sums[1:2, :] = sum_v
    grad_far[...] = far_sum[...].astype(BF16)
    wait_for(loads[9])
    final_copy.wait_recv()
    result[...] = (final_mine[...] + final_in[...].astype(F32)).astype(BF16)
    for stage in stages:
        stage.collect()
    for copy in moving:
        copy.wait_recv()
    for copy in links.made:
        copy.wait_send()


def back(grad_part, final_theirs, gain, later):
    scratch = []
    for piece in EARLY:
        scratch += phase_scratch(piece, 0)
    copies = 2 + 1 + 1 + 10 + 6 * len(EARLY)
    seq = (2 * LEN, SLOT)
    rows = (2 * BLOCK, D)
    outs = [struct((10, BLOCK, SLOT)), struct((10, BLOCK, SLOT)), struct((2, SLOT), F32), struct(seq)]
    outs += [struct((BLOCK, D), F32), struct((BLOCK, D)), struct((2 * BLOCK, SLOT)), struct((8, D), F32)]
    outs += [struct(after_shape(piece, 1)) for piece in EARLY]
    return pl.pallas_call(
        back_kernel,
        out_shape=outs,
        in_specs=[IN_VMEM] * 3 + [ANYWHERE] * len(later),
        out_specs=[IN_VMEM] * len(outs),
        scratch_shapes=[
            pltpu.SemaphoreType.DMA((copies,)),
            pltpu.SemaphoreType.DMA((copies,)),
            pltpu.SemaphoreType.DMA((len(later),)),
        ]
        + [pltpu.VMEM(operand.shape, operand.dtype) for operand in later]
        + [
            pltpu.VMEM(rows, BF16),
            pltpu.VMEM((BLOCK, D), BF16),
            pltpu.VMEM((2, 2, BLOCK, SLOT), BF16),
            pltpu.VMEM((2, BLOCK, SLOT), BF16),
            pltpu.VMEM(rows, BF16),
            pltpu.VMEM((2 * BLOCK, EXPERTS), F32),
            pltpu.VMEM((LEN, SLOT), BF16),
            pltpu.VMEM((LEN, SLOT), F32),
            pltpu.VMEM((LEN, SLOT), BF16),
            pltpu.VMEM(seq, BF16),
            pltpu.VMEM(seq, BF16),
            pltpu.VMEM(seq, F32),
        ]
        + [pltpu.VMEM(full_shape(array), BF16) for array in (UP, DOWN, OUT)]
        + scratch,
        compiler_params=pltpu.CompilerParams(
            collective_id=1, has_side_effects=True, vmem_limit_bytes=VMEM_BYTES
        ),
    )(grad_part, final_theirs, gain, *later)


COUNT_ROW = 2 * H
VECTOR_ROW = 16
UP_BIAS_ROW = VECTOR_ROW + 5 * 8
SMALL_ROWS = UP_BIAS_ROW + FF // SLOT


def lay(target, first, vector):
    for row in range(vector.shape[1] // SLOT):
        target[first + row : first + row + 1, :] = vector[:, row * SLOT : (row + 1) * SLOT]


def close_kernel(*refs):
    refs = list(refs)
    take = lambda count: [refs.pop(0) for _ in range(count)]
    gain, feed_sums, grad_up_bias, bias_sums, counts, pay, pay_in, grad_logit, grad_far = take(9)
    early = take(len(EARLY))
    far_away = take(8)
    grad_tokens, small_out, down_out = take(3)
    both = dict(zip((UP, OUT, WIDE_GRAD, REST), take(4)))
    send_sem, recv_sem, own_sem, fetch_sem = take(4)
    local = take(8)
    experts, gates, wide, normed, sinus, memory, tokens, grad_resid = local
    part, part_in, half_bias, grad_all = take(4)
    late = dict(zip((WIDE_GRAD, REST), take(2)))
    totals = take(5)
    slots = take(4)
    links, fetches = Links(send_sem, recv_sem), Fetches(fetch_sem)
    loads = [fetches.start(src, dst) for src, dst in zip(far_away, local)]
    at = place()
    core, chip = at["core"], at["y"] // 2
    sibling = dict(at)
    sibling["core"] = 1 - core
    sibling = device_of(sibling)
    high, low = at["x"] // 2, at["x"] % 2
    stays = (high == low) & (low == core)
    ahead, behind = dict(at), dict(at)
    ahead["x"], ahead["core"] = 2 * core + high, low
    behind["x"], behind["core"] = 2 * low + core, high
    ahead, behind = device_of(ahead), device_of(behind)
    devices = [moved(at, axis, steps) for axis in "xyz" for steps in (1, 2, 3)] + [sibling]
    greet(devices)

    def greet_more():
        greet([ahead, behind])
        pl.semaphore_wait(pltpu.get_barrier_semaphore(), len(devices) + 2)

    pl.when(jnp.logical_not(stays))(greet_more)
    pl.when(stays)(lambda: pl.semaphore_wait(pltpu.get_barrier_semaphore(), len(devices)))

    def begin(jobs):
        stages, later = [], []
        for piece, phase, ref in jobs:
            bufs = take(6)
            after = take(1)[0] if phase < 2 else totals[piece[0]].at[:, pl.ds(piece[1], piece[2])]
            stages.append(stage_for(links, at, piece, phase, ref, bufs, after))
            if phase < 2:
                later.append((piece, phase + 1, after))
        launch(stages)
        return stages, later

    def forward(stages):
        for stage in stages:
            stage.forward()

    def collect(stages):
        for stage in stages:
            stage.collect()

    def spread(number, value):
        axis = "xyz"[number]
        here = slots[number].at[at[axis]]
        here[...] = value
        return [links.send(here, here, moved(at, axis, steps)) for steps in (1, 2, 3)]

    def gathered(number, copies):
        for copy in copies:
            copy.wait_recv()
        one = slots[number]
        return (one[0] + one[1]) + (one[2] + one[3])

    early_stages, early_jobs = begin([(piece, 1, ref) for piece, ref in zip(EARLY, early)])
    lane = lax.broadcasted_iota(jnp.int32, (BLOCK, SLOT), 1)

    def shape_rows(block):
        rows = slice(block * BLOCK, (block + 1) * BLOCK)
        gate = gates[rows, :]
        key_heads = two_heads(chip, pay[block], pay_in[block])
        value_heads = two_heads(chip, pay[4 + block], pay_in[4 + block])
        total = jnp.zeros((BLOCK, SLOT), F32)
        for slot in range(2 * E):
            cols = slice(slot * SLOT, (slot + 1) * SLOT)
            grad = value_heads[slot // E]
            grad_all[rows, cols] = (gate[:, slot : slot + 1] * grad).astype(BF16)
            inner = jnp.sum(grad * experts[rows, cols].astype(F32), axis=1, keepdims=True)
            total += jnp.where(lane == slot, inner, 0.0)
        total = total * gate * (1.0 - gate)
        if block >= 2:
            total += grad_logit[(block - 2) * BLOCK : (block - 1) * BLOCK, :].astype(F32)
            queries = two_heads(chip, pay[6 + block], pay_in[6 + block])
        for pair in range(2):
            grad_all[rows, KEY_AT + pair * SLOT : KEY_AT + (pair + 1) * SLOT] = key_heads[pair].astype(BF16)
            query = queries[pair].astype(BF16) if block >= 2 else jnp.zeros((BLOCK, SLOT), BF16)
            grad_all[rows, QUERY_AT + pair * SLOT : QUERY_AT + (pair + 1) * SLOT] = query
        grad_all[rows, ROUTER_AT:WIDE] = total.astype(BF16)

    halves_in = []
    wait_for(*loads[:3])
    for block in (1, 3, 0, 2):
        shape_rows(block)
        rows = slice(block * BLOCK, (block + 1) * BLOCK)
        part[block] = dot(grad_all[rows, :], wide[...]).astype(BF16)
        if block % 2 == 1:
            halves_in.append(links.send(part.at[block], part_in.at[block // 2], sibling))
    forward(early_stages)

    def fill(start, width):
        cols = pl.ds(start, width)
        block = dot(normed[...], grad_all[:, start : start + width], 0, 0).astype(BF16)
        late[WIDE_GRAD][..., cols] = block.reshape(lead_shape(PLAIN) + (16, width))

    late_stages, late_jobs = [], []

    def go(pieces):
        stages, jobs = begin([(piece, 0, columns_of(late[piece[0]], piece)) for piece in pieces])
        late_stages.extend(stages)
        late_jobs.extend(jobs)

    wait_for(loads[3])
    fill(0, 768)
    go(LATE[:1])
    fill(768, 768)
    go(LATE[1:2])
    fill(1536, 384)
    wait_for(loads[4])
    rel = dot(sinus[...], grad_far[...], 0, 0).astype(BF16).reshape(lead_shape(PLAIN) + (16, SLOT))
    blank = jnp.zeros((), BF16)
    late[REST][..., :SLOT] = jnp.where(chip == 0, rel, blank)
    late[REST][..., SLOT:] = jnp.where(chip == 1, rel, blank)
    go(LATE[2:])
    collect(early_stages)
    early_stages, early_jobs = begin(early_jobs)
    wait_for(*loads[5:])
    for copy in halves_in:
        copy.wait_recv()
    gain_sum = jnp.zeros((1, D), F32)
    bias_sum = jnp.zeros((1, D), F32)
    for side, rows in enumerate((memory, tokens)):
        scaled, inverse = centered(rows[...].astype(F32))
        grad = part[2 * side].astype(F32) + part_in[side].astype(F32)
        gain_sum += jnp.sum(grad * scaled, axis=0, keepdims=True)
        bias_sum += jnp.sum(grad, axis=0, keepdims=True)
        if side == 1:
            grad_tokens[...] = grad_resid[...] + norm_back(grad, scaled, inverse, as_row(gain))
    small = small_out
    small[:COUNT_ROW, :] = jnp.zeros((COUNT_ROW, SLOT), F32)
    small[COUNT_ROW:VECTOR_ROW, :] = counts[...]
    for number in range(2):
        small[pl.ds(H * number + 2 * chip + core, 1), :] = bias_sums[number : number + 1, :]
    lay(small, VECTOR_ROW, gain_sum)
    lay(small, VECTOR_ROW + 8, bias_sum)
    for number in range(3):
        lay(small, VECTOR_ROW + 16 + 8 * number, feed_sums[number : number + 1, :])
    small[UP_BIAS_ROW:, :] = jnp.zeros((FF // SLOT, SLOT), F32)
    lay(half_bias, 0, grad_up_bias[...])
    half = FF // 2 // SLOT
    small[pl.ds(pl.multiple_of(UP_BIAS_ROW + core * half, 8), half), :] = half_bias[...]
    copies = spread(0, small[...])
    forward(late_stages)
    forward(early_stages)
    collect(early_stages)
    collect(late_stages)
    late_stages, late_jobs = begin(late_jobs)
    copies = spread(1, gathered(0, copies))
    forward(late_stages)
    collect(late_stages)
    late_stages, late_jobs = begin(late_jobs)
    copies = spread(2, gathered(1, copies))
    last = []
    away = links.prepared(totals[DOWN], down_out, ahead)
    here = pltpu.make_async_copy(totals[DOWN], down_out, own_sem)
    pl.when(jnp.logical_not(stays))(away.start)
    pl.when(stays)(here.start)

    def exchange(arrays):
        for array in arrays:
            other = pl.ds(pl.multiple_of((1 - core) * 8, 8), 8)
            last.append(links.send(totals[array].at[other], both[array].at[core], sibling))
            both[array][core] = totals[array][pl.ds(pl.multiple_of(core * 8, 8), 8), :]

    exchange((UP, OUT))
    forward(late_stages)
    collect(late_stages)
    exchange((WIDE_GRAD, REST))
    pair = slots[3]
    pair[core] = gathered(2, copies)
    last.append(links.send(pair.at[core], pair.at[core], sibling))
    for copy in last:
        copy.wait_recv()
    small_out[...] = pair[0] + pair[1]
    pl.when(jnp.logical_not(stays))(away.wait)
    pl.when(stays)(here.wait)
    for copy in links.made:
        if copy is not away:
            copy.wait_send()


def close(gain, feed_sums, grad_up_bias, bias_sums, counts, pay, pay_in, grad_logit, grad_far, early, later):
    scratch = []
    copies = 2 + 9 + 1 + 1 + 4

    def round_of(jobs):
        nonlocal copies
        for piece, phase in jobs:
            scratch.extend(phase_scratch(piece, phase))
            copies += 6
            if phase < 2:
                scratch.append(pltpu.VMEM(after_shape(piece, phase + 1), BF16))

    round_of([(piece, 1) for piece in EARLY])
    round_of([(piece, 0) for piece in LATE])
    round_of([(piece, 2) for piece in EARLY])
    round_of([(piece, 1) for piece in LATE])
    round_of([(piece, 2) for piece in LATE])
    outs = [struct((BLOCK, D), F32), struct((SMALL_ROWS, SLOT), F32), struct(SHAPES[DOWN], F32)]
    outs += [struct((2, 8, SHAPES[array][1]), F32) for array in (UP, OUT, WIDE_GRAD, REST)]
    return pl.pallas_call(
        close_kernel,
        out_shape=outs,
        in_specs=[IN_VMEM] * (9 + len(EARLY)) + [ANYWHERE] * len(later),
        out_specs=[IN_VMEM] * len(outs),
        scratch_shapes=[
            pltpu.SemaphoreType.DMA((copies,)),
            pltpu.SemaphoreType.DMA((copies,)),
            pltpu.SemaphoreType.DMA,
            pltpu.SemaphoreType.DMA((len(later),)),
        ]
        + [pltpu.VMEM(operand.shape, operand.dtype) for operand in later]
        + [
            pltpu.VMEM((4, BLOCK, D), BF16),
            pltpu.VMEM((2, BLOCK, D), BF16),
            pltpu.VMEM((FF // 2 // SLOT, SLOT), F32),
            pltpu.VMEM((4 * BLOCK, WIDE), BF16),
            pltpu.VMEM(full_shape(WIDE_GRAD), BF16),
            pltpu.VMEM(full_shape(REST), BF16),
        ]
        + [pltpu.VMEM(shape, F32) for shape in SHAPES]
        + [pltpu.VMEM((4, SMALL_ROWS, SLOT), F32)] * 3
        + [pltpu.VMEM((2, SMALL_ROWS, SLOT), F32)]
        + scratch,
        compiler_params=pltpu.CompilerParams(
            collective_id=2, has_side_effects=True, vmem_limit_bytes=VMEM_BYTES
        ),
    )(gain, feed_sums, grad_up_bias, bias_sums, counts, pay, pay_in, grad_logit, grad_far, *early, *later)


FRONT_OUTS = (
    ((2 * BLOCK, D), BF16),
    ((2 * BLOCK, D), BF16),
    ((WIDE, D), BF16),
    ((EXPERTS, D), BF16),
    ((4 * BLOCK, D), BF16),
    ((4 * BLOCK, EXPERTS), BF16),
    ((4 * BLOCK, SLOT), F32),
    ((2 * LEN, SLOT), BF16),
    ((2 * LEN, SLOT), BF16),
    ((4 * LEN, SLOT), BF16),
    ((LEN, SLOT), F32),
    ((LEN, 2 * LEN), BF16),
    ((2, BLOCK, SLOT), BF16),
    ((2, BLOCK, SLOT), BF16),
    ((2 * BLOCK, EXPERTS), BF16),
    ((2 * BLOCK, D), BF16),
    ((2 * BLOCK, D), BF16),
    ((2 * LEN, D), BF16),
    ((8, SLOT), F32),
)
FRONT_FETCHES = 3 + 2 * E * 2 + 2 * 2 + 1


def front_kernel(*refs):
    refs = list(refs)
    take = lambda count: [refs.pop(0) for _ in range(count)]
    (mem_len,) = take(1)
    gain, shift, value_route, out_route, bias_u, bias_v, value_router, out_router, coarse, fine = take(10)
    memory, tokens, cotangent, value_weight, key_weight, query_weight, rel_weight, out_weight = take(8)
    outs = take(len(FRONT_OUTS))
    kept = take(len(FRONT_OUTS))
    tok, cot, wide, out_wide, normed, experts, gates, keys, values, queries, attended, probs, heads_own, heads_peer, mixed, part, part_in, sinus, counts = kept
    send_sem, recv_sem, fetch_sem, out_sem = take(4)
    mem, routes, routes_in, turned, rel, full, pay, pay_in, back = take(9)
    links, fetches, writes = Links(send_sem, recv_sem), Fetches(fetch_sem), Fetches(out_sem)
    at = place()
    core, chip = at["core"], at["y"] // 2
    peer = moved(at, "y", 2)
    sibling = dict(at)
    sibling["core"] = 1 - core
    sibling = device_of(sibling)
    mine, theirs = pl.ds(0, BLOCK), pl.ds(BLOCK, BLOCK)
    row_loads = [
        fetches.start(memory, mem.at[mine]),
        fetches.start(tokens, tok.at[mine]),
        fetches.start(cotangent, cot.at[mine]),
    ]

    def slots_from(target, slot, source, start):
        src = source.at[pl.ds(pl.multiple_of(start, 16), DH)]
        return fetches.start(src, target.at[pl.ds(slot, DH)])

    wide_loads, out_loads = [], []
    for pair in range(2):
        head = 2 * pair + core
        for expert in range(E):
            slot = (pair * E + expert) * SLOT
            wide_loads.append(slots_from(wide, slot, value_weight, (head * E + expert) * DH))
        wide_loads.append(slots_from(wide, KEY_AT + pair * SLOT, key_weight, head * DH))
        wide_loads.append(slots_from(wide, QUERY_AT + pair * SLOT, query_weight, head * DH))
    rel_load = slots_from(rel, 0, rel_weight, (2 * chip + core) * DH)
    for pair in range(2):
        head = 2 * pair + core
        for expert in range(E):
            slot = (pair * E + expert) * SLOT
            out_loads.append(slots_from(out_wide, slot, out_weight, (head * E + expert) * DH))
    routes[:8, :] = value_route[:, 0, :]
    routes[8:16, :] = value_route[:, 1, :]
    for number in range(H):
        routes[16 + 2 * number : 18 + 2 * number, :] = out_route[number]
    greet([sibling, peer])
    pl.semaphore_wait(pltpu.get_barrier_semaphore(), 2)
    mem_copy = links.send(memory, mem.at[theirs], sibling)
    tok_copy = links.send(tokens, tok.at[theirs], sibling)
    route_copy = links.send(routes, routes_in, sibling)
    cot_copy = links.send(cotangent, cot.at[theirs], sibling)
    blank = jnp.zeros((SLOT - DH, D), BF16)
    for slot in range(DH, EXPERTS, SLOT):
        out_wide[slot : slot + SLOT - DH, :] = blank
    for slot in range(DH, ROUTER_AT, SLOT):
        wide[slot : slot + SLOT - DH, :] = blank
    rel[DH:, :] = blank
    routers = []
    for router in (value_router, out_router):
        for pair in range(2):
            one = router[2 * pair * E : (2 * pair + 1) * E, :].astype(F32)
            two = router[(2 * pair + 1) * E : (2 * pair + 2) * E, :].astype(F32)
            routers.append(jnp.where(core == 0, one, two))
    routers.append(jnp.zeros((SLOT - 4 * E, D), F32))
    wide[ROUTER_AT:, :] = jnp.concatenate(routers, axis=0).astype(BF16)
    lane = lax.broadcasted_iota(jnp.int32, (BLOCK, SLOT), 1)
    turned[0] = routes[...].astype(F32).T.astype(jnp.int32)
    slot_of = lax.broadcasted_iota(jnp.int32, (2 * H, SLOT), 1) - lax.broadcasted_iota(jnp.int32, (2 * H, SLOT), 0) // 2 * E
    counted = jnp.zeros((1, SLOT), F32)
    for first in (0, 8, 16):
        for expert in range(E):
            named = (routes[first : first + 2 * H, :] == expert).astype(F32)
            number = jnp.sum(named, axis=1, keepdims=True)
            at_slot = slot_of == expert + (H * E if first == 16 else 0)
            counted += jnp.sum(jnp.where(at_slot, number, 0.0), axis=0, keepdims=True)
    counts[...] = jnp.zeros_like(counts)
    counts[0:1, :] = counted
    wait_for(*row_loads[:2])

    def normalize(block):
        rows = slice(block * BLOCK, (block + 1) * BLOCK)
        given = (mem, tok)[block // 2][(block % 2) * BLOCK : (block % 2 + 1) * BLOCK, :]
        scaled, _ = centered(given.astype(F32))
        normed[rows, :] = (scaled * as_row(gain) + as_row(shift)).astype(BF16)

    moving = []

    def project(block, buffer):
        rows = slice(block * BLOCK, (block + 1) * BLOCK)
        space = full.at[buffer]
        space[...] = dot(normed[rows, :], wide[...], 1, 1)
        experts[rows, :] = space[:, :EXPERTS].astype(BF16)
        named = turned[block % 2]
        token = block // 2
        chosen = chosen_lanes(named, 2 * H * token, core, lane, 0) & (lane < 2 * E)
        if token:
            chosen = chosen | chosen_lanes(named, 4 * H, core, lane, 2 * E)
        gate = jnp.where(chosen, jax.nn.sigmoid(space[:, ROUTER_AT:WIDE]), 0.0)
        gates[rows, :] = gate
        for pair in range(2):
            total = jnp.zeros((BLOCK, SLOT), F32)
            for expert in range(E):
                slot = pair * E + expert
                total += gate[:, slot : slot + 1] * space[:, slot * SLOT : (slot + 1) * SLOT]
            pay[pair, block] = space[:, KEY_AT + pair * SLOT : KEY_AT + (pair + 1) * SLOT].astype(BF16)
            pay[pair, 4 + block] = total.astype(BF16)
            if token:
                pay[pair, 6 + block] = space[:, QUERY_AT + pair * SLOT : QUERY_AT + (pair + 1) * SLOT].astype(BF16)
        for segment in (block, 4 + block) + ((6 + block,) if token else ()):
            moving.append(links.send(pay.at[1 - chip, segment], pay_in.at[segment], peer))

    normalize(0)
    normalize(2)
    wait_for(*wide_loads)
    project(0, 0)
    project(2, 1)
    mem_copy.wait_recv()
    normalize(1)
    tok_copy.wait_recv()
    normalize(3)
    route_copy.wait_recv()
    turned[1] = routes_in[...].astype(F32).T.astype(jnp.int32)
    project(1, 0)
    project(3, 1)
    for number in (0, 2, 4, 5, 6):
        writes.start(kept[number], outs[number])
    sin_b, cos_b = fine[0], fine[1]
    for number in range(32):
        sin_a, cos_a = coarse[0, number : number + 1, :], coarse[1, number : number + 1, :]
        rows = slice(64 * number, 64 * (number + 1))
        sinus[rows, : D // 2] = (sin_a * cos_b + cos_a * sin_b).astype(BF16)
        sinus[rows, D // 2 :] = (cos_a * cos_b - sin_a * sin_b).astype(BF16)
    writes.start(kept[17], outs[17])
    writes.start(kept[18], outs[18])
    rel_load.wait()
    far_rel = queries.at[pl.ds(2 * LEN, 2 * LEN)]
    far_rel[...] = dot(sinus[...], rel[...], 1, 1).astype(BF16)
    places = spots_of(core, chip)
    head = 2 * chip + core

    def own_head(bias):
        row = bias[...].astype(F32).reshape(1, H * DH)
        total = jnp.zeros((1, DH), F32)
        for number in range(H):
            total += jnp.where(head == number, row[:, number * DH : (number + 1) * DH], 0.0)
        return jnp.concatenate([total, jnp.zeros((1, SLOT - DH), F32)], axis=1)

    head_u, head_v = own_head(bias_u), own_head(bias_v)
    qu, qv = queries.at[pl.ds(0, LEN)], queries.at[pl.ds(LEN, LEN)]

    def assemble(number, segment_of):
        side = number % 2
        start = places[number]
        keys[rows_at(start), :] = segment_of(side)
        keys[rows_at(start + LEN), :] = segment_of(2 + side)
        values[rows_at(start), :] = segment_of(4 + side)
        values[rows_at(start + LEN), :] = segment_of(6 + side)
        query = segment_of(8 + side).astype(F32)
        qu[rows_at(start), :] = (query + head_u).astype(BF16)
        qv[rows_at(start), :] = (query + head_v).astype(BF16)

    for number in range(2):
        assemble(number, lambda segment: pay[chip, segment])
    for copy in moving:
        copy.wait_recv()
    for number in range(2, 4):
        assemble(number, lambda segment: pay_in[segment])
    for number in (7, 8, 9):
        writes.start(kept[number], outs[number])
    shown = mem_len[0]
    for block in range(LEN // BLOCK):
        attend(block, shown, qu, qv, keys, values, far_rel, attended, probs)
    for side in range(2):
        heads_own[side] = attended[rows_at(places[side]), :].astype(BF16)
        back[side] = attended[rows_at(places[2 + side]), :].astype(BF16)
    returned = links.send(back, heads_peer, peer)
    for number in (10, 11, 12):
        writes.start(kept[number], outs[number])
    wait_for(*out_loads)
    writes.start(kept[3], outs[3])
    returned.wait_recv()
    writes.start(kept[13], outs[13])
    sent = []
    for side in range(2):
        heads = two_heads(chip, heads_own[side], heads_peer[side])
        rows = slice(side * BLOCK, (side + 1) * BLOCK)
        gate = gates[(2 + side) * BLOCK : (3 + side) * BLOCK, :]
        for slot in range(2 * E):
            weight = gate[:, 2 * E + slot : 2 * E + slot + 1]
            mixed[rows, slot * SLOT : (slot + 1) * SLOT] = (weight * heads[slot // E]).astype(BF16)
        part[rows, :] = dot(mixed[rows, :], out_wide[...]).astype(BF16)
        other = pl.ds((1 - side) * BLOCK, BLOCK)
        sent.append(links.send(part.at[pl.ds(side * BLOCK, BLOCK)], part_in.at[other], sibling))
    writes.start(kept[14], outs[14])
    writes.start(kept[15], outs[15])
    row_loads[2].wait()
    cot_copy.wait_recv()
    writes.start(kept[1], outs[1])
    for copy in sent:
        copy.wait_recv()
    writes.start(kept[16], outs[16])
    wait_for(*writes.copies)
    for copy in links.made:
        copy.wait_send()


def front(mem_len, small, large):
    copies = 4 + 10 + 1 + 2
    return pl.pallas_call(
        front_kernel,
        out_shape=[struct(*out) for out in FRONT_OUTS],
        in_specs=[IN_SMEM] + [IN_VMEM] * len(small) + [ANYWHERE] * len(large),
        out_specs=[ANYWHERE] * len(FRONT_OUTS),
        scratch_shapes=[pltpu.VMEM(*out) for out in FRONT_OUTS]
        + [
            pltpu.SemaphoreType.DMA((copies,)),
            pltpu.SemaphoreType.DMA((copies,)),
            pltpu.SemaphoreType.DMA((FRONT_FETCHES,)),
            pltpu.SemaphoreType.DMA((len(FRONT_OUTS),)),
            pltpu.VMEM((2 * BLOCK, D), BF16),
            pltpu.VMEM((6 * H, BLOCK), jnp.int32),
            pltpu.VMEM((6 * H, BLOCK), jnp.int32),
            pltpu.VMEM((2, BLOCK, 6 * H), jnp.int32),
            pltpu.VMEM((SLOT, D), BF16),
            pltpu.VMEM((2, BLOCK, WIDE), F32),
            pltpu.VMEM((2, 10, BLOCK, SLOT), BF16),
            pltpu.VMEM((10, BLOCK, SLOT), BF16),
            pltpu.VMEM((2, BLOCK, SLOT), BF16),
        ],
        compiler_params=pltpu.CompilerParams(
            collective_id=0, has_side_effects=True, vmem_limit_bytes=VMEM_BYTES
        ),
    )(mem_len, *small, *large)


ARRANGED = (
    ((BLOCK, D), BF16),
    ((BLOCK, D), F32),
    ((8,), F32),
    ((8,), F32),
    ((8, H * DH), F32),
    ((8, H * DH), F32),
    ((8, H * DH), F32),
    ((H * DH,), F32),
    ((H * DH,), F32),
    ((8, H * E), F32),
    ((8, H * E * DH), F32),
    ((8, H * E), F32),
    ((8, H * E * DH), F32),
    ((8,), F32),
    ((8,), F32),
    ((8, FF), F32),
    ((32,), F32),
    ((32, D), F32),
    ((8,), F32),
    ((2, H, E), jnp.int32),
)


def arrange_kernel(result_in, tokens_in, small, down_in, up, out, wide, rest, *outs):
    (
        result,
        grad_tokens,
        attn_gain,
        attn_bias,
        grad_query,
        grad_key,
        grad_rel,
        grad_bias_u,
        grad_bias_v,
        value_router,
        grad_value,
        out_router,
        grad_out,
        ffn_gain,
        ffn_bias,
        grad_up,
        up_bias,
        grad_down,
        down_bias,
        counts,
    ) = outs
    result[...] = result_in[...]
    grad_tokens[...] = tokens_in[...]
    grad_down[...] = down_in[...]
    grad_up[:, : FF // 2] = up[0]
    grad_up[:, FF // 2 :] = up[1]
    for head in range(H):
        core, pair = head % 2, head // 2
        for expert in range(E):
            slot = (pair * E + expert) * SLOT
            start = (head * E + expert) * DH
            grad_out[:, start : start + DH] = out[core, :, slot : slot + DH]
            grad_value[:, start : start + DH] = wide[core, :, slot : slot + DH]
        start = head * DH
        for target, source, slot in ((grad_key, wide, KEY_AT), (grad_query, wide, QUERY_AT), (grad_rel, rest, 0)):
            slot += pair * SLOT
            target[:, start : start + DH] = source[core, :, slot : slot + DH]
        for kind, target in enumerate((value_router, out_router)):
            at = ROUTER_AT + (2 * kind + pair) * E
            target[:, head * E : (head + 1) * E] = wide[core, :, at : at + E]
    device = lax.axis_index("dp") * 4 + lax.axis_index("seq")

    def share(target, first, size):
        per_row = SLOT // size
        row = small[pl.ds(first + device // per_row, 1), :]
        row = pltpu.roll(row, SLOT - device % per_row * size, 1)
        target[...] = row[:, :size].reshape(size)

    for number, target in enumerate((attn_gain, attn_bias, ffn_gain, ffn_bias, down_bias)):
        share(target, VECTOR_ROW + 8 * number, 8)
    share(up_bias, UP_BIAS_ROW, 32)
    for first, target in ((0, grad_bias_u), (H, grad_bias_v)):
        heads = [small[first + head : first + head + 1, :DH] for head in range(H)]
        target[...] = jnp.concatenate(heads, axis=1).reshape(H * DH)
    row = (small[COUNT_ROW : COUNT_ROW + 1, :] + 0.5).astype(jnp.int32)
    for kind in range(2):
        for head in range(H):
            at = (kind * H + head) * E
            counts[kind, head : head + 1, :] = row[:, at : at + E]


def arrange(*operands):
    return local_call(arrange_kernel, [struct(*out) for out in ARRANGED], vmem=len(operands))(*operands)


def angle_tables():
    frequency = jnp.exp(jnp.arange(D // 2, dtype=jnp.int32).astype(F32) * (-2.0 * math.log(10000.0) / D))
    coarse = (64 * (31 - jnp.arange(32, dtype=jnp.int32))).astype(F32)[:, None] * frequency
    fine = (63 - jnp.arange(64, dtype=jnp.int32)).astype(F32)[:, None] * frequency
    return jnp.stack([jnp.sin(coarse), jnp.cos(coarse)]), jnp.stack([jnp.sin(fine), jnp.cos(fine)])


def body(
    tokens,
    memory,
    cotangent,
    mem_len,
    value_route,
    output_route,
    attn_norm_gain,
    attn_norm_bias,
    query_weight,
    key_weight,
    rel_weight,
    bias_u,
    bias_v,
    value_router,
    value_weight,
    out_router,
    out_weight,
    ffn_norm_gain,
    ffn_norm_bias,
    up_weight,
    up_bias,
    down_weight,
    down_bias,
):
    spot = (lax.axis_index("seq") % 2).reshape(1).astype(jnp.int32)
    tokens, memory, cotangent = tokens[0], memory[0], cotangent[0]
    coarse, fine = angle_tables()
    (
        tokens_pair,
        cot,
        wide,
        out_wide,
        normed,
        experts,
        gates,
        keys,
        values,
        queries,
        attended,
        probs,
        heads_own,
        heads_peer,
        mixed,
        out_part,
        out_part_in,
        sinus,
        counts,
    ) = front(
        mem_len,
        [
            attn_norm_gain,
            attn_norm_bias,
            value_route[0].transpose(2, 3, 0, 1).reshape(2 * H, 2, BLOCK),
            output_route[0].transpose(1, 2, 0),
            bias_u,
            bias_v,
            value_router.T,
            out_router.T,
            coarse,
            fine,
        ],
        [memory, tokens, cotangent, value_weight.T, key_weight.T, query_weight.T, rel_weight.T, out_weight],
    )
    resid, final_mine, final_theirs, norm_part, low, hidden, grad_before, grad_up_bias = feed(
        spot,
        tokens_pair,
        out_part,
        out_part_in,
        cot,
        ffn_norm_gain,
        ffn_norm_bias,
        up_weight,
        up_bias,
        down_weight,
        down_bias,
    )
    pay_back, pay_in, bias_sums, grad_far, grad_resid, result, grad_out_logit, feed_sums, *early = back(
        norm_part,
        final_theirs,
        ffn_norm_gain,
        [
            low,
            hidden,
            grad_before,
            cot,
            resid,
            out_wide,
            heads_own,
            heads_peer,
            gates,
            final_mine,
            mixed,
            values,
            probs,
            attended,
            keys,
            queries,
        ],
    )
    grad_tokens, small_sum, grad_down, up_both, out_both, wide_both, rest_both = close(
        attn_norm_gain,
        feed_sums,
        grad_up_bias,
        bias_sums,
        counts,
        pay_back,
        pay_in,
        grad_out_logit,
        grad_far,
        early,
        [experts, gates, wide, normed, sinus, memory, tokens, grad_resid],
    )
    outs = list(arrange(result, grad_tokens, small_sum, grad_down, up_both, out_both, wide_both, rest_both))
    outs[0], outs[1], outs[12] = outs[0][None], outs[1][None], outs[12].T
    return tuple(outs)


def solution(mesh):
    in_specs = (
        P("dp", "seq", None),
        P("dp", "seq", None),
        P("dp", "seq", None),
        P("dp"),
        P("dp", None, "seq", None, None),
        P("dp", "seq", None, None),
        P(),
        P(),
        P(),
        P(),
        P(),
        P(),
        P(),
        P(),
        P(),
        P(),
        P(),
        P(),
        P(),
        P(),
        P(),
        P(),
        P(),
    )
    out_specs = (
        P("dp", "seq", None),
        P("dp", "seq", None),
        P(("dp", "seq")),
        P(("dp", "seq")),
        P(("dp", "seq"), None),
        P(("dp", "seq"), None),
        P(("dp", "seq"), None),
        P(),
        P(),
        P(("dp", "seq"), None),
        P(("dp", "seq"), None),
        P(("dp", "seq"), None),
        P(None, ("dp", "seq")),
        P(("dp", "seq")),
        P(("dp", "seq")),
        P(("dp", "seq"), None),
        P(("dp", "seq")),
        P(("dp", "seq"), None),
        P(("dp", "seq")),
        P(),
    )
    return jax.shard_map(body, mesh=mesh, in_specs=in_specs, out_specs=out_specs, check_vma=False)
```

```python
from functools import partial
import math

import jax
import jax.numpy as jnp
from jax import lax
from jax.experimental import pallas as pl
from jax.experimental.pallas import tpu as pltpu
from jax.sharding import PartitionSpec as P

D = 1024
H = 4
DH = 112
E = 5
FF = 4096
LEN = 1024
SLOT = 128
BLOCK = 256
EXPERTS = 2 * E * SLOT
KEY_AT = EXPERTS
QUERY_AT = KEY_AT + 2 * SLOT
ROUTER_AT = QUERY_AT + 2 * SLOT
WIDE = ROUTER_AT + SLOT
SCALE = DH ** (-0.5)
MASKED = -1e30
EPS = 1e-05
BF16 = jnp.bfloat16
F32 = jnp.float32
VMEM_BYTES = 60 * 1024 * 1024
IN_VMEM = pl.BlockSpec(memory_space=pltpu.VMEM)
IN_SMEM = pl.BlockSpec(memory_space=pltpu.SMEM)
ANYWHERE = pl.BlockSpec(memory_space=pl.ANY)
MESH = pl.DeviceIdType.MESH


def dot(left, right, left_dim=1, right_dim=0):
    return lax.dot_general(
        left, right, (((left_dim,), (right_dim,)), ((), ())), preferred_element_type=F32
    )


def struct(shape, kind=BF16):
    return jax.ShapeDtypeStruct(shape, kind)


def local_call(kernel, out_shape, scratch_shapes=(), smem=0, vmem=0, **kw):
    return pl.pallas_call(
        kernel,
        out_shape=out_shape,
        in_specs=[IN_SMEM] * smem + [IN_VMEM] * vmem,
        out_specs=[IN_VMEM] * len(out_shape),
        scratch_shapes=scratch_shapes,
        compiler_params=pltpu.CompilerParams(vmem_limit_bytes=VMEM_BYTES),
        **kw,
    )


def centered(rows):
    center = rows - jnp.mean(rows, axis=1, keepdims=True)
    inverse = lax.rsqrt(jnp.mean(center * center, axis=1, keepdims=True) + EPS)
    return center * inverse, inverse


def norm_back(grad, scaled, inverse, gain):
    through = grad * gain
    return inverse * (
        through
        - jnp.mean(through, axis=1, keepdims=True)
        - scaled * jnp.mean(through * scaled, axis=1, keepdims=True)
    )


def as_row(vector):
    return vector[...].astype(F32).reshape(1, vector.shape[0])


def chosen_lanes(route, first, core, lane, start):
    chosen = None
    for pair in range(2):
        for number in range(2):
            column = first + 4 * pair + number
            one = jnp.where(core == 0, route[:, column : column + 1], route[:, column + 2 : column + 3])
            hit = lane == one + (start + E * pair)
            chosen = hit if chosen is None else chosen | hit
    return chosen


def spots_of(core, chip):
    return [
        chip * 512 + core * BLOCK,
        chip * 512 + (1 - core) * BLOCK,
        (1 - chip) * 512 + core * BLOCK,
        (1 - chip) * 512 + (1 - core) * BLOCK,
    ]


def rows_at(start):
    return pl.ds(pl.multiple_of(start, BLOCK), BLOCK)


def attend(block, shown, qu, qv, keys, values, far_rel, attended, probs):
    rows = pl.ds(block * BLOCK, BLOCK)
    width = LEN + (block + 1) * BLOCK
    first_far = 2 * LEN - width
    content = dot(qu[rows, :], keys[:width, :], 1, 1)
    far = dot(qv[rows, :], far_rel[first_far:, :], 1, 1)
    near = pltpu.roll(far, width - BLOCK + 1, 1, stride=1, stride_axis=0)
    row_at = lax.broadcasted_iota(jnp.int32, (BLOCK, width), 0) + (LEN + block * BLOCK)
    key_at = lax.broadcasted_iota(jnp.int32, (BLOCK, width), 1)
    visible = (key_at <= row_at) & (key_at >= LEN - shown)
    scores = jnp.where(visible, (content + near) * SCALE, MASKED)
    highest = jnp.max(scores, axis=1, keepdims=True)
    weights = jnp.exp(scores - highest)
    total = jnp.sum(weights, axis=1, keepdims=True)
    low = (weights * (1.0 / total)).astype(BF16)
    probs[rows, :width] = low
    attended[rows, :] = dot(low, values[:width, :], 1, 0)


def two_heads(chip, own, peer):
    first = jnp.where(chip == 0, own.astype(F32), peer.astype(F32))
    second = jnp.where(chip == 0, peer.astype(F32), own.astype(F32))
    return first, second


def place():
    dp = lax.axis_index("dp")
    sq = lax.axis_index("seq")
    return dict(x=dp // 8, z=(dp // 2) % 4, y=(sq // 2) * 2 + dp % 2, core=sq % 2)


def device_of(at):
    return (at["x"] * 8 + at["z"] * 2 + at["y"] % 2, (at["y"] // 2) * 2 + at["core"])


def moved(at, axis, steps):
    other = dict(at)
    other[axis] = (at[axis] + steps) % 4
    return device_of(other)


PLAIN = (("x", 4), ("z", 4), ("ylo", 2), ("yhi", 2))
SPLIT = (("xhi", 2), ("z", 4), ("ylo", 2), ("yhi", 2), ("xlo", 2))


def part_of(name, where):
    return {"hi": where // 2, "lo": where % 2}.get(name[1:], where)


def chunk_of(ref, dims, axis, where):
    return ref.at[tuple(part_of(name, where) if name[0] == axis else slice(None) for name, _ in dims)]


def without(dims, axes):
    return tuple(dim for dim in dims if dim[0][0] not in axes)


def lead_shape(dims):
    return tuple(size for _, size in dims)


def halves(width):
    one = (width // 2 + 127) // 128 * 128
    return (0, one), (one, width - one)


def each_block(lead, size, step):
    if math.prod(lead) * size <= 64 * 1024:
        step(Ellipsis)
        return

    def run(number, carry):
        step(number)
        return carry

    lax.fori_loop(0, lead[0], run, 0)


class Links:
    def __init__(self, send_sem, recv_sem):
        self.send_sem, self.recv_sem, self.made, self.open = send_sem, recv_sem, [], {}

    def prepared(self, src, dst, device):
        slot = len(self.made)
        copy = pltpu.make_async_remote_copy(
            src_ref=src,
            dst_ref=dst,
            send_sem=self.send_sem.at[slot],
            recv_sem=self.recv_sem.at[slot],
            device_id=device,
            device_id_type=MESH,
        )
        self.made.append(copy)
        self.open[id(copy)] = copy
        return copy

    def settle(self, copies=None):
        for copy in list(self.open.values()) if copies is None else copies:
            copy.wait_send()
            del self.open[id(copy)]

    def send(self, src, dst, device):
        copy = self.prepared(src, dst, device)
        copy.start()
        return copy


def added(target, *terms):
    def add(index):
        total = terms[0][index].astype(F32)
        for term in terms[1:]:
            total += term[index].astype(F32)
        target[index] = total.astype(target.dtype)

    return add


class Stage:
    def __init__(self, links, at, ref, dims, axis, width, bufs, after):
        self.links, self.bufs, self.after = links, bufs, after
        self.left = lead_shape(without(dims, axis))
        self.cols = [pl.ds(*half) for half in halves(width)]
        self.sizes = [half[1] * bufs[0].shape[-2] for half in halves(width)]
        self.near = [chunk_of(ref, dims, axis, (at[axis] + steps) % 4) for steps in range(4)]
        self.ahead = [self.near[steps].at[..., self.cols[side]] for side, steps in ((0, 1), (1, 3))]
        self.far, self.close, self.summed = [], [], []
        for side, steps in ((0, 1), (1, 3)):
            device = moved(at, axis, steps)
            other = self.cols[1 - side]
            self.far.append(links.prepared(self.near[2].at[..., self.cols[side]], bufs[side], device))
            self.close.append(links.prepared(self.near[steps].at[..., other], bufs[2 + side], device))
            self.summed.append(links.prepared(bufs[side], bufs[4 + side], device))

    def launch_far(self):
        for copy in self.far:
            copy.start()

    def launch_near(self):
        for copy in self.close:
            copy.start()

    def forward(self):
        for side in range(2):
            self.far[side].wait_recv()
            each_block(self.left, self.sizes[side], added(self.bufs[side], self.bufs[side], self.ahead[side]))
            self.summed[side].start()

    def collect(self):
        for copy in self.close + self.summed:
            copy.wait_recv()
        for side in (0, 1):
            cols = self.cols[side]
            terms = self.near[0].at[..., cols], self.bufs[4 + side], self.bufs[3 - side]
            each_block(self.left, self.sizes[side], added(self.after.at[..., cols], *terms))

    def settle(self):
        self.links.settle(self.far + self.close + self.summed)


class DirectStage:
    def __init__(self, links, at, ref, dims, axis, width, bufs, after):
        self.bufs, self.after = bufs, after
        self.left = lead_shape(without(dims, axis))
        self.size = width * bufs[0].shape[-2]
        self.near = [chunk_of(ref, dims, axis, (at[axis] + steps) % 4) for steps in range(4)]
        self.copies = [
            links.prepared(self.near[steps], bufs[steps - 1], moved(at, axis, steps)) for steps in (1, 2, 3)
        ]

    def launch_far(self):
        for copy in self.copies:
            copy.start()

    def launch_near(self):
        pass

    def forward(self):
        pass

    def collect(self):
        for copy in self.copies:
            copy.wait_recv()
        each_block(self.left, self.size, added(self.after, self.near[0], *self.bufs))


def direct_scratch(dims, axis, rows, width):
    return [pltpu.VMEM(lead_shape(without(dims, axis)) + (rows, width), BF16)] * 3


def stage_scratch(dims, axis, rows, width):
    left = lead_shape(without(dims, axis))
    (_, one), (_, two) = halves(width)
    return [pltpu.VMEM(left + (rows, size), BF16) for size in (one, two, two, one, one, two)]


def launch(stages):
    for stage in stages:
        stage.launch_far()
    for stage in stages:
        stage.launch_near()


def greet(devices):
    barrier = pltpu.get_barrier_semaphore()
    for device in devices:
        pl.semaphore_signal(barrier, inc=1, device_id=device, device_id_type=MESH)


UP, DOWN, OUT, VALUE, KEYS, REST = range(6)
LAYOUTS = (PLAIN, SPLIT, PLAIN, PLAIN, PLAIN, PLAIN)
SHAPES = ((16, FF // 2), (32, D), (16, EXPERTS), (16, EXPERTS), (16, 4 * SLOT), (16, 3 * SLOT))
UP_FIRST = ((UP, 0, 256, "xyz"), (UP, 256, 256, "zxy"), (UP, 512, 256, "yzx"))
UP_PIECES = ((UP, 768, 512, "xyz"), (UP, 1280, 512, "zxy"), (UP, 1792, 256, "yzx"))
DOWN_PIECES = ((DOWN, 0, 384, "xyz"), (DOWN, 384, 384, "zxy"), (DOWN, 768, 256, "yzx"))
OUT_PIECES = ((OUT, 0, 512, "xzy"), (OUT, 512, 512, "zyx"), (OUT, 1024, 256, "yzx"))
VALUE_PIECES = ((VALUE, 0, 512, "xyz"), (VALUE, 512, 512, "zxy"), (VALUE, 1024, 256, "yzx"))
KEYS_PIECES = ((KEYS, 0, 256, "xyz"), (KEYS, 256, 256, "zxy"))
REST_PIECES = ((REST, 0, 384, "yzx"),)
BACK_PIECES = UP_PIECES + DOWN_PIECES + OUT_PIECES
EARLY = UP_FIRST + BACK_PIECES
LATE = VALUE_PIECES + KEYS_PIECES + REST_PIECES


def dims_after(piece, phases):
    return without(LAYOUTS[piece[0]], piece[3][:phases])


def after_shape(piece, phases):
    return lead_shape(dims_after(piece, phases)) + (SHAPES[piece[0]][0], piece[2])


def is_direct(piece, phase):
    return phase == 2 or phase == 1 and piece in LATE


def phase_scratch(piece, phase):
    made = direct_scratch if is_direct(piece, phase) else stage_scratch
    return made(dims_after(piece, phase), piece[3][phase], SHAPES[piece[0]][0], piece[2])


def copies_of(piece, phase):
    return 3 if is_direct(piece, phase) else 6


def stage_for(links, at, piece, phase, ref, take, after):
    made = DirectStage if is_direct(piece, phase) else Stage
    bufs = take(3 if is_direct(piece, phase) else 6)
    return made(links, at, ref, dims_after(piece, phase), piece[3][phase], piece[2], bufs, after)


def full_shape(array):
    return lead_shape(LAYOUTS[array]) + SHAPES[array]


def columns_of(ref, piece):
    return ref.at[..., pl.ds(piece[1], piece[2])]


class Fetches:
    def __init__(self, sems):
        self.sems, self.copies = sems, []

    def start(self, src, dst):
        copy = pltpu.make_async_copy(src, dst, self.sems.at[len(self.copies)])
        copy.start()
        self.copies.append(copy)
        return copy


def wait_for(*copies):
    for copy in copies:
        copy.wait()


def forward(stages):
    for stage in stages:
        stage.forward()


def collect(stages):
    for stage in stages:
        stage.collect()


def others_of(at):
    sibling = dict(at)
    sibling["core"] = 1 - at["core"]
    return device_of(sibling), moved(at, "y", 2)


STEP = 256
STEPS = FF // 2 // STEP


def feed_kernel(*refs):
    refs = list(refs)
    take = lambda count: [refs.pop(0) for _ in range(count)]
    rows, part_mine, part_theirs, cot, gain, shift, up_bias, down_bias = take(8)
    up_given, down_given = take(2)
    final_mine, final_theirs, grad_part, grad_up_bias = take(4)
    afters = take(len(UP_FIRST))
    outs = take(3)
    resid, hidden, grad_up, write_sem = take(4)
    send_sem, recv_sem, fetch_sem, up, down, low, low_turned, grad_all, bias_row = take(9)
    before_a, before_b, above_a, above_b = take(4)
    fetches, writes = Fetches(fetch_sem), Fetches(write_sem)
    links = Links(send_sem, recv_sem)
    at = place()
    first = at["core"] * (FF // 2)

    def own(step):
        return pl.ds(step * STEP, STEP)

    for step in range(STEPS):
        there = pl.ds(pl.multiple_of(first + step * STEP, STEP), STEP)
        fetches.start(up_given.at[:, there], up.at[:, own(step)])
        fetches.start(down_given.at[there, :], down.at[own(step), :])
    devices = [moved(at, axis, steps) for axis in "xyz" for steps in (1, 3)]
    greet(devices)
    for side in range(2):
        here = slice(side * BLOCK, (side + 1) * BLOCK)
        total = rows[here, :].astype(F32) + (part_mine[here, :].astype(F32) + part_theirs[here, :].astype(F32))
        resid[here, :] = total
        scaled, _ = centered(total)
        low[here, :] = (scaled * as_row(gain) + as_row(shift)).astype(BF16)
    writes.start(resid, outs[0])
    low_turned[...] = low[...].T
    bias_row[...] = as_row(up_bias)

    def ahead(step, before, above):
        bias = bias_row[:, pl.ds(pl.multiple_of(first + step * STEP, STEP), STEP)]
        before[...] = dot(low[...], up[:, own(step)]) + bias
        above[...] = dot(cot[...], down[own(step), :], 1, 1)

    def weigh(step):
        block = dot(low_turned[...], grad_all[:, own(step)]).astype(BF16)
        grad_up[..., own(step)] = block.reshape(lead_shape(PLAIN) + (16, STEP))

    def activate(step, before, above):
        value = before[...]
        below = 0.5 * (1.0 + lax.erf(value * (0.5**0.5)))
        hidden[:, own(step)] = (value * below).astype(BF16)
        slope = below + value * (jnp.exp(-0.5 * value * value) * ((2.0 * math.pi) ** -0.5))
        grad_low = (above[...] * slope).astype(BF16)
        grad_all[:, own(step)] = grad_low
        grad_up_bias[:, own(step)] = jnp.sum(grad_low.astype(F32), axis=0, keepdims=True)

    stages = []
    for piece, after in zip(UP_FIRST, afters):
        stages.append(stage_for(links, at, piece, 0, columns_of(grad_up, piece), take, after))
    pairs = (before_a, above_a), (before_b, above_b)
    wait_for(*fetches.copies[:2])
    ahead(0, *pairs[0])
    for step in range(STEPS):
        if step + 1 < STEPS:
            wait_for(*fetches.copies[2 * step + 2 : 2 * step + 4])
            ahead(step + 1, *pairs[(step + 1) % 2])
        activate(step, *pairs[step % 2])
        if step > 0:
            weigh(step - 1)
        if step == 1:
            pl.semaphore_wait(pltpu.get_barrier_semaphore(), len(devices))
        if 1 <= step <= len(stages):
            launch(stages[step - 1 : step])
        if 4 <= step < 4 + len(stages):
            forward(stages[step - 4 : step - 3])
    weigh(STEPS - 1)
    writes.start(hidden, outs[1])
    writes.start(grad_up, outs[2])
    grad_part[...] = dot(grad_all[...], up[...], 1, 1).astype(BF16)
    final_mine[...] = resid[:BLOCK, :] + dot(hidden[:BLOCK, :], down[...]) + as_row(down_bias)
    final_theirs[...] = dot(hidden[BLOCK:, :], down[...]).astype(BF16)
    collect(stages)
    wait_for(*writes.copies)
    links.settle()


def feed(rows, part_mine, part_theirs, cot, gain, shift, up_bias, down_bias, up, down):
    pair = (2 * BLOCK, D)
    outs = [struct((BLOCK, D), F32), struct((BLOCK, D)), struct(pair), struct((1, FF // 2), F32)]
    outs += [struct(after_shape(piece, 1)) for piece in UP_FIRST]
    scratch = []
    for piece in UP_FIRST:
        scratch += phase_scratch(piece, 0)
    written = [struct(pair, F32), struct((2 * BLOCK, FF // 2)), struct(full_shape(UP))]
    return pl.pallas_call(
        feed_kernel,
        out_shape=outs + written,
        in_specs=[IN_VMEM] * 8 + [ANYWHERE] * 2,
        out_specs=[IN_VMEM] * len(outs) + [ANYWHERE] * len(written),
        scratch_shapes=[pltpu.VMEM(out.shape, out.dtype) for out in written]
        + [
            pltpu.SemaphoreType.DMA((len(written),)),
            pltpu.SemaphoreType.DMA((6 * len(UP_FIRST),)),
            pltpu.SemaphoreType.DMA((6 * len(UP_FIRST),)),
            pltpu.SemaphoreType.DMA((2 * STEPS,)),
            pltpu.VMEM((D, FF // 2), BF16),
            pltpu.VMEM((FF // 2, D), BF16),
            pltpu.VMEM(pair, BF16),
            pltpu.VMEM((D, 2 * BLOCK), BF16),
            pltpu.VMEM((2 * BLOCK, FF // 2), BF16),
            pltpu.VMEM((1, FF), F32),
        ]
        + [pltpu.VMEM((2 * BLOCK, STEP), F32)] * 4
        + scratch,
        compiler_params=pltpu.CompilerParams(
            collective_id=3, has_side_effects=True, vmem_limit_bytes=VMEM_BYTES
        ),
    )(rows, part_mine, part_theirs, cot, gain, shift, up_bias, down_bias, up, down)


KEY_BLOCKS = 2 * LEN // BLOCK


def rows_seeing(block):
    return pl.ds(max(0, block - 4) * BLOCK, LEN - max(0, block - 4) * BLOCK)


def back_kernel(*refs):
    refs = list(refs)
    take = lambda count: [refs.pop(0) for _ in range(count)]
    grad_part, final_theirs, gain = take(3)
    far_away = take(16)
    pay, pay_in, sums, grad_far, grad_resid, result, grad_logit, feed_sums = take(8)
    afters = take(len(BACK_PIECES))
    written = take(2)
    send_sem, recv_sem, fetch_sem, write_sem = take(4)
    writes = Fetches(write_sem)
    local = take(16)
    grads = {UP: local[0]}
    hidden, cot, resid, out_wide, gates, heads_own, heads_peer, mixed, probs, attended, values, keys, queries, normed, final_mine = local[1:]
    qu, qv, far_rel = (queries.at[pl.ds(start, size)] for start, size in ((0, LEN), (LEN, LEN), (2 * LEN, 2 * LEN)))
    part_in, final_in, given, given_in, grad_low, grad_mixed = take(6)
    grad_out, grad_u, grad_query, grad_keys, grad_values, far_sum, grad_experts = take(7)
    grads.update(zip((DOWN, OUT), take(2)))
    grads[VALUE] = grads[UP].at[..., pl.ds(0, EXPERTS)]
    links, fetches = Links(send_sem, recv_sem), Fetches(fetch_sem)
    loads = [fetches.start(src, dst) for src, dst in zip(far_away, local)]
    up_load = loads.pop(0)
    at = place()
    core, chip = at["core"], at["y"] // 2
    sibling, peer = others_of(at)
    devices = [moved(at, axis, steps) for axis in "xyz" for steps in (1, 2, 3)] + [sibling]
    greet(devices)
    pl.semaphore_wait(pltpu.get_barrier_semaphore(), len(devices))
    parts = [
        links.send(grad_part.at[pl.ds((1 - side) * BLOCK, BLOCK)], part_in.at[pl.ds(side * BLOCK, BLOCK)], sibling)
        for side in range(2)
    ]
    final_copy = links.send(final_theirs, final_in, sibling)

    unused = list(afters)

    def go(pieces):
        stages = []
        for piece in pieces:
            source = columns_of(grads[piece[0]], piece)
            stages.append(stage_for(links, at, piece, 0, source, take, unused.pop(0)))
        launch(stages)
        return stages

    up_load.wait()
    up_stages = go(UP_PIECES)

    def fill(array, left, right, start, width):
        block = dot(left[...], right[:, start : start + width], 0, 0).astype(BF16)
        grads[array][..., pl.ds(start, width)] = block.reshape(lead_shape(LAYOUTS[array]) + (SHAPES[array][0], width))

    wait_for(*loads[:2])
    down_stages = []
    for piece in DOWN_PIECES:
        fill(DOWN, hidden, cot, piece[1], piece[2])
        if piece[3][0] != "y":
            down_stages += go([piece])
    loads[2].wait()
    for copy in parts:
        copy.wait_recv()
    for side in range(2):
        here = slice(side * BLOCK, (side + 1) * BLOCK)
        scaled, inverse = centered(resid[here, :])
        grad = grad_part[here, :].astype(F32) + part_in[here, :].astype(F32)
        above = cot[here, :].astype(F32)
        total = above + norm_back(grad, scaled, inverse, as_row(gain))
        grad_low[here, :] = total.astype(BF16)
        if side == 0:
            grad_resid[...] = total
            feed_sums[0:1, :] = jnp.sum(grad * scaled, axis=0, keepdims=True)
            feed_sums[1:2, :] = jnp.sum(grad, axis=0, keepdims=True)
            feed_sums[2:3, :] = jnp.sum(above, axis=0, keepdims=True)
    wait_for(*loads[3:5])
    grad_mixed[...] = dot(grad_low[...], out_wide[...], 1, 1)
    for side in range(2):
        here = slice(side * BLOCK, (side + 1) * BLOCK)
        gate = gates[(2 + side) * BLOCK : (3 + side) * BLOCK, :]
        totals = []
        for pair in range(2):
            total = jnp.zeros((BLOCK, SLOT), F32)
            for expert in range(E):
                slot = pair * E + expert
                weight = gate[:, 2 * E + slot : 2 * E + slot + 1]
                total += weight * grad_mixed[here, slot * SLOT : (slot + 1) * SLOT]
            totals.append(total)
        given[0, side] = jnp.where(chip == 0, totals[0], totals[1]).astype(BF16)
        given[1, side] = jnp.where(chip == 0, totals[1], totals[0]).astype(BF16)
    arrived = links.send(given.at[1], given_in, peer)
    down_stages += go(DOWN_PIECES[2:])
    forward(up_stages)
    wait_for(*loads[5:8])
    out_stages = []
    for piece in OUT_PIECES:
        fill(OUT, grad_low, mixed, piece[1], piece[2])
        out_stages += go([piece])
    places = spots_of(core, chip)
    for side in range(2):
        grad_out[rows_at(places[side]), :] = given[0, side]
    wait_for(*loads[8:10])
    arrived.wait_recv()
    for side in range(2):
        grad_out[rows_at(places[2 + side]), :] = given_in[side]
    moving = []

    def give(first, held, base):
        for side in range(2):
            pay[first + side] = held[rows_at(places[side] + base), :]
            src = held.at[rows_at(places[2 + side] + base)]
            moving.append(links.send(src, pay_in.at[first + side], peer))

    for block in range(KEY_BLOCKS):
        cols, rows = pl.ds(block * BLOCK, BLOCK), rows_seeing(block)
        grad_values[cols, :] = dot(probs[rows, cols], grad_out[rows, :], 0, 0).astype(BF16)
    give(4, grad_values, 0)
    give(6, grad_values, LEN)
    value_moves = list(moving)
    lane = lax.broadcasted_iota(jnp.int32, (BLOCK, SLOT), 1)
    for side in range(2):
        here = slice(side * BLOCK, (side + 1) * BLOCK)
        gate = gates[(2 + side) * BLOCK : (3 + side) * BLOCK, :]
        heads = two_heads(chip, heads_own[side], heads_peer[side])
        total = jnp.zeros((BLOCK, SLOT), F32)
        for slot in range(2 * E):
            part = grad_mixed[here, slot * SLOT : (slot + 1) * SLOT] * heads[slot // E]
            total += jnp.where(lane == 2 * E + slot, jnp.sum(part, axis=1, keepdims=True), 0.0)
        grad_logit[here, :] = (total * gate * (1.0 - gate)).astype(BF16)
    forward(down_stages)
    wait_for(*loads[10:13])
    blocks = LEN // BLOCK
    sum_u = jnp.zeros((1, SLOT), F32)

    def score_rows(block):
        rows = pl.ds(block * BLOCK, BLOCK)
        width = LEN + (block + 1) * BLOCK
        above = grad_out[rows, :]
        grad_probs = dot(above, values[:width, :], 1, 1)
        inner = jnp.sum(above.astype(F32) * attended[rows, :], axis=1, keepdims=True)
        scores = (probs[rows, :width].astype(F32) * ((grad_probs - inner) * SCALE)).astype(BF16)
        probs[rows, :width] = scores
        part = dot(scores, keys[:width, :])
        grad_u[rows, :] = part
        return jnp.sum(part, axis=0, keepdims=True)

    for block in (0, 1):
        sum_u += score_rows(block)
    forward(out_stages)
    for block in (2, 3):
        sum_u += score_rows(block)
    for block in range(KEY_BLOCKS):
        cols, rows = pl.ds(block * BLOCK, BLOCK), rows_seeing(block)
        grad_keys[cols, :] = dot(probs[rows, cols], qu[rows, :], 0, 0).astype(BF16)
    give(0, grad_keys, 0)
    give(2, grad_keys, LEN)
    far_sum[...] = jnp.zeros_like(far_sum)
    down = lax.broadcasted_iota(jnp.int32, (BLOCK, BLOCK), 0)
    across = lax.broadcasted_iota(jnp.int32, (BLOCK, BLOCK), 1)
    flip = (down + across == BLOCK - 1).astype(F32).astype(BF16)
    sum_v = jnp.zeros((1, SLOT), F32)
    for block in range(blocks):
        rows = pl.ds(block * BLOCK, BLOCK)
        width = LEN + (block + 1) * BLOCK
        first_far = 2 * LEN - width
        far = pltpu.roll(dot(flip, probs[rows, :width]), 0, 1, stride=1, stride_axis=0).astype(BF16)
        turned = dot(flip, far).astype(BF16)
        part = dot(turned, far_rel[first_far:, :])
        far_sum[first_far:, :] += dot(turned, qv[rows, :], 0, 0)
        grad_query[rows, :] = (grad_u[rows, :] + part).astype(BF16)
        sum_v += jnp.sum(part, axis=0, keepdims=True)
    give(8, grad_query, 0)
    sums[0:1, :] = sum_u
    sums[1:2, :] = sum_v
    grad_far[...] = far_sum[...].astype(BF16)
    for copy in value_moves:
        copy.wait_recv()
    for block in range(4):
        rows = slice(block * BLOCK, (block + 1) * BLOCK)
        heads = two_heads(chip, pay[4 + block], pay_in[4 + block])
        for slot in range(2 * E):
            weight = gates[rows, slot : slot + 1]
            grad_experts[rows, slot * SLOT : (slot + 1) * SLOT] = (weight * heads[slot // E]).astype(BF16)
    writes.start(grad_experts, written[0])
    loads[13].wait()
    collect(up_stages)
    for stage in up_stages:
        stage.settle()
    for piece in VALUE_PIECES:
        fill(VALUE, normed, grad_experts, piece[1], piece[2])
    writes.start(grads[VALUE], written[1])
    loads[14].wait()
    final_copy.wait_recv()
    result[...] = (final_mine[...] + final_in[...].astype(F32)).astype(BF16)
    collect(down_stages)
    collect(out_stages)
    for copy in moving[4:]:
        copy.wait_recv()
    wait_for(*writes.copies)
    links.settle()


def back(grad_part, final_theirs, gain, later):
    scratch = []
    for piece in BACK_PIECES:
        scratch += phase_scratch(piece, 0)
    copies = 2 + 1 + 1 + 10 + 6 * len(BACK_PIECES)
    seq = (2 * LEN, SLOT)
    rows = (2 * BLOCK, D)
    outs = [struct((10, BLOCK, SLOT)), struct((10, BLOCK, SLOT)), struct((2, SLOT), F32), struct(seq)]
    outs += [struct((BLOCK, D), F32), struct((BLOCK, D)), struct((2 * BLOCK, SLOT)), struct((8, D), F32)]
    outs += [struct(after_shape(piece, 1)) for piece in BACK_PIECES]
    return pl.pallas_call(
        back_kernel,
        out_shape=outs + [struct((4 * BLOCK, EXPERTS)), struct(full_shape(VALUE))],
        in_specs=[IN_VMEM] * 3 + [ANYWHERE] * len(later),
        out_specs=[IN_VMEM] * len(outs) + [ANYWHERE] * 2,
        scratch_shapes=[
            pltpu.SemaphoreType.DMA((copies,)),
            pltpu.SemaphoreType.DMA((copies,)),
            pltpu.SemaphoreType.DMA((len(later),)),
            pltpu.SemaphoreType.DMA((2,)),
        ]
        + [pltpu.VMEM(operand.shape, operand.dtype) for operand in later]
        + [
            pltpu.VMEM(rows, BF16),
            pltpu.VMEM((BLOCK, D), BF16),
            pltpu.VMEM((2, 2, BLOCK, SLOT), BF16),
            pltpu.VMEM((2, BLOCK, SLOT), BF16),
            pltpu.VMEM(rows, BF16),
            pltpu.VMEM((2 * BLOCK, EXPERTS), F32),
            pltpu.VMEM((LEN, SLOT), BF16),
            pltpu.VMEM((LEN, SLOT), F32),
            pltpu.VMEM((LEN, SLOT), BF16),
            pltpu.VMEM(seq, BF16),
            pltpu.VMEM(seq, BF16),
            pltpu.VMEM(seq, F32),
            pltpu.VMEM((4 * BLOCK, EXPERTS), BF16),
        ]
        + [pltpu.VMEM(full_shape(array), BF16) for array in (DOWN, OUT)]
        + scratch,
        compiler_params=pltpu.CompilerParams(
            collective_id=1, has_side_effects=True, vmem_limit_bytes=VMEM_BYTES
        ),
    )(grad_part, final_theirs, gain, *later)


COUNT_ROW = 2 * H
VECTOR_ROW = 16
UP_BIAS_ROW = VECTOR_ROW + 5 * 8
SMALL_ROWS = UP_BIAS_ROW + FF // SLOT


def lay(target, first, vector):
    for row in range(vector.shape[1] // SLOT):
        target[first + row : first + row + 1, :] = vector[:, row * SLOT : (row + 1) * SLOT]


def close_kernel(*refs):
    refs = list(refs)
    take = lambda count: [refs.pop(0) for _ in range(count)]
    gain, feed_sums, grad_up_bias, bias_sums, counts, pay, pay_in, grad_logit, grad_far = take(9)
    early = take(len(EARLY))
    far_away = take(10)
    grad_tokens, small_out, down_out = take(3)
    both = dict(zip((UP, OUT, VALUE, KEYS, REST), take(5)))
    send_sem, recv_sem, own_sem, fetch_sem = take(4)
    local = take(10)
    grads = {VALUE: local.pop(0)}
    normed, experts, gates, wide, grad_experts, sinus, memory, tokens, grad_resid = local
    part, part_in, half_bias, grad_keys, grad_routers = take(5)
    grads.update(zip((KEYS, REST), take(2)))
    totals = dict(zip((UP, DOWN, OUT, VALUE, KEYS, REST), take(6)))
    slots = take(4)
    links, fetches = Links(send_sem, recv_sem), Fetches(fetch_sem)
    loads = [fetches.start(src, dst) for src, dst in zip(far_away, [grads[VALUE]] + local)]
    value_load = loads.pop(0)
    at = place()
    core, chip = at["core"], at["y"] // 2
    sibling, _ = others_of(at)
    high, low = at["x"] // 2, at["x"] % 2
    stays = (high == low) & (low == core)
    ahead, behind = dict(at), dict(at)
    ahead["x"], ahead["core"] = 2 * core + high, low
    behind["x"], behind["core"] = 2 * low + core, high
    ahead, behind = device_of(ahead), device_of(behind)
    devices = [moved(at, axis, steps) for axis in "xyz" for steps in (1, 2, 3)] + [sibling]
    greet(devices)

    def greet_more():
        greet([ahead, behind])
        pl.semaphore_wait(pltpu.get_barrier_semaphore(), len(devices) + 2)

    pl.when(jnp.logical_not(stays))(greet_more)
    pl.when(stays)(lambda: pl.semaphore_wait(pltpu.get_barrier_semaphore(), len(devices)))

    def begin(jobs):
        stages, later = [], []
        for piece, phase, ref in jobs:
            after = take(1)[0] if phase < 2 else totals[piece[0]].at[:, pl.ds(piece[1], piece[2])]
            stages.append(stage_for(links, at, piece, phase, ref, take, after))
            if phase < 2:
                later.append((piece, phase + 1, after))
        launch(stages)
        return stages, later

    def spread(number, value):
        axis = "xyz"[number]
        here = slots[number].at[at[axis]]
        here[...] = value
        return [links.send(here, here, moved(at, axis, steps)) for steps in (1, 2, 3)]

    def gathered(number, copies):
        for copy in copies:
            copy.wait_recv()
        one = slots[number]
        return (one[0] + one[1]) + (one[2] + one[3])

    def fill(array, right, start):
        width = right.shape[1]
        block = dot(normed[...], right[...], 0, 0).astype(BF16)
        grads[array][..., pl.ds(start, width)] = block.reshape(lead_shape(PLAIN) + (16, width))

    value_load.wait()
    value_stages, value_jobs = begin([(piece, 0, columns_of(grads[VALUE], piece)) for piece in VALUE_PIECES])
    for block in range(4):
        rows = slice(block * BLOCK, (block + 1) * BLOCK)
        key_heads = two_heads(chip, pay[block], pay_in[block])
        if block >= 2:
            query_heads = two_heads(chip, pay[6 + block], pay_in[6 + block])
        for pair in range(2):
            grad_keys[rows, pair * SLOT : (pair + 1) * SLOT] = key_heads[pair].astype(BF16)
            query = query_heads[pair].astype(BF16) if block >= 2 else jnp.zeros((BLOCK, SLOT), BF16)
            grad_keys[rows, (2 + pair) * SLOT : (3 + pair) * SLOT] = query
    loads[0].wait()
    fill(KEYS, grad_keys, 0)
    key_stages, key_jobs = begin([(piece, 0, columns_of(grads[KEYS], piece)) for piece in KEYS_PIECES])
    wait_for(*loads[1:3])
    lane = lax.broadcasted_iota(jnp.int32, (BLOCK, SLOT), 1)
    for block in range(4):
        rows = slice(block * BLOCK, (block + 1) * BLOCK)
        gate = gates[rows, :]
        value_heads = two_heads(chip, pay[4 + block], pay_in[4 + block])
        total = jnp.zeros((BLOCK, SLOT), F32)
        for slot in range(2 * E):
            expert = experts[rows, slot * SLOT : (slot + 1) * SLOT].astype(F32)
            inner = jnp.sum(value_heads[slot // E] * expert, axis=1, keepdims=True)
            total += jnp.where(lane == slot, inner, 0.0)
        total = total * gate * (1.0 - gate)
        if block >= 2:
            total += grad_logit[(block - 2) * BLOCK : (block - 1) * BLOCK, :].astype(F32)
        grad_routers[rows, :] = total.astype(BF16)
    fill(REST, grad_routers, 2 * SLOT)
    loads[5].wait()
    rel = dot(sinus[...], grad_far[...], 0, 0).astype(BF16).reshape(lead_shape(PLAIN) + (16, SLOT))
    blank = jnp.zeros((), BF16)
    grads[REST][..., :SLOT] = jnp.where(chip == 0, rel, blank)
    grads[REST][..., SLOT : 2 * SLOT] = jnp.where(chip == 1, rel, blank)
    rest_stages, rest_jobs = begin([(piece, 0, columns_of(grads[REST], piece)) for piece in REST_PIECES])
    forward(value_stages)
    early_stages, early_jobs = begin([(piece, 1, ref) for piece, ref in zip(EARLY, early)])
    wait_for(*loads[3:5])
    halves_in = []
    for block in (1, 3, 0, 2):
        rows = slice(block * BLOCK, (block + 1) * BLOCK)
        total = dot(grad_experts[rows, :], wide[:EXPERTS, :]) + dot(grad_keys[rows, :], wide[KEY_AT:ROUTER_AT, :])
        part[block] = (total + dot(grad_routers[rows, :], wide[ROUTER_AT:, :])).astype(BF16)
        if block % 2 == 1:
            halves_in.append(links.send(part.at[block], part_in.at[block // 2], sibling))
        if block == 3:
            forward(key_stages)
    forward(rest_stages)
    collect(value_stages)
    value_stages, value_jobs = begin(value_jobs)
    collect(key_stages)
    key_stages, key_jobs = begin(key_jobs)
    wait_for(*loads[6:])
    for copy in halves_in:
        copy.wait_recv()
    gain_sum = jnp.zeros((1, D), F32)
    bias_sum = jnp.zeros((1, D), F32)
    for side, rows in enumerate((memory, tokens)):
        scaled, inverse = centered(rows[...].astype(F32))
        grad = part[2 * side].astype(F32) + part_in[side].astype(F32)
        gain_sum += jnp.sum(grad * scaled, axis=0, keepdims=True)
        bias_sum += jnp.sum(grad, axis=0, keepdims=True)
        if side == 1:
            grad_tokens[...] = grad_resid[...] + norm_back(grad, scaled, inverse, as_row(gain))
    small = small_out
    small[:COUNT_ROW, :] = jnp.zeros((COUNT_ROW, SLOT), F32)
    small[COUNT_ROW:VECTOR_ROW, :] = counts[...]
    for number in range(2):
        small[pl.ds(H * number + 2 * chip + core, 1), :] = bias_sums[number : number + 1, :]
    lay(small, VECTOR_ROW, gain_sum)
    lay(small, VECTOR_ROW + 8, bias_sum)
    for number in range(3):
        lay(small, VECTOR_ROW + 16 + 8 * number, feed_sums[number : number + 1, :])
    small[UP_BIAS_ROW:, :] = jnp.zeros((FF // SLOT, SLOT), F32)
    lay(half_bias, 0, grad_up_bias[...])
    half = FF // 2 // SLOT
    small[pl.ds(pl.multiple_of(UP_BIAS_ROW + core * half, 8), half), :] = half_bias[...]
    copies = spread(0, small[...])
    forward(early_stages)
    collect(rest_stages)
    rest_stages, rest_jobs = begin(rest_jobs)
    collect(value_stages)
    value_stages, value_jobs = begin(value_jobs)
    collect(key_stages)
    key_stages, key_jobs = begin(key_jobs)
    copies = spread(1, gathered(0, copies))
    collect(early_stages)
    early_stages, early_jobs = begin(early_jobs)
    collect(rest_stages)
    rest_stages, rest_jobs = begin(rest_jobs)
    copies = spread(2, gathered(1, copies))
    collect(early_stages)
    last = []
    away = links.prepared(totals[DOWN], down_out, ahead)
    here = pltpu.make_async_copy(totals[DOWN], down_out, own_sem)
    pl.when(jnp.logical_not(stays))(away.start)
    pl.when(stays)(here.start)

    def exchange(arrays):
        for array in arrays:
            other = pl.ds(pl.multiple_of((1 - core) * 8, 8), 8)
            last.append(links.send(totals[array].at[other], both[array].at[core], sibling))
            both[array][core] = totals[array][pl.ds(pl.multiple_of(core * 8, 8), 8), :]

    exchange((UP, OUT))
    collect(value_stages)
    collect(key_stages)
    exchange((VALUE, KEYS))
    collect(rest_stages)
    exchange((REST,))
    pair = slots[3]
    pair[core] = gathered(2, copies)
    last.append(links.send(pair.at[core], pair.at[core], sibling))
    for copy in last:
        copy.wait_recv()
    small_out[...] = pair[0] + pair[1]
    pl.when(jnp.logical_not(stays))(away.wait)
    pl.when(stays)(here.wait)
    for copy in links.made:
        if copy is not away:
            copy.wait_send()


def close(gain, feed_sums, grad_up_bias, bias_sums, counts, pay, pay_in, grad_logit, grad_far, early, later):
    scratch = []
    copies = 2 + 9 + 1 + 1 + 5

    def round_of(pieces, phase):
        nonlocal copies
        for piece in pieces:
            if phase < 2:
                scratch.append(pltpu.VMEM(after_shape(piece, phase + 1), BF16))
            scratch.extend(phase_scratch(piece, phase))
            copies += copies_of(piece, phase)

    round_of(VALUE_PIECES, 0)
    round_of(KEYS_PIECES, 0)
    round_of(REST_PIECES, 0)
    round_of(EARLY, 1)
    round_of(VALUE_PIECES + KEYS_PIECES, 1)
    round_of(REST_PIECES, 1)
    round_of(VALUE_PIECES + KEYS_PIECES, 2)
    round_of(EARLY, 2)
    round_of(REST_PIECES, 2)
    outs = [struct((BLOCK, D), F32), struct((SMALL_ROWS, SLOT), F32), struct(SHAPES[DOWN], F32)]
    outs += [struct((2, 8, SHAPES[array][1]), F32) for array in (UP, OUT, VALUE, KEYS, REST)]
    return pl.pallas_call(
        close_kernel,
        out_shape=outs,
        in_specs=[IN_VMEM] * (9 + len(EARLY)) + [ANYWHERE] * len(later),
        out_specs=[IN_VMEM] * len(outs),
        scratch_shapes=[
            pltpu.SemaphoreType.DMA((copies,)),
            pltpu.SemaphoreType.DMA((copies,)),
            pltpu.SemaphoreType.DMA,
            pltpu.SemaphoreType.DMA((len(later),)),
        ]
        + [pltpu.VMEM(operand.shape, operand.dtype) for operand in later]
        + [
            pltpu.VMEM((4, BLOCK, D), BF16),
            pltpu.VMEM((2, BLOCK, D), BF16),
            pltpu.VMEM((FF // 2 // SLOT, SLOT), F32),
            pltpu.VMEM((4 * BLOCK, 4 * SLOT), BF16),
            pltpu.VMEM((4 * BLOCK, SLOT), BF16),
        ]
        + [pltpu.VMEM(full_shape(array), BF16) for array in (KEYS, REST)]
        + [pltpu.VMEM(SHAPES[array], F32) for array in (UP, DOWN, OUT, VALUE, KEYS, REST)]
        + [pltpu.VMEM((4, SMALL_ROWS, SLOT), F32)] * 3
        + [pltpu.VMEM((2, SMALL_ROWS, SLOT), F32)]
        + scratch,
        compiler_params=pltpu.CompilerParams(
            collective_id=2, has_side_effects=True, vmem_limit_bytes=VMEM_BYTES
        ),
    )(gain, feed_sums, grad_up_bias, bias_sums, counts, pay, pay_in, grad_logit, grad_far, *early, *later)


FRONT_OUTS = (
    ((2 * BLOCK, D), BF16),
    ((2 * BLOCK, D), BF16),
    ((WIDE, D), BF16),
    ((EXPERTS, D), BF16),
    ((4 * BLOCK, D), BF16),
    ((4 * BLOCK, EXPERTS), BF16),
    ((4 * BLOCK, SLOT), F32),
    ((2 * LEN, SLOT), BF16),
    ((2 * LEN, SLOT), BF16),
    ((4 * LEN, SLOT), BF16),
    ((LEN, SLOT), F32),
    ((LEN, 2 * LEN), BF16),
    ((2, BLOCK, SLOT), BF16),
    ((2, BLOCK, SLOT), BF16),
    ((2 * BLOCK, EXPERTS), BF16),
    ((2 * BLOCK, D), BF16),
    ((2 * BLOCK, D), BF16),
    ((2 * LEN, D), BF16),
    ((8, SLOT), F32),
)
FRONT_FETCHES = 3 + 2 * E * 2 + 2 * 2 + 1


def front_kernel(*refs):
    refs = list(refs)
    take = lambda count: [refs.pop(0) for _ in range(count)]
    (mem_len,) = take(1)
    gain, shift, value_route, out_route, bias_u, bias_v, value_router, out_router, coarse, fine = take(10)
    memory, tokens, cotangent, value_weight, key_weight, query_weight, rel_weight, out_weight = take(8)
    outs = take(len(FRONT_OUTS))
    kept = take(len(FRONT_OUTS))
    tok, cot, wide, out_wide, normed, experts, gates, keys, values, queries, attended, probs, heads_own, heads_peer, mixed, part, part_in, sinus, counts = kept
    send_sem, recv_sem, fetch_sem, out_sem = take(4)
    mem, routes, routes_in, turned, rel, full, pay, pay_in, back = take(9)
    links, fetches, writes = Links(send_sem, recv_sem), Fetches(fetch_sem), Fetches(out_sem)
    at = place()
    core, chip = at["core"], at["y"] // 2
    peer = moved(at, "y", 2)
    sibling = dict(at)
    sibling["core"] = 1 - core
    sibling = device_of(sibling)
    mine, theirs = pl.ds(0, BLOCK), pl.ds(BLOCK, BLOCK)
    row_loads = [
        fetches.start(memory, mem.at[mine]),
        fetches.start(tokens, tok.at[mine]),
        fetches.start(cotangent, cot.at[mine]),
    ]

    def slots_from(target, slot, source, start):
        src = source.at[pl.ds(pl.multiple_of(start, 16), DH)]
        return fetches.start(src, target.at[pl.ds(slot, DH)])

    wide_loads, out_loads = [], []
    for pair in range(2):
        head = 2 * pair + core
        for expert in range(E):
            slot = (pair * E + expert) * SLOT
            wide_loads.append(slots_from(wide, slot, value_weight, (head * E + expert) * DH))
        wide_loads.append(slots_from(wide, KEY_AT + pair * SLOT, key_weight, head * DH))
        wide_loads.append(slots_from(wide, QUERY_AT + pair * SLOT, query_weight, head * DH))
    rel_load = slots_from(rel, 0, rel_weight, (2 * chip + core) * DH)
    for pair in range(2):
        head = 2 * pair + core
        for expert in range(E):
            slot = (pair * E + expert) * SLOT
            out_loads.append(slots_from(out_wide, slot, out_weight, (head * E + expert) * DH))
    routes[:8, :] = value_route[:, 0, :]
    routes[8:16, :] = value_route[:, 1, :]
    for number in range(H):
        routes[16 + 2 * number : 18 + 2 * number, :] = out_route[number]
    greet([sibling, peer])
    pl.semaphore_wait(pltpu.get_barrier_semaphore(), 2)
    mem_copy = links.send(memory, mem.at[theirs], sibling)
    tok_copy = links.send(tokens, tok.at[theirs], sibling)
    route_copy = links.send(routes, routes_in, sibling)
    cot_copy = links.send(cotangent, cot.at[theirs], sibling)
    blank = jnp.zeros((SLOT - DH, D), BF16)
    for slot in range(DH, EXPERTS, SLOT):
        out_wide[slot : slot + SLOT - DH, :] = blank
    for slot in range(DH, ROUTER_AT, SLOT):
        wide[slot : slot + SLOT - DH, :] = blank
    rel[DH:, :] = blank
    routers = []
    for router in (value_router, out_router):
        for pair in range(2):
            one = router[2 * pair * E : (2 * pair + 1) * E, :].astype(F32)
            two = router[(2 * pair + 1) * E : (2 * pair + 2) * E, :].astype(F32)
            routers.append(jnp.where(core == 0, one, two))
    routers.append(jnp.zeros((SLOT - 4 * E, D), F32))
    wide[ROUTER_AT:, :] = jnp.concatenate(routers, axis=0).astype(BF16)
    lane = lax.broadcasted_iota(jnp.int32, (BLOCK, SLOT), 1)
    turned[0] = routes[...].astype(F32).T.astype(jnp.int32)
    slot_of = lax.broadcasted_iota(jnp.int32, (2 * H, SLOT), 1) - lax.broadcasted_iota(jnp.int32, (2 * H, SLOT), 0) // 2 * E
    counted = jnp.zeros((1, SLOT), F32)
    for first in (0, 8, 16):
        for expert in range(E):
            named = (routes[first : first + 2 * H, :] == expert).astype(F32)
            number = jnp.sum(named, axis=1, keepdims=True)
            at_slot = slot_of == expert + (H * E if first == 16 else 0)
            counted += jnp.sum(jnp.where(at_slot, number, 0.0), axis=0, keepdims=True)
    counts[...] = jnp.zeros_like(counts)
    counts[0:1, :] = counted
    wait_for(*row_loads[:2])

    def normalize(block):
        rows = slice(block * BLOCK, (block + 1) * BLOCK)
        given = (mem, tok)[block // 2][(block % 2) * BLOCK : (block % 2 + 1) * BLOCK, :]
        scaled, _ = centered(given.astype(F32))
        normed[rows, :] = (scaled * as_row(gain) + as_row(shift)).astype(BF16)

    moving = []

    def project(block, buffer):
        rows = slice(block * BLOCK, (block + 1) * BLOCK)
        space = full.at[buffer]
        space[...] = dot(normed[rows, :], wide[...], 1, 1)
        experts[rows, :] = space[:, :EXPERTS].astype(BF16)
        named = turned[block % 2]
        token = block // 2
        chosen = chosen_lanes(named, 2 * H * token, core, lane, 0) & (lane < 2 * E)
        if token:
            chosen = chosen | chosen_lanes(named, 4 * H, core, lane, 2 * E)
        gate = jnp.where(chosen, jax.nn.sigmoid(space[:, ROUTER_AT:WIDE]), 0.0)
        gates[rows, :] = gate
        for pair in range(2):
            total = jnp.zeros((BLOCK, SLOT), F32)
            for expert in range(E):
                slot = pair * E + expert
                total += gate[:, slot : slot + 1] * space[:, slot * SLOT : (slot + 1) * SLOT]
            pay[pair, block] = space[:, KEY_AT + pair * SLOT : KEY_AT + (pair + 1) * SLOT].astype(BF16)
            pay[pair, 4 + block] = total.astype(BF16)
            if token:
                pay[pair, 6 + block] = space[:, QUERY_AT + pair * SLOT : QUERY_AT + (pair + 1) * SLOT].astype(BF16)
        for segment in (block, 4 + block) + ((6 + block,) if token else ()):
            moving.append(links.send(pay.at[1 - chip, segment], pay_in.at[segment], peer))

    normalize(0)
    normalize(2)
    wait_for(*wide_loads)
    project(0, 0)
    project(2, 1)
    mem_copy.wait_recv()
    normalize(1)
    tok_copy.wait_recv()
    normalize(3)
    route_copy.wait_recv()
    turned[1] = routes_in[...].astype(F32).T.astype(jnp.int32)
    project(1, 0)
    project(3, 1)
    for number in (0, 2, 4, 5, 6):
        writes.start(kept[number], outs[number])
    sin_b, cos_b = fine[0], fine[1]
    for number in range(32):
        sin_a, cos_a = coarse[0, number : number + 1, :], coarse[1, number : number + 1, :]
        rows = slice(64 * number, 64 * (number + 1))
        sinus[rows, : D // 2] = (sin_a * cos_b + cos_a * sin_b).astype(BF16)
        sinus[rows, D // 2 :] = (cos_a * cos_b - sin_a * sin_b).astype(BF16)
    writes.start(kept[17], outs[17])
    writes.start(kept[18], outs[18])
    rel_load.wait()
    far_rel = queries.at[pl.ds(2 * LEN, 2 * LEN)]
    far_rel[...] = dot(sinus[...], rel[...], 1, 1).astype(BF16)
    places = spots_of(core, chip)
    head = 2 * chip + core

    def own_head(bias):
        row = bias[...].astype(F32).reshape(1, H * DH)
        total = jnp.zeros((1, DH), F32)
        for number in range(H):
            total += jnp.where(head == number, row[:, number * DH : (number + 1) * DH], 0.0)
        return jnp.concatenate([total, jnp.zeros((1, SLOT - DH), F32)], axis=1)

    head_u, head_v = own_head(bias_u), own_head(bias_v)
    qu, qv = queries.at[pl.ds(0, LEN)], queries.at[pl.ds(LEN, LEN)]

    def assemble(number, segment_of):
        side = number % 2
        start = places[number]
        keys[rows_at(start), :] = segment_of(side)
        keys[rows_at(start + LEN), :] = segment_of(2 + side)
        values[rows_at(start), :] = segment_of(4 + side)
        values[rows_at(start + LEN), :] = segment_of(6 + side)
        query = segment_of(8 + side).astype(F32)
        qu[rows_at(start), :] = (query + head_u).astype(BF16)
        qv[rows_at(start), :] = (query + head_v).astype(BF16)

    for number in range(2):
        assemble(number, lambda segment: pay[chip, segment])
    for copy in moving:
        copy.wait_recv()
    for number in range(2, 4):
        assemble(number, lambda segment: pay_in[segment])
    for number in (7, 8, 9):
        writes.start(kept[number], outs[number])
    shown = mem_len[0]
    for block in range(LEN // BLOCK):
        attend(block, shown, qu, qv, keys, values, far_rel, attended, probs)
    for side in range(2):
        heads_own[side] = attended[rows_at(places[side]), :].astype(BF16)
        back[side] = attended[rows_at(places[2 + side]), :].astype(BF16)
    returned = links.send(back, heads_peer, peer)
    for number in (10, 11, 12):
        writes.start(kept[number], outs[number])
    wait_for(*out_loads)
    writes.start(kept[3], outs[3])
    returned.wait_recv()
    writes.start(kept[13], outs[13])
    sent = []
    for side in range(2):
        heads = two_heads(chip, heads_own[side], heads_peer[side])
        rows = slice(side * BLOCK, (side + 1) * BLOCK)
        gate = gates[(2 + side) * BLOCK : (3 + side) * BLOCK, :]
        for slot in range(2 * E):
            weight = gate[:, 2 * E + slot : 2 * E + slot + 1]
            mixed[rows, slot * SLOT : (slot + 1) * SLOT] = (weight * heads[slot // E]).astype(BF16)
        part[rows, :] = dot(mixed[rows, :], out_wide[...]).astype(BF16)
        other = pl.ds((1 - side) * BLOCK, BLOCK)
        sent.append(links.send(part.at[pl.ds(side * BLOCK, BLOCK)], part_in.at[other], sibling))
    writes.start(kept[14], outs[14])
    writes.start(kept[15], outs[15])
    row_loads[2].wait()
    cot_copy.wait_recv()
    writes.start(kept[1], outs[1])
    for copy in sent:
        copy.wait_recv()
    writes.start(kept[16], outs[16])
    wait_for(*writes.copies)
    for copy in links.made:
        copy.wait_send()


def front(mem_len, small, large):
    copies = 4 + 10 + 1 + 2
    return pl.pallas_call(
        front_kernel,
        out_shape=[struct(*out) for out in FRONT_OUTS],
        in_specs=[IN_SMEM] + [IN_VMEM] * len(small) + [ANYWHERE] * len(large),
        out_specs=[ANYWHERE] * len(FRONT_OUTS),
        scratch_shapes=[pltpu.VMEM(*out) for out in FRONT_OUTS]
        + [
            pltpu.SemaphoreType.DMA((copies,)),
            pltpu.SemaphoreType.DMA((copies,)),
            pltpu.SemaphoreType.DMA((FRONT_FETCHES,)),
            pltpu.SemaphoreType.DMA((len(FRONT_OUTS),)),
            pltpu.VMEM((2 * BLOCK, D), BF16),
            pltpu.VMEM((6 * H, BLOCK), jnp.int32),
            pltpu.VMEM((6 * H, BLOCK), jnp.int32),
            pltpu.VMEM((2, BLOCK, 6 * H), jnp.int32),
            pltpu.VMEM((SLOT, D), BF16),
            pltpu.VMEM((2, BLOCK, WIDE), F32),
            pltpu.VMEM((2, 10, BLOCK, SLOT), BF16),
            pltpu.VMEM((10, BLOCK, SLOT), BF16),
            pltpu.VMEM((2, BLOCK, SLOT), BF16),
        ],
        compiler_params=pltpu.CompilerParams(
            collective_id=0, has_side_effects=True, vmem_limit_bytes=VMEM_BYTES
        ),
    )(mem_len, *small, *large)


ARRANGED = (
    ((BLOCK, D), BF16),
    ((BLOCK, D), F32),
    ((8,), F32),
    ((8,), F32),
    ((8, H * DH), F32),
    ((8, H * DH), F32),
    ((8, H * DH), F32),
    ((H * DH,), F32),
    ((H * DH,), F32),
    ((8, H * E), F32),
    ((8, H * E * DH), F32),
    ((8, H * E), F32),
    ((8, H * E * DH), F32),
    ((8,), F32),
    ((8,), F32),
    ((8, FF), F32),
    ((32,), F32),
    ((32, D), F32),
    ((8,), F32),
    ((2, H, E), jnp.int32),
)


def arrange_kernel(result_in, tokens_in, small, down_in, up, out, value, keys, rest, *outs):
    (
        result,
        grad_tokens,
        attn_gain,
        attn_bias,
        grad_query,
        grad_key,
        grad_rel,
        grad_bias_u,
        grad_bias_v,
        value_router,
        grad_value,
        out_router,
        grad_out,
        ffn_gain,
        ffn_bias,
        grad_up,
        up_bias,
        grad_down,
        down_bias,
        counts,
    ) = outs
    result[...] = result_in[...]
    grad_tokens[...] = tokens_in[...]
    grad_down[...] = down_in[...]
    grad_up[:, : FF // 2] = up[0]
    grad_up[:, FF // 2 :] = up[1]
    for head in range(H):
        core, pair = head % 2, head // 2
        for expert in range(E):
            slot = (pair * E + expert) * SLOT
            start = (head * E + expert) * DH
            grad_out[:, start : start + DH] = out[core, :, slot : slot + DH]
            grad_value[:, start : start + DH] = value[core, :, slot : slot + DH]
        start = head * DH
        for target, source, slot in ((grad_key, keys, 0), (grad_query, keys, 2 * SLOT), (grad_rel, rest, 0)):
            slot += pair * SLOT
            target[:, start : start + DH] = source[core, :, slot : slot + DH]
        for kind, target in enumerate((value_router, out_router)):
            at = 2 * SLOT + (2 * kind + pair) * E
            target[:, head * E : (head + 1) * E] = rest[core, :, at : at + E]
    device = lax.axis_index("dp") * 4 + lax.axis_index("seq")

    def share(target, first, size):
        per_row = SLOT // size
        row = small[pl.ds(first + device // per_row, 1), :]
        row = pltpu.roll(row, SLOT - device % per_row * size, 1)
        target[...] = row[:, :size].reshape(size)

    for number, target in enumerate((attn_gain, attn_bias, ffn_gain, ffn_bias, down_bias)):
        share(target, VECTOR_ROW + 8 * number, 8)
    share(up_bias, UP_BIAS_ROW, 32)
    for first, target in ((0, grad_bias_u), (H, grad_bias_v)):
        heads = [small[first + head : first + head + 1, :DH] for head in range(H)]
        target[...] = jnp.concatenate(heads, axis=1).reshape(H * DH)
    row = (small[COUNT_ROW : COUNT_ROW + 1, :] + 0.5).astype(jnp.int32)
    for kind in range(2):
        for head in range(H):
            at = (kind * H + head) * E
            counts[kind, head : head + 1, :] = row[:, at : at + E]


def arrange(*operands):
    return local_call(arrange_kernel, [struct(*out) for out in ARRANGED], vmem=len(operands))(*operands)


def angle_tables():
    frequency = jnp.exp(jnp.arange(D // 2, dtype=jnp.int32).astype(F32) * (-2.0 * math.log(10000.0) / D))
    coarse = (64 * (31 - jnp.arange(32, dtype=jnp.int32))).astype(F32)[:, None] * frequency
    fine = (63 - jnp.arange(64, dtype=jnp.int32)).astype(F32)[:, None] * frequency
    return jnp.stack([jnp.sin(coarse), jnp.cos(coarse)]), jnp.stack([jnp.sin(fine), jnp.cos(fine)])


def body(
    tokens,
    memory,
    cotangent,
    mem_len,
    value_route,
    output_route,
    attn_norm_gain,
    attn_norm_bias,
    query_weight,
    key_weight,
    rel_weight,
    bias_u,
    bias_v,
    value_router,
    value_weight,
    out_router,
    out_weight,
    ffn_norm_gain,
    ffn_norm_bias,
    up_weight,
    up_bias,
    down_weight,
    down_bias,
):
    tokens, memory, cotangent = tokens[0], memory[0], cotangent[0]
    coarse, fine = angle_tables()
    (
        tokens_pair,
        cot,
        wide,
        out_wide,
        normed,
        experts,
        gates,
        keys,
        values,
        queries,
        attended,
        probs,
        heads_own,
        heads_peer,
        mixed,
        out_part,
        out_part_in,
        sinus,
        counts,
    ) = front(
        mem_len,
        [
            attn_norm_gain,
            attn_norm_bias,
            value_route[0].transpose(2, 3, 0, 1).reshape(2 * H, 2, BLOCK),
            output_route[0].transpose(1, 2, 0),
            bias_u,
            bias_v,
            value_router.T,
            out_router.T,
            coarse,
            fine,
        ],
        [memory, tokens, cotangent, value_weight.T, key_weight.T, query_weight.T, rel_weight.T, out_weight],
    )
    final_mine, final_theirs, norm_part, grad_up_bias, *first, resid, hidden, grad_up = feed(
        tokens_pair,
        out_part,
        out_part_in,
        cot,
        ffn_norm_gain,
        ffn_norm_bias,
        up_bias,
        down_bias,
        up_weight,
        down_weight,
    )
    pay, pay_in, bias_sums, grad_far, grad_resid, result, grad_logit, feed_sums, *early = back(
        norm_part,
        final_theirs,
        ffn_norm_gain,
        [
            grad_up,
            hidden,
            cot,
            resid,
            out_wide,
            gates,
            heads_own,
            heads_peer,
            mixed,
            probs,
            attended,
            values,
            keys,
            queries,
            normed,
            final_mine,
        ],
    )
    *early, grad_experts, grad_value = first + early
    grad_tokens, small_sum, grad_down, up_both, out_both, value_both, keys_both, rest_both = close(
        attn_norm_gain,
        feed_sums,
        grad_up_bias,
        bias_sums,
        counts,
        pay,
        pay_in,
        grad_logit,
        grad_far,
        early,
        [grad_value, normed, experts, gates, wide, grad_experts, sinus, memory, tokens, grad_resid],
    )
    outs = arrange(
        result, grad_tokens, small_sum, grad_down, up_both, out_both, value_both, keys_both, rest_both
    )
    outs = list(outs)
    outs[0], outs[1], outs[12] = outs[0][None], outs[1][None], outs[12].T
    return tuple(outs)


def solution(mesh):
    in_specs = (
        P("dp", "seq", None),
        P("dp", "seq", None),
        P("dp", "seq", None),
        P("dp"),
        P("dp", None, "seq", None, None),
        P("dp", "seq", None, None),
        P(),
        P(),
        P(),
        P(),
        P(),
        P(),
        P(),
        P(),
        P(),
        P(),
        P(),
        P(),
        P(),
        P(),
        P(),
        P(),
        P(),
    )
    out_specs = (
        P("dp", "seq", None),
        P("dp", "seq", None),
        P(("dp", "seq")),
        P(("dp", "seq")),
        P(("dp", "seq"), None),
        P(("dp", "seq"), None),
        P(("dp", "seq"), None),
        P(),
        P(),
        P(("dp", "seq"), None),
        P(("dp", "seq"), None),
        P(("dp", "seq"), None),
        P(None, ("dp", "seq")),
        P(("dp", "seq")),
        P(("dp", "seq")),
        P(("dp", "seq"), None),
        P(("dp", "seq")),
        P(("dp", "seq"), None),
        P(("dp", "seq")),
        P(),
    )
    return jax.shard_map(body, mesh=mesh, in_specs=in_specs, out_specs=out_specs, check_vma=False)
```

```python
from functools import partial
import math

import jax
import jax.numpy as jnp
from jax import lax
from jax.experimental import pallas as pl
from jax.experimental.pallas import tpu as pltpu
from jax.sharding import PartitionSpec as P

D = 1024
H = 4
DH = 112
E = 5
FF = 4096
LEN = 1024
SLOT = 128
BLOCK = 256
EXPERTS = 2 * E * SLOT
KEY_AT = EXPERTS
QUERY_AT = KEY_AT + 2 * SLOT
ROUTER_AT = QUERY_AT + 2 * SLOT
WIDE = ROUTER_AT + SLOT
SCALE = DH ** (-0.5)
MASKED = -1e30
EPS = 1e-05
BF16 = jnp.bfloat16
F32 = jnp.float32
VMEM_BYTES = 60 * 1024 * 1024
IN_VMEM = pl.BlockSpec(memory_space=pltpu.VMEM)
IN_SMEM = pl.BlockSpec(memory_space=pltpu.SMEM)
ANYWHERE = pl.BlockSpec(memory_space=pl.ANY)
MESH = pl.DeviceIdType.MESH


def dot(left, right, left_dim=1, right_dim=0):
    return lax.dot_general(
        left, right, (((left_dim,), (right_dim,)), ((), ())), preferred_element_type=F32
    )


def struct(shape, kind=BF16):
    return jax.ShapeDtypeStruct(shape, kind)


def local_call(kernel, out_shape, scratch_shapes=(), smem=0, vmem=0, **kw):
    return pl.pallas_call(
        kernel,
        out_shape=out_shape,
        in_specs=[IN_SMEM] * smem + [IN_VMEM] * vmem,
        out_specs=[IN_VMEM] * len(out_shape),
        scratch_shapes=scratch_shapes,
        compiler_params=pltpu.CompilerParams(vmem_limit_bytes=VMEM_BYTES),
        **kw,
    )


def centered(rows):
    center = rows - jnp.mean(rows, axis=1, keepdims=True)
    inverse = lax.rsqrt(jnp.mean(center * center, axis=1, keepdims=True) + EPS)
    return center * inverse, inverse


def norm_back(grad, scaled, inverse, gain):
    through = grad * gain
    return inverse * (
        through
        - jnp.mean(through, axis=1, keepdims=True)
        - scaled * jnp.mean(through * scaled, axis=1, keepdims=True)
    )


def as_row(vector):
    return vector[...].astype(F32).reshape(1, vector.shape[0])


def chosen_lanes(route, first, core, lane, start):
    chosen = None
    for pair in range(2):
        for number in range(2):
            column = first + 4 * pair + number
            one = jnp.where(core == 0, route[:, column : column + 1], route[:, column + 2 : column + 3])
            hit = lane == one + (start + E * pair)
            chosen = hit if chosen is None else chosen | hit
    return chosen


def spots_of(core, chip):
    return [
        chip * 512 + core * BLOCK,
        chip * 512 + (1 - core) * BLOCK,
        (1 - chip) * 512 + core * BLOCK,
        (1 - chip) * 512 + (1 - core) * BLOCK,
    ]


def rows_at(start):
    return pl.ds(pl.multiple_of(start, BLOCK), BLOCK)


def attend(block, mem_mask, own_mask, qu, qv, keys, values, far_rel, attended, probs):
    rows = pl.ds(block * BLOCK, BLOCK)
    width = LEN + (block + 1) * BLOCK
    first_far = 2 * LEN - width
    content = dot(qu[rows, :], keys[:width, :], 1, 1)
    far = dot(qv[rows, :], far_rel[first_far:, :], 1, 1)
    raw = content + pltpu.roll(far, width - BLOCK + 1, 1, stride=1, stride_axis=0)
    parts = [raw[:, :LEN] + mem_mask]
    if block > 0:
        parts.append(raw[:, LEN : width - BLOCK])
    parts.append(raw[:, width - BLOCK :] + own_mask)
    highest = parts[0].max(axis=1, keepdims=True)
    for part in parts[1:]:
        highest = jnp.maximum(highest, part.max(axis=1, keepdims=True))
    parts = [jnp.exp2((part - highest) * (SCALE * math.log2(math.e))) for part in parts]
    total = parts[0].sum(axis=1, keepdims=True)
    for part in parts[1:]:
        total += part.sum(axis=1, keepdims=True)
    share = 1.0 / total
    start = 0
    for part in parts:
        size = part.shape[1]
        probs[rows, start : start + size] = (part * share).astype(BF16)
        start += size
    attended[rows, :] = dot(probs[rows, :width], values[:width, :], 1, 0)


def two_heads(chip, own, peer):
    first = jnp.where(chip == 0, own.astype(F32), peer.astype(F32))
    second = jnp.where(chip == 0, peer.astype(F32), own.astype(F32))
    return first, second


def place():
    dp = lax.axis_index("dp")
    sq = lax.axis_index("seq")
    return dict(x=dp // 8, z=(dp // 2) % 4, y=(sq // 2) * 2 + dp % 2, core=sq % 2)


def device_of(at):
    return (at["x"] * 8 + at["z"] * 2 + at["y"] % 2, (at["y"] // 2) * 2 + at["core"])


def moved(at, axis, steps):
    other = dict(at)
    other[axis] = (at[axis] + steps) % 4
    return device_of(other)


PLAIN = (("x", 4), ("z", 4), ("ylo", 2), ("yhi", 2))
SPLIT = (("xhi", 2), ("z", 4), ("ylo", 2), ("yhi", 2), ("xlo", 2))


def part_of(name, where):
    return {"hi": where // 2, "lo": where % 2}.get(name[1:], where)


def chunk_of(ref, dims, axis, where):
    return ref.at[tuple(part_of(name, where) if name[0] == axis else slice(None) for name, _ in dims)]


def without(dims, axes):
    return tuple(dim for dim in dims if dim[0][0] not in axes)


def lead_shape(dims):
    return tuple(size for _, size in dims)


def halves(width):
    one = (width // 2 + 127) // 128 * 128
    return (0, one), (one, width - one)


def each_block(lead, size, step):
    if math.prod(lead) * size <= 64 * 1024:
        step(Ellipsis)
        return

    def run(number, carry):
        step(number)
        return carry

    lax.fori_loop(0, lead[0], run, 0)


class Links:
    def __init__(self, send_sem, recv_sem):
        self.send_sem, self.recv_sem, self.made, self.open = send_sem, recv_sem, [], {}

    def prepared(self, src, dst, device):
        slot = len(self.made)
        copy = pltpu.make_async_remote_copy(
            src_ref=src,
            dst_ref=dst,
            send_sem=self.send_sem.at[slot],
            recv_sem=self.recv_sem.at[slot],
            device_id=device,
            device_id_type=MESH,
        )
        self.made.append(copy)
        self.open[id(copy)] = copy
        return copy

    def settle(self, copies=None):
        for copy in list(self.open.values()) if copies is None else copies:
            copy.wait_send()
            del self.open[id(copy)]

    def send(self, src, dst, device):
        copy = self.prepared(src, dst, device)
        copy.start()
        return copy


def added(target, *terms):
    def add(index):
        total = terms[0][index].astype(F32)
        for term in terms[1:]:
            total += term[index].astype(F32)
        target[index] = total.astype(target.dtype)

    return add


class Stage:
    def __init__(self, links, at, ref, dims, axis, width, bufs, after):
        self.links, self.bufs, self.after = links, bufs, after
        self.left = lead_shape(without(dims, axis))
        self.cols = [pl.ds(*half) for half in halves(width)]
        self.sizes = [half[1] * bufs[0].shape[-2] for half in halves(width)]
        self.near = [chunk_of(ref, dims, axis, (at[axis] + steps) % 4) for steps in range(4)]
        self.ahead = [self.near[steps].at[..., self.cols[side]] for side, steps in ((0, 1), (1, 3))]
        self.far, self.close, self.summed = [], [], []
        for side, steps in ((0, 1), (1, 3)):
            device = moved(at, axis, steps)
            other = self.cols[1 - side]
            self.far.append(links.prepared(self.near[2].at[..., self.cols[side]], bufs[side], device))
            self.close.append(links.prepared(self.near[steps].at[..., other], bufs[2 + side], device))
            self.summed.append(links.prepared(bufs[side], bufs[4 + side], device))

    def launch_far(self):
        for copy in self.far:
            copy.start()

    def launch_near(self):
        for copy in self.close:
            copy.start()

    def forward(self):
        for side in range(2):
            self.far[side].wait_recv()
            each_block(self.left, self.sizes[side], added(self.bufs[side], self.bufs[side], self.ahead[side]))
            self.summed[side].start()

    def collect(self):
        for copy in self.close + self.summed:
            copy.wait_recv()
        for side in (0, 1):
            cols = self.cols[side]
            terms = self.near[0].at[..., cols], self.bufs[4 + side], self.bufs[3 - side]
            each_block(self.left, self.sizes[side], added(self.after.at[..., cols], *terms))

    def settle(self):
        self.links.settle(self.far + self.close + self.summed)


class DirectStage:
    def __init__(self, links, at, ref, dims, axis, width, bufs, after):
        self.bufs, self.after = bufs, after
        self.left = lead_shape(without(dims, axis))
        self.size = width * bufs[0].shape[-2]
        self.near = [chunk_of(ref, dims, axis, (at[axis] + steps) % 4) for steps in range(4)]
        self.copies = [
            links.prepared(self.near[steps], bufs[steps - 1], moved(at, axis, steps)) for steps in (1, 2, 3)
        ]

    def launch_far(self):
        for copy in self.copies:
            copy.start()

    def launch_near(self):
        pass

    def forward(self):
        pass

    def collect(self):
        for copy in self.copies:
            copy.wait_recv()
        each_block(self.left, self.size, added(self.after, self.near[0], *self.bufs))


def direct_scratch(dims, axis, rows, width):
    return [pltpu.VMEM(lead_shape(without(dims, axis)) + (rows, width), BF16)] * 3


def stage_scratch(dims, axis, rows, width):
    left = lead_shape(without(dims, axis))
    (_, one), (_, two) = halves(width)
    return [pltpu.VMEM(left + (rows, size), BF16) for size in (one, two, two, one, one, two)]


def launch(stages):
    for stage in stages:
        stage.launch_far()
    for stage in stages:
        stage.launch_near()


def greet(devices):
    barrier = pltpu.get_barrier_semaphore()
    for device in devices:
        pl.semaphore_signal(barrier, inc=1, device_id=device, device_id_type=MESH)


UP, DOWN, OUT, VALUE, KEYS, REST = range(6)
LAYOUTS = (PLAIN, SPLIT, PLAIN, PLAIN, PLAIN, PLAIN)
SHAPES = ((16, FF // 2), (32, D), (16, EXPERTS), (16, EXPERTS), (16, 4 * SLOT), (16, 3 * SLOT))
UP_FIRST = ((UP, 0, 256, "xyz"), (UP, 256, 256, "zxy"), (UP, 512, 256, "yzx"))
UP_PIECES = ((UP, 768, 512, "xyz"), (UP, 1280, 512, "zxy"), (UP, 1792, 256, "yzx"))
DOWN_PIECES = ((DOWN, 0, 512, "xyz"), (DOWN, 512, 512, "zxy"))
OUT_PIECES = ((OUT, 0, 512, "xzy"), (OUT, 512, 512, "zyx"), (OUT, 1024, 256, "yzx"))
VALUE_PIECES = ((VALUE, 0, 512, "xyz"), (VALUE, 512, 512, "zxy"), (VALUE, 1024, 256, "yzx"))
KEYS_PIECES = ((KEYS, 0, 256, "xyz"), (KEYS, 256, 256, "zxy"))
REST_PIECES = ((REST, 0, 384, "yzx"),)
BACK_PIECES = UP_PIECES + DOWN_PIECES + OUT_PIECES
EARLY = UP_FIRST + BACK_PIECES
LATE = VALUE_PIECES + KEYS_PIECES + REST_PIECES


def dims_after(piece, phases):
    return without(LAYOUTS[piece[0]], piece[3][:phases])


def after_shape(piece, phases):
    return lead_shape(dims_after(piece, phases)) + (SHAPES[piece[0]][0], piece[2])


def is_direct(piece, phase):
    return phase == 2 or phase == 1 and piece in LATE


def phase_scratch(piece, phase):
    made = direct_scratch if is_direct(piece, phase) else stage_scratch
    return made(dims_after(piece, phase), piece[3][phase], SHAPES[piece[0]][0], piece[2])


def copies_of(piece, phase):
    return 3 if is_direct(piece, phase) else 6


def stage_for(links, at, piece, phase, ref, take, after):
    made = DirectStage if is_direct(piece, phase) else Stage
    bufs = take(3 if is_direct(piece, phase) else 6)
    return made(links, at, ref, dims_after(piece, phase), piece[3][phase], piece[2], bufs, after)


def full_shape(array):
    return lead_shape(LAYOUTS[array]) + SHAPES[array]


def columns_of(ref, piece):
    return ref.at[..., pl.ds(piece[1], piece[2])]


class Fetches:
    def __init__(self, sems):
        self.sems, self.copies = sems, []

    def start(self, src, dst):
        copy = pltpu.make_async_copy(src, dst, self.sems.at[len(self.copies)])
        copy.start()
        self.copies.append(copy)
        return copy


def wait_for(*copies):
    for copy in copies:
        copy.wait()


def forward(stages):
    for stage in stages:
        stage.forward()


def collect(stages):
    for stage in stages:
        stage.collect()


def others_of(at):
    sibling = dict(at)
    sibling["core"] = 1 - at["core"]
    return device_of(sibling), moved(at, "y", 2)


STEP = 256
STEPS = FF // 2 // STEP


def feed_kernel(*refs):
    refs = list(refs)
    take = lambda count: [refs.pop(0) for _ in range(count)]
    rows, part_mine, part_theirs, cot, gain, shift, up_bias, down_bias = take(8)
    up_given, down_given = take(2)
    final_mine, final_theirs, grad_part, grad_up_bias = take(4)
    afters = take(len(UP_FIRST))
    outs = take(3)
    resid, hidden, grad_up, write_sem = take(4)
    send_sem, recv_sem, fetch_sem, up, down, low, low_turned, grad_all, bias_row = take(9)
    before_a, before_b, above_a, above_b = take(4)
    fetches, writes = Fetches(fetch_sem), Fetches(write_sem)
    links = Links(send_sem, recv_sem)
    at = place()
    first = at["core"] * (FF // 2)

    def own(step):
        return pl.ds(step * STEP, STEP)

    for step in range(STEPS):
        there = pl.ds(pl.multiple_of(first + step * STEP, STEP), STEP)
        fetches.start(up_given.at[:, there], up.at[:, own(step)])
        fetches.start(down_given.at[there, :], down.at[own(step), :])
    devices = [moved(at, axis, steps) for axis in "xyz" for steps in (1, 3)]
    greet(devices)
    for side in range(2):
        here = slice(side * BLOCK, (side + 1) * BLOCK)
        total = rows[here, :].astype(F32) + (part_mine[here, :].astype(F32) + part_theirs[here, :].astype(F32))
        resid[here, :] = total
        scaled, _ = centered(total)
        low[here, :] = (scaled * as_row(gain) + as_row(shift)).astype(BF16)
    writes.start(resid, outs[0])
    low_turned[...] = low[...].T
    bias_row[...] = as_row(up_bias)

    def ahead(step, before, above):
        bias = bias_row[:, pl.ds(pl.multiple_of(first + step * STEP, STEP), STEP)]
        before[...] = dot(low[...], up[:, own(step)]) + bias
        above[...] = dot(cot[...], down[own(step), :], 1, 1)

    def weigh(step):
        block = dot(low_turned[...], grad_all[:, own(step)]).astype(BF16)
        grad_up[..., own(step)] = block.reshape(lead_shape(PLAIN) + (16, STEP))

    def activate(step, before, above):
        value = before[...]
        below = 0.5 * (1.0 + lax.erf(value * (0.5**0.5)))
        hidden[:, own(step)] = (value * below).astype(BF16)
        slope = below + value * (jnp.exp(-0.5 * value * value) * ((2.0 * math.pi) ** -0.5))
        grad_low = (above[...] * slope).astype(BF16)
        grad_all[:, own(step)] = grad_low
        grad_up_bias[:, own(step)] = jnp.sum(grad_low.astype(F32), axis=0, keepdims=True)

    stages = []
    for piece, after in zip(UP_FIRST, afters):
        stages.append(stage_for(links, at, piece, 0, columns_of(grad_up, piece), take, after))
    pairs = (before_a, above_a), (before_b, above_b)
    wait_for(*fetches.copies[:2])
    ahead(0, *pairs[0])
    for step in range(STEPS):
        if step + 1 < STEPS:
            wait_for(*fetches.copies[2 * step + 2 : 2 * step + 4])
            ahead(step + 1, *pairs[(step + 1) % 2])
        activate(step, *pairs[step % 2])
        if step > 0:
            weigh(step - 1)
        if step == 1:
            pl.semaphore_wait(pltpu.get_barrier_semaphore(), len(devices))
        if 1 <= step <= len(stages):
            launch(stages[step - 1 : step])
        if 4 <= step < 4 + len(stages):
            forward(stages[step - 4 : step - 3])
    weigh(STEPS - 1)
    writes.start(hidden, outs[1])
    writes.start(grad_up, outs[2])
    grad_part[...] = dot(grad_all[...], up[...], 1, 1).astype(BF16)
    final_mine[...] = resid[:BLOCK, :] + dot(hidden[:BLOCK, :], down[...]) + as_row(down_bias)
    final_theirs[...] = dot(hidden[BLOCK:, :], down[...]).astype(BF16)
    collect(stages)
    wait_for(*writes.copies)
    links.settle()


def feed(rows, part_mine, part_theirs, cot, gain, shift, up_bias, down_bias, up, down):
    pair = (2 * BLOCK, D)
    outs = [struct((BLOCK, D), F32), struct((BLOCK, D)), struct(pair), struct((1, FF // 2), F32)]
    outs += [struct(after_shape(piece, 1)) for piece in UP_FIRST]
    scratch = []
    for piece in UP_FIRST:
        scratch += phase_scratch(piece, 0)
    written = [struct(pair, F32), struct((2 * BLOCK, FF // 2)), struct(full_shape(UP))]
    return pl.pallas_call(
        feed_kernel,
        out_shape=outs + written,
        in_specs=[IN_VMEM] * 8 + [ANYWHERE] * 2,
        out_specs=[IN_VMEM] * len(outs) + [ANYWHERE] * len(written),
        scratch_shapes=[pltpu.VMEM(out.shape, out.dtype) for out in written]
        + [
            pltpu.SemaphoreType.DMA((len(written),)),
            pltpu.SemaphoreType.DMA((6 * len(UP_FIRST),)),
            pltpu.SemaphoreType.DMA((6 * len(UP_FIRST),)),
            pltpu.SemaphoreType.DMA((2 * STEPS,)),
            pltpu.VMEM((D, FF // 2), BF16),
            pltpu.VMEM((FF // 2, D), BF16),
            pltpu.VMEM(pair, BF16),
            pltpu.VMEM((D, 2 * BLOCK), BF16),
            pltpu.VMEM((2 * BLOCK, FF // 2), BF16),
            pltpu.VMEM((1, FF), F32),
        ]
        + [pltpu.VMEM((2 * BLOCK, STEP), F32)] * 4
        + scratch,
        compiler_params=pltpu.CompilerParams(
            collective_id=3, has_side_effects=True, vmem_limit_bytes=VMEM_BYTES
        ),
    )(rows, part_mine, part_theirs, cot, gain, shift, up_bias, down_bias, up, down)


KEY_BLOCKS = 2 * LEN // BLOCK


def rows_seeing(block):
    return pl.ds(max(0, block - 4) * BLOCK, LEN - max(0, block - 4) * BLOCK)


def back_kernel(*refs):
    refs = list(refs)
    take = lambda count: [refs.pop(0) for _ in range(count)]
    grad_part, final_theirs, gain = take(3)
    far_away = take(16)
    pay, pay_in, sums, grad_far, grad_resid, result, grad_logit, feed_sums = take(8)
    afters = take(len(BACK_PIECES))
    written = take(2)
    send_sem, recv_sem, fetch_sem, write_sem = take(4)
    writes = Fetches(write_sem)
    local = take(16)
    grads = {UP: local[0]}
    hidden, cot, resid, out_wide, gates, heads_own, heads_peer, mixed, probs, attended, values, keys, queries, normed, final_mine = local[1:]
    qu, qv, far_rel = (queries.at[pl.ds(start, size)] for start, size in ((0, LEN), (LEN, LEN), (2 * LEN, 2 * LEN)))
    part_in, final_in, given, given_in, grad_low, grad_mixed = take(6)
    grad_out, grad_u, grad_query, grad_keys, grad_values, far_sum, grad_experts = take(7)
    grads.update(zip((DOWN, OUT), take(2)))
    grads[VALUE] = grads[UP].at[..., pl.ds(0, EXPERTS)]
    links, fetches = Links(send_sem, recv_sem), Fetches(fetch_sem)
    loads = [fetches.start(src, dst) for src, dst in zip(far_away, local)]
    up_load = loads.pop(0)
    at = place()
    core, chip = at["core"], at["y"] // 2
    sibling, peer = others_of(at)
    devices = [moved(at, axis, steps) for axis in "xyz" for steps in (1, 2, 3)] + [sibling]
    greet(devices)
    pl.semaphore_wait(pltpu.get_barrier_semaphore(), len(devices))
    parts = [
        links.send(grad_part.at[pl.ds((1 - side) * BLOCK, BLOCK)], part_in.at[pl.ds(side * BLOCK, BLOCK)], sibling)
        for side in range(2)
    ]
    final_copy = links.send(final_theirs, final_in, sibling)

    unused = list(afters)

    def go(pieces):
        stages = []
        for piece in pieces:
            source = columns_of(grads[piece[0]], piece)
            stages.append(stage_for(links, at, piece, 0, source, take, unused.pop(0)))
        launch(stages)
        return stages

    up_load.wait()
    up_stages = go(UP_PIECES)

    def fill(array, left, right, start, width):
        block = dot(left[...], right[:, start : start + width], 0, 0).astype(BF16)
        grads[array][..., pl.ds(start, width)] = block.reshape(lead_shape(LAYOUTS[array]) + (SHAPES[array][0], width))

    wait_for(*loads[:2])
    down_stages = []
    for piece in DOWN_PIECES:
        fill(DOWN, hidden, cot, piece[1], piece[2])
        if piece[3][0] != "y":
            down_stages += go([piece])
    loads[2].wait()
    for copy in parts:
        copy.wait_recv()
    for side in range(2):
        here = slice(side * BLOCK, (side + 1) * BLOCK)
        scaled, inverse = centered(resid[here, :])
        grad = grad_part[here, :].astype(F32) + part_in[here, :].astype(F32)
        above = cot[here, :].astype(F32)
        total = above + norm_back(grad, scaled, inverse, as_row(gain))
        grad_low[here, :] = total.astype(BF16)
        if side == 0:
            grad_resid[...] = total
            feed_sums[0:1, :] = jnp.sum(grad * scaled, axis=0, keepdims=True)
            feed_sums[1:2, :] = jnp.sum(grad, axis=0, keepdims=True)
            feed_sums[2:3, :] = jnp.sum(above, axis=0, keepdims=True)
    wait_for(*loads[3:5])
    grad_mixed[...] = dot(grad_low[...], out_wide[...], 1, 1)
    for side in range(2):
        here = slice(side * BLOCK, (side + 1) * BLOCK)
        gate = gates[(2 + side) * BLOCK : (3 + side) * BLOCK, :]
        totals = []
        for pair in range(2):
            total = jnp.zeros((BLOCK, SLOT), F32)
            for expert in range(E):
                slot = pair * E + expert
                weight = gate[:, 2 * E + slot : 2 * E + slot + 1]
                total += weight * grad_mixed[here, slot * SLOT : (slot + 1) * SLOT]
            totals.append(total)
        given[0, side] = jnp.where(chip == 0, totals[0], totals[1]).astype(BF16)
        given[1, side] = jnp.where(chip == 0, totals[1], totals[0]).astype(BF16)
    arrived = links.send(given.at[1], given_in, peer)
    down_stages += go(DOWN_PIECES[2:])
    forward(up_stages)
    wait_for(*loads[5:8])
    out_stages = []
    for piece in OUT_PIECES:
        fill(OUT, grad_low, mixed, piece[1], piece[2])
        out_stages += go([piece])
    places = spots_of(core, chip)
    for side in range(2):
        grad_out[rows_at(places[side]), :] = given[0, side]
    wait_for(*loads[8:10])
    arrived.wait_recv()
    for side in range(2):
        grad_out[rows_at(places[2 + side]), :] = given_in[side]
    moving = []

    def give(first, held, base):
        for side in range(2):
            pay[first + side] = held[rows_at(places[side] + base), :]
            src = held.at[rows_at(places[2 + side] + base)]
            moving.append(links.send(src, pay_in.at[first + side], peer))

    for block in range(KEY_BLOCKS):
        cols, rows = pl.ds(block * BLOCK, BLOCK), rows_seeing(block)
        grad_values[cols, :] = dot(probs[rows, cols], grad_out[rows, :], 0, 0).astype(BF16)
    give(4, grad_values, 0)
    give(6, grad_values, LEN)
    value_moves = list(moving)
    lane = lax.broadcasted_iota(jnp.int32, (BLOCK, SLOT), 1)
    for side in range(2):
        here = slice(side * BLOCK, (side + 1) * BLOCK)
        gate = gates[(2 + side) * BLOCK : (3 + side) * BLOCK, :]
        heads = two_heads(chip, heads_own[side], heads_peer[side])
        total = jnp.zeros((BLOCK, SLOT), F32)
        for slot in range(2 * E):
            part = grad_mixed[here, slot * SLOT : (slot + 1) * SLOT] * heads[slot // E]
            total += jnp.where(lane == 2 * E + slot, jnp.sum(part, axis=1, keepdims=True), 0.0)
        grad_logit[here, :] = (total * gate * (1.0 - gate)).astype(BF16)
    forward(down_stages)
    wait_for(*loads[10:13])
    blocks = LEN // BLOCK
    sum_u = jnp.zeros((1, SLOT), F32)

    def score_rows(block):
        rows = pl.ds(block * BLOCK, BLOCK)
        width = LEN + (block + 1) * BLOCK
        above = grad_out[rows, :]
        grad_probs = dot(above, values[:width, :], 1, 1)
        inner = jnp.sum(above.astype(F32) * attended[rows, :], axis=1, keepdims=True)
        scores = (probs[rows, :width].astype(F32) * ((grad_probs - inner) * SCALE)).astype(BF16)
        probs[rows, :width] = scores
        part = dot(scores, keys[:width, :])
        grad_u[rows, :] = part
        return jnp.sum(part, axis=0, keepdims=True)

    for block in (0, 1):
        sum_u += score_rows(block)
    forward(out_stages)
    for block in (2, 3):
        sum_u += score_rows(block)
    for block in range(KEY_BLOCKS):
        cols, rows = pl.ds(block * BLOCK, BLOCK), rows_seeing(block)
        grad_keys[cols, :] = dot(probs[rows, cols], qu[rows, :], 0, 0).astype(BF16)
    give(0, grad_keys, 0)
    give(2, grad_keys, LEN)
    far_sum[...] = jnp.zeros_like(far_sum)
    down = lax.broadcasted_iota(jnp.int32, (BLOCK, BLOCK), 0)
    across = lax.broadcasted_iota(jnp.int32, (BLOCK, BLOCK), 1)
    flip = (down + across == BLOCK - 1).astype(F32).astype(BF16)
    sum_v = jnp.zeros((1, SLOT), F32)
    for block in range(blocks):
        rows = pl.ds(block * BLOCK, BLOCK)
        width = LEN + (block + 1) * BLOCK
        first_far = 2 * LEN - width
        far = pltpu.roll(dot(flip, probs[rows, :width]), 0, 1, stride=1, stride_axis=0).astype(BF16)
        turned = dot(flip, far).astype(BF16)
        part = dot(turned, far_rel[first_far:, :])
        far_sum[first_far:, :] += dot(turned, qv[rows, :], 0, 0)
        grad_query[rows, :] = (grad_u[rows, :] + part).astype(BF16)
        sum_v += jnp.sum(part, axis=0, keepdims=True)
    give(8, grad_query, 0)
    sums[0:1, :] = sum_u
    sums[1:2, :] = sum_v
    grad_far[...] = far_sum[...].astype(BF16)
    for copy in value_moves:
        copy.wait_recv()
    for block in range(4):
        rows = slice(block * BLOCK, (block + 1) * BLOCK)
        heads = two_heads(chip, pay[4 + block], pay_in[4 + block])
        for slot in range(2 * E):
            weight = gates[rows, slot : slot + 1]
            grad_experts[rows, slot * SLOT : (slot + 1) * SLOT] = (weight * heads[slot // E]).astype(BF16)
    writes.start(grad_experts, written[0])
    loads[13].wait()
    collect(up_stages)
    for stage in up_stages:
        stage.settle()
    for piece in VALUE_PIECES:
        fill(VALUE, normed, grad_experts, piece[1], piece[2])
    writes.start(grads[VALUE], written[1])
    loads[14].wait()
    final_copy.wait_recv()
    result[...] = (final_mine[...] + final_in[...].astype(F32)).astype(BF16)
    collect(down_stages)
    collect(out_stages)
    for copy in moving[4:]:
        copy.wait_recv()
    wait_for(*writes.copies)
    links.settle()


def back(grad_part, final_theirs, gain, later):
    scratch = []
    for piece in BACK_PIECES:
        scratch += phase_scratch(piece, 0)
    copies = 2 + 1 + 1 + 10 + 6 * len(BACK_PIECES)
    seq = (2 * LEN, SLOT)
    rows = (2 * BLOCK, D)
    outs = [struct((10, BLOCK, SLOT)), struct((10, BLOCK, SLOT)), struct((2, SLOT), F32), struct(seq)]
    outs += [struct((BLOCK, D), F32), struct((BLOCK, D)), struct((2 * BLOCK, SLOT)), struct((8, D), F32)]
    outs += [struct(after_shape(piece, 1)) for piece in BACK_PIECES]
    return pl.pallas_call(
        back_kernel,
        out_shape=outs + [struct((4 * BLOCK, EXPERTS)), struct(full_shape(VALUE))],
        in_specs=[IN_VMEM] * 3 + [ANYWHERE] * len(later),
        out_specs=[IN_VMEM] * len(outs) + [ANYWHERE] * 2,
        scratch_shapes=[
            pltpu.SemaphoreType.DMA((copies,)),
            pltpu.SemaphoreType.DMA((copies,)),
            pltpu.SemaphoreType.DMA((len(later),)),
            pltpu.SemaphoreType.DMA((2,)),
        ]
        + [pltpu.VMEM(operand.shape, operand.dtype) for operand in later]
        + [
            pltpu.VMEM(rows, BF16),
            pltpu.VMEM((BLOCK, D), BF16),
            pltpu.VMEM((2, 2, BLOCK, SLOT), BF16),
            pltpu.VMEM((2, BLOCK, SLOT), BF16),
            pltpu.VMEM(rows, BF16),
            pltpu.VMEM((2 * BLOCK, EXPERTS), F32),
            pltpu.VMEM((LEN, SLOT), BF16),
            pltpu.VMEM((LEN, SLOT), F32),
            pltpu.VMEM((LEN, SLOT), BF16),
            pltpu.VMEM(seq, BF16),
            pltpu.VMEM(seq, BF16),
            pltpu.VMEM(seq, F32),
            pltpu.VMEM((4 * BLOCK, EXPERTS), BF16),
        ]
        + [pltpu.VMEM(full_shape(array), BF16) for array in (DOWN, OUT)]
        + scratch,
        compiler_params=pltpu.CompilerParams(
            collective_id=1, has_side_effects=True, vmem_limit_bytes=VMEM_BYTES
        ),
    )(grad_part, final_theirs, gain, *later)


COUNT_ROW = 2 * H
VECTOR_ROW = 16
UP_BIAS_ROW = VECTOR_ROW + 5 * 8
SMALL_ROWS = UP_BIAS_ROW + FF // SLOT


def lay(target, first, vector):
    for row in range(vector.shape[1] // SLOT):
        target[first + row : first + row + 1, :] = vector[:, row * SLOT : (row + 1) * SLOT]


def close_kernel(*refs):
    refs = list(refs)
    take = lambda count: [refs.pop(0) for _ in range(count)]
    gain, feed_sums, grad_up_bias, bias_sums, counts, pay, pay_in, grad_logit, grad_far = take(9)
    early = take(len(EARLY))
    far_away = take(10)
    grad_tokens, small_out, down_out = take(3)
    both = dict(zip((UP, OUT, VALUE, KEYS, REST), take(5)))
    send_sem, recv_sem, own_sem, fetch_sem = take(4)
    local = take(10)
    grads = {VALUE: local.pop(0)}
    normed, experts, gates, wide, grad_experts, sinus, memory, tokens, grad_resid = local
    part, part_in, half_bias, grad_keys, grad_routers = take(5)
    grads.update(zip((KEYS, REST), take(2)))
    totals = dict(zip((UP, DOWN, OUT, VALUE, KEYS, REST), take(6)))
    slots = take(4)
    links, fetches = Links(send_sem, recv_sem), Fetches(fetch_sem)
    loads = [fetches.start(src, dst) for src, dst in zip(far_away, [grads[VALUE]] + local)]
    value_load = loads.pop(0)
    at = place()
    core, chip = at["core"], at["y"] // 2
    sibling, _ = others_of(at)
    high, low = at["x"] // 2, at["x"] % 2
    stays = (high == low) & (low == core)
    ahead, behind = dict(at), dict(at)
    ahead["x"], ahead["core"] = 2 * core + high, low
    behind["x"], behind["core"] = 2 * low + core, high
    ahead, behind = device_of(ahead), device_of(behind)
    devices = [moved(at, axis, steps) for axis in "xyz" for steps in (1, 2, 3)] + [sibling]
    greet(devices)

    def greet_more():
        greet([ahead, behind])
        pl.semaphore_wait(pltpu.get_barrier_semaphore(), len(devices) + 2)

    pl.when(jnp.logical_not(stays))(greet_more)
    pl.when(stays)(lambda: pl.semaphore_wait(pltpu.get_barrier_semaphore(), len(devices)))

    def begin(jobs):
        stages, later = [], []
        for piece, phase, ref in jobs:
            after = take(1)[0] if phase < 2 else totals[piece[0]].at[:, pl.ds(piece[1], piece[2])]
            stages.append(stage_for(links, at, piece, phase, ref, take, after))
            if phase < 2:
                later.append((piece, phase + 1, after))
        launch(stages)
        return stages, later

    def spread(number, value):
        axis = "xyz"[number]
        here = slots[number].at[at[axis]]
        here[...] = value
        return [links.send(here, here, moved(at, axis, steps)) for steps in (1, 2, 3)]

    def gathered(number, copies):
        for copy in copies:
            copy.wait_recv()
        one = slots[number]
        return (one[0] + one[1]) + (one[2] + one[3])

    def fill(array, right, start):
        width = right.shape[1]
        block = dot(normed[...], right[...], 0, 0).astype(BF16)
        grads[array][..., pl.ds(start, width)] = block.reshape(lead_shape(PLAIN) + (16, width))

    value_load.wait()
    value_stages, value_jobs = begin([(piece, 0, columns_of(grads[VALUE], piece)) for piece in VALUE_PIECES])
    for block in range(4):
        rows = slice(block * BLOCK, (block + 1) * BLOCK)
        key_heads = two_heads(chip, pay[block], pay_in[block])
        if block >= 2:
            query_heads = two_heads(chip, pay[6 + block], pay_in[6 + block])
        for pair in range(2):
            grad_keys[rows, pair * SLOT : (pair + 1) * SLOT] = key_heads[pair].astype(BF16)
            query = query_heads[pair].astype(BF16) if block >= 2 else jnp.zeros((BLOCK, SLOT), BF16)
            grad_keys[rows, (2 + pair) * SLOT : (3 + pair) * SLOT] = query
    loads[0].wait()
    fill(KEYS, grad_keys, 0)
    key_stages, key_jobs = begin([(piece, 0, columns_of(grads[KEYS], piece)) for piece in KEYS_PIECES])
    wait_for(*loads[1:3])
    lane = lax.broadcasted_iota(jnp.int32, (BLOCK, SLOT), 1)
    for block in range(4):
        rows = slice(block * BLOCK, (block + 1) * BLOCK)
        gate = gates[rows, :]
        value_heads = two_heads(chip, pay[4 + block], pay_in[4 + block])
        total = jnp.zeros((BLOCK, SLOT), F32)
        for slot in range(2 * E):
            expert = experts[rows, slot * SLOT : (slot + 1) * SLOT].astype(F32)
            inner = jnp.sum(value_heads[slot // E] * expert, axis=1, keepdims=True)
            total += jnp.where(lane == slot, inner, 0.0)
        total = total * gate * (1.0 - gate)
        if block >= 2:
            total += grad_logit[(block - 2) * BLOCK : (block - 1) * BLOCK, :].astype(F32)
        grad_routers[rows, :] = total.astype(BF16)
    fill(REST, grad_routers, 2 * SLOT)
    loads[5].wait()
    rel = dot(sinus[...], grad_far[...], 0, 0).astype(BF16).reshape(lead_shape(PLAIN) + (16, SLOT))
    blank = jnp.zeros((), BF16)
    grads[REST][..., :SLOT] = jnp.where(chip == 0, rel, blank)
    grads[REST][..., SLOT : 2 * SLOT] = jnp.where(chip == 1, rel, blank)
    rest_stages, rest_jobs = begin([(piece, 0, columns_of(grads[REST], piece)) for piece in REST_PIECES])
    forward(value_stages)
    early_stages, early_jobs = begin([(piece, 1, ref) for piece, ref in zip(EARLY, early)])
    wait_for(*loads[3:5])
    halves_in = []
    for block in (1, 3, 0, 2):
        rows = slice(block * BLOCK, (block + 1) * BLOCK)
        total = dot(grad_experts[rows, :], wide[:EXPERTS, :]) + dot(grad_keys[rows, :], wide[KEY_AT:ROUTER_AT, :])
        part[block] = (total + dot(grad_routers[rows, :], wide[ROUTER_AT:, :])).astype(BF16)
        if block % 2 == 1:
            halves_in.append(links.send(part.at[block], part_in.at[block // 2], sibling))
        if block == 3:
            forward(key_stages)
    forward(rest_stages)
    collect(value_stages)
    value_stages, value_jobs = begin(value_jobs)
    collect(key_stages)
    key_stages, key_jobs = begin(key_jobs)
    wait_for(*loads[6:])
    for copy in halves_in:
        copy.wait_recv()
    gain_sum = jnp.zeros((1, D), F32)
    bias_sum = jnp.zeros((1, D), F32)
    for side, rows in enumerate((memory, tokens)):
        scaled, inverse = centered(rows[...].astype(F32))
        grad = part[2 * side].astype(F32) + part_in[side].astype(F32)
        gain_sum += jnp.sum(grad * scaled, axis=0, keepdims=True)
        bias_sum += jnp.sum(grad, axis=0, keepdims=True)
        if side == 1:
            grad_tokens[...] = grad_resid[...] + norm_back(grad, scaled, inverse, as_row(gain))
    small = small_out
    small[:COUNT_ROW, :] = jnp.zeros((COUNT_ROW, SLOT), F32)
    small[COUNT_ROW:VECTOR_ROW, :] = counts[...]
    for number in range(2):
        small[pl.ds(H * number + 2 * chip + core, 1), :] = bias_sums[number : number + 1, :]
    lay(small, VECTOR_ROW, gain_sum)
    lay(small, VECTOR_ROW + 8, bias_sum)
    for number in range(3):
        lay(small, VECTOR_ROW + 16 + 8 * number, feed_sums[number : number + 1, :])
    small[UP_BIAS_ROW:, :] = jnp.zeros((FF // SLOT, SLOT), F32)
    lay(half_bias, 0, grad_up_bias[...])
    half = FF // 2 // SLOT
    small[pl.ds(pl.multiple_of(UP_BIAS_ROW + core * half, 8), half), :] = half_bias[...]
    copies = spread(0, small[...])
    forward(early_stages)
    collect(rest_stages)
    rest_stages, rest_jobs = begin(rest_jobs)
    collect(value_stages)
    value_stages, value_jobs = begin(value_jobs)
    collect(key_stages)
    key_stages, key_jobs = begin(key_jobs)
    copies = spread(1, gathered(0, copies))
    collect(early_stages)
    early_stages, early_jobs = begin(early_jobs)
    collect(rest_stages)
    rest_stages, rest_jobs = begin(rest_jobs)
    copies = spread(2, gathered(1, copies))
    collect(early_stages)
    last = []
    away = links.prepared(totals[DOWN], down_out, ahead)
    here = pltpu.make_async_copy(totals[DOWN], down_out, own_sem)
    pl.when(jnp.logical_not(stays))(away.start)
    pl.when(stays)(here.start)

    def exchange(arrays):
        for array in arrays:
            other = pl.ds(pl.multiple_of((1 - core) * 8, 8), 8)
            last.append(links.send(totals[array].at[other], both[array].at[core], sibling))
            both[array][core] = totals[array][pl.ds(pl.multiple_of(core * 8, 8), 8), :]

    exchange((UP, OUT))
    collect(value_stages)
    collect(key_stages)
    exchange((VALUE, KEYS))
    collect(rest_stages)
    exchange((REST,))
    pair = slots[3]
    pair[core] = gathered(2, copies)
    last.append(links.send(pair.at[core], pair.at[core], sibling))
    for copy in last:
        copy.wait_recv()
    small_out[...] = pair[0] + pair[1]
    pl.when(jnp.logical_not(stays))(away.wait)
    pl.when(stays)(here.wait)
    for copy in links.made:
        if copy is not away:
            copy.wait_send()


def close(gain, feed_sums, grad_up_bias, bias_sums, counts, pay, pay_in, grad_logit, grad_far, early, later):
    scratch = []
    copies = 2 + 9 + 1 + 1 + 5

    def round_of(pieces, phase):
        nonlocal copies
        for piece in pieces:
            if phase < 2:
                scratch.append(pltpu.VMEM(after_shape(piece, phase + 1), BF16))
            scratch.extend(phase_scratch(piece, phase))
            copies += copies_of(piece, phase)

    round_of(VALUE_PIECES, 0)
    round_of(KEYS_PIECES, 0)
    round_of(REST_PIECES, 0)
    round_of(EARLY, 1)
    round_of(VALUE_PIECES + KEYS_PIECES, 1)
    round_of(REST_PIECES, 1)
    round_of(VALUE_PIECES + KEYS_PIECES, 2)
    round_of(EARLY, 2)
    round_of(REST_PIECES, 2)
    outs = [struct((BLOCK, D), F32), struct((SMALL_ROWS, SLOT), F32), struct(SHAPES[DOWN], F32)]
    outs += [struct((2, 8, SHAPES[array][1]), F32) for array in (UP, OUT, VALUE, KEYS, REST)]
    return pl.pallas_call(
        close_kernel,
        out_shape=outs,
        in_specs=[IN_VMEM] * (9 + len(EARLY)) + [ANYWHERE] * len(later),
        out_specs=[IN_VMEM] * len(outs),
        scratch_shapes=[
            pltpu.SemaphoreType.DMA((copies,)),
            pltpu.SemaphoreType.DMA((copies,)),
            pltpu.SemaphoreType.DMA,
            pltpu.SemaphoreType.DMA((len(later),)),
        ]
        + [pltpu.VMEM(operand.shape, operand.dtype) for operand in later]
        + [
            pltpu.VMEM((4, BLOCK, D), BF16),
            pltpu.VMEM((2, BLOCK, D), BF16),
            pltpu.VMEM((FF // 2 // SLOT, SLOT), F32),
            pltpu.VMEM((4 * BLOCK, 4 * SLOT), BF16),
            pltpu.VMEM((4 * BLOCK, SLOT), BF16),
        ]
        + [pltpu.VMEM(full_shape(array), BF16) for array in (KEYS, REST)]
        + [pltpu.VMEM(SHAPES[array], F32) for array in (UP, DOWN, OUT, VALUE, KEYS, REST)]
        + [pltpu.VMEM((4, SMALL_ROWS, SLOT), F32)] * 3
        + [pltpu.VMEM((2, SMALL_ROWS, SLOT), F32)]
        + scratch,
        compiler_params=pltpu.CompilerParams(
            collective_id=2, has_side_effects=True, vmem_limit_bytes=VMEM_BYTES
        ),
    )(gain, feed_sums, grad_up_bias, bias_sums, counts, pay, pay_in, grad_logit, grad_far, *early, *later)


FRONT_OUTS = (
    ((2 * BLOCK, D), BF16),
    ((2 * BLOCK, D), BF16),
    ((WIDE, D), BF16),
    ((EXPERTS, D), BF16),
    ((4 * BLOCK, D), BF16),
    ((4 * BLOCK, EXPERTS), BF16),
    ((4 * BLOCK, SLOT), F32),
    ((2 * LEN, SLOT), BF16),
    ((2 * LEN, SLOT), BF16),
    ((4 * LEN, SLOT), BF16),
    ((LEN, SLOT), F32),
    ((LEN, 2 * LEN), BF16),
    ((2, BLOCK, SLOT), BF16),
    ((2, BLOCK, SLOT), BF16),
    ((2 * BLOCK, EXPERTS), BF16),
    ((2 * BLOCK, D), BF16),
    ((2 * BLOCK, D), BF16),
    ((2 * LEN, D), BF16),
    ((8, SLOT), F32),
)
FRONT_FETCHES = 3 + 2 * E * 2 + 2 * 2 + 1


def front_kernel(*refs):
    refs = list(refs)
    take = lambda count: [refs.pop(0) for _ in range(count)]
    (mem_len,) = take(1)
    gain, shift, value_route, out_route, bias_u, bias_v, value_router, out_router, sin_coarse, cos_coarse, sin_fine, cos_fine = take(12)
    memory, tokens, cotangent, value_weight, key_weight, query_weight, rel_weight, out_weight = take(8)
    outs = take(len(FRONT_OUTS))
    kept = take(len(FRONT_OUTS))
    tok, cot, wide, out_wide, normed, experts, gates, keys, values, queries, attended, probs, heads_own, heads_peer, mixed, part, part_in, sinus, counts = kept
    send_sem, recv_sem, fetch_sem, out_sem = take(4)
    mem, routes, routes_in, turned, rel, full, pay, pay_in, back = take(9)
    links, fetches, writes = Links(send_sem, recv_sem), Fetches(fetch_sem), Fetches(out_sem)
    at = place()
    core, chip = at["core"], at["y"] // 2
    peer = moved(at, "y", 2)
    sibling = dict(at)
    sibling["core"] = 1 - core
    sibling = device_of(sibling)
    mine, theirs = pl.ds(0, BLOCK), pl.ds(BLOCK, BLOCK)
    row_loads = [
        fetches.start(memory, mem.at[mine]),
        fetches.start(tokens, tok.at[mine]),
        fetches.start(cotangent, cot.at[mine]),
    ]

    def slots_from(target, slot, source, start):
        src = source.at[pl.ds(pl.multiple_of(start, 16), DH)]
        return fetches.start(src, target.at[pl.ds(slot, DH)])

    wide_loads, out_loads = [], []
    for pair in range(2):
        head = 2 * pair + core
        for expert in range(E):
            slot = (pair * E + expert) * SLOT
            wide_loads.append(slots_from(wide, slot, value_weight, (head * E + expert) * DH))
        wide_loads.append(slots_from(wide, KEY_AT + pair * SLOT, key_weight, head * DH))
        wide_loads.append(slots_from(wide, QUERY_AT + pair * SLOT, query_weight, head * DH))
    rel_load = slots_from(rel, 0, rel_weight, (2 * chip + core) * DH)
    for pair in range(2):
        head = 2 * pair + core
        for expert in range(E):
            slot = (pair * E + expert) * SLOT
            out_loads.append(slots_from(out_wide, slot, out_weight, (head * E + expert) * DH))
    for number in range(H):
        for kind in range(2):
            routes[8 * kind + 2 * number : 8 * kind + 2 * number + 2, :] = value_route[kind, number]
        routes[16 + 2 * number : 18 + 2 * number, :] = out_route[number]
    greet([sibling, peer])
    pl.semaphore_wait(pltpu.get_barrier_semaphore(), 2)
    mem_copy = links.send(memory, mem.at[theirs], sibling)
    tok_copy = links.send(tokens, tok.at[theirs], sibling)
    route_copy = links.send(routes, routes_in, sibling)
    cot_copy = links.send(cotangent, cot.at[theirs], sibling)
    blank = jnp.zeros((SLOT - DH, D), BF16)
    for slot in range(DH, EXPERTS, SLOT):
        out_wide[slot : slot + SLOT - DH, :] = blank
    for slot in range(DH, ROUTER_AT, SLOT):
        wide[slot : slot + SLOT - DH, :] = blank
    rel[DH:, :] = blank
    routers = []
    for router in (value_router, out_router):
        for pair in range(2):
            one = router[2 * pair * E : (2 * pair + 1) * E, :].astype(F32)
            two = router[(2 * pair + 1) * E : (2 * pair + 2) * E, :].astype(F32)
            routers.append(jnp.where(core == 0, one, two))
    routers.append(jnp.zeros((SLOT - 4 * E, D), F32))
    wide[ROUTER_AT:, :] = jnp.concatenate(routers, axis=0).astype(BF16)
    lane = lax.broadcasted_iota(jnp.int32, (BLOCK, SLOT), 1)
    turned[0] = routes[...].astype(F32).T.astype(jnp.int32)
    slot_of = lax.broadcasted_iota(jnp.int32, (2 * H, SLOT), 1) - lax.broadcasted_iota(jnp.int32, (2 * H, SLOT), 0) // 2 * E
    counted = jnp.zeros((1, SLOT), F32)
    for first in (0, 8, 16):
        for expert in range(E):
            named = (routes[first : first + 2 * H, :] == expert).astype(F32)
            number = jnp.sum(named, axis=1, keepdims=True)
            at_slot = slot_of == expert + (H * E if first == 16 else 0)
            counted += jnp.sum(jnp.where(at_slot, number, 0.0), axis=0, keepdims=True)
    counts[...] = jnp.zeros_like(counts)
    counts[0:1, :] = counted
    wait_for(*row_loads[:2])

    def normalize(block):
        rows = slice(block * BLOCK, (block + 1) * BLOCK)
        given = (mem, tok)[block // 2][(block % 2) * BLOCK : (block % 2 + 1) * BLOCK, :]
        scaled, _ = centered(given.astype(F32))
        normed[rows, :] = (scaled * as_row(gain) + as_row(shift)).astype(BF16)

    moving = []

    def project(block, buffer):
        rows = slice(block * BLOCK, (block + 1) * BLOCK)
        space = full.at[buffer]
        space[...] = dot(normed[rows, :], wide[...], 1, 1)
        experts[rows, :] = space[:, :EXPERTS].astype(BF16)
        named = turned[block % 2]
        token = block // 2
        chosen = chosen_lanes(named, 2 * H * token, core, lane, 0) & (lane < 2 * E)
        if token:
            chosen = chosen | chosen_lanes(named, 4 * H, core, lane, 2 * E)
        gate = jnp.where(chosen, jax.nn.sigmoid(space[:, ROUTER_AT:WIDE]), 0.0)
        gates[rows, :] = gate
        for pair in range(2):
            total = jnp.zeros((BLOCK, SLOT), F32)
            for expert in range(E):
                slot = pair * E + expert
                total += gate[:, slot : slot + 1] * space[:, slot * SLOT : (slot + 1) * SLOT]
            pay[pair, block] = space[:, KEY_AT + pair * SLOT : KEY_AT + (pair + 1) * SLOT].astype(BF16)
            pay[pair, 4 + block] = total.astype(BF16)
            if token:
                pay[pair, 6 + block] = space[:, QUERY_AT + pair * SLOT : QUERY_AT + (pair + 1) * SLOT].astype(BF16)
        for segment in (block, 4 + block) + ((6 + block,) if token else ()):
            moving.append(links.send(pay.at[1 - chip, segment], pay_in.at[segment], peer))

    normalize(0)
    normalize(2)
    wait_for(*wide_loads)
    project(0, 0)
    project(2, 1)
    mem_copy.wait_recv()
    normalize(1)
    tok_copy.wait_recv()
    normalize(3)
    route_copy.wait_recv()
    turned[1] = routes_in[...].astype(F32).T.astype(jnp.int32)
    project(1, 0)
    project(3, 1)
    for number in (0, 2, 4, 5, 6):
        writes.start(kept[number], outs[number])
    sin_b, cos_b = sin_fine[...], cos_fine[...]
    for number in range(32):
        sin_a, cos_a = sin_coarse[number : number + 1, :], cos_coarse[number : number + 1, :]
        rows = slice(64 * number, 64 * (number + 1))
        sinus[rows, : D // 2] = (sin_a * cos_b + cos_a * sin_b).astype(BF16)
        sinus[rows, D // 2 :] = (cos_a * cos_b - sin_a * sin_b).astype(BF16)
    writes.start(kept[17], outs[17])
    writes.start(kept[18], outs[18])
    rel_load.wait()
    far_rel = queries.at[pl.ds(2 * LEN, 2 * LEN)]
    far_rel[...] = dot(sinus[...], rel[...], 1, 1).astype(BF16)
    places = spots_of(core, chip)
    head = 2 * chip + core

    def own_head(bias):
        row = bias[...].astype(F32).reshape(1, H * DH)
        total = jnp.zeros((1, DH), F32)
        for number in range(H):
            total += jnp.where(head == number, row[:, number * DH : (number + 1) * DH], 0.0)
        return jnp.concatenate([total, jnp.zeros((1, SLOT - DH), F32)], axis=1)

    head_u, head_v = own_head(bias_u), own_head(bias_v)
    qu, qv = queries.at[pl.ds(0, LEN)], queries.at[pl.ds(LEN, LEN)]

    def assemble(number, segment_of):
        side = number % 2
        start = places[number]
        keys[rows_at(start), :] = segment_of(side)
        keys[rows_at(start + LEN), :] = segment_of(2 + side)
        values[rows_at(start), :] = segment_of(4 + side)
        values[rows_at(start + LEN), :] = segment_of(6 + side)
        query = segment_of(8 + side).astype(F32)
        qu[rows_at(start), :] = (query + head_u).astype(BF16)
        qv[rows_at(start), :] = (query + head_v).astype(BF16)

    for number in range(2):
        assemble(number, lambda segment: pay[chip, segment])
    for copy in moving:
        copy.wait_recv()
    for number in range(2, 4):
        assemble(number, lambda segment: pay_in[segment])
    for number in (7, 8, 9):
        writes.start(kept[number], outs[number])
    mem_at = lax.broadcasted_iota(jnp.int32, (1, LEN), 1)
    mem_mask = jnp.where(mem_at >= LEN - mem_len[0], 0.0, MASKED)
    down = lax.broadcasted_iota(jnp.int32, (BLOCK, BLOCK), 0)
    across = lax.broadcasted_iota(jnp.int32, (BLOCK, BLOCK), 1)
    own_mask = jnp.where(across <= down, 0.0, MASKED)
    for block in range(LEN // BLOCK):
        attend(block, mem_mask, own_mask, qu, qv, keys, values, far_rel, attended, probs)
    for side in range(2):
        heads_own[side] = attended[rows_at(places[side]), :].astype(BF16)
        back[side] = attended[rows_at(places[2 + side]), :].astype(BF16)
    returned = links.send(back, heads_peer, peer)
    for number in (10, 11, 12):
        writes.start(kept[number], outs[number])
    wait_for(*out_loads)
    writes.start(kept[3], outs[3])
    returned.wait_recv()
    writes.start(kept[13], outs[13])
    sent = []
    for side in range(2):
        heads = two_heads(chip, heads_own[side], heads_peer[side])
        rows = slice(side * BLOCK, (side + 1) * BLOCK)
        gate = gates[(2 + side) * BLOCK : (3 + side) * BLOCK, :]
        for slot in range(2 * E):
            weight = gate[:, 2 * E + slot : 2 * E + slot + 1]
            mixed[rows, slot * SLOT : (slot + 1) * SLOT] = (weight * heads[slot // E]).astype(BF16)
        part[rows, :] = dot(mixed[rows, :], out_wide[...]).astype(BF16)
        other = pl.ds((1 - side) * BLOCK, BLOCK)
        sent.append(links.send(part.at[pl.ds(side * BLOCK, BLOCK)], part_in.at[other], sibling))
    writes.start(kept[14], outs[14])
    writes.start(kept[15], outs[15])
    row_loads[2].wait()
    cot_copy.wait_recv()
    writes.start(kept[1], outs[1])
    for copy in sent:
        copy.wait_recv()
    writes.start(kept[16], outs[16])
    wait_for(*writes.copies)
    for copy in links.made:
        copy.wait_send()


def front(mem_len, small, large):
    copies = 4 + 10 + 1 + 2
    return pl.pallas_call(
        front_kernel,
        out_shape=[struct(*out) for out in FRONT_OUTS],
        in_specs=[IN_SMEM] + [IN_VMEM] * len(small) + [ANYWHERE] * len(large),
        out_specs=[ANYWHERE] * len(FRONT_OUTS),
        scratch_shapes=[pltpu.VMEM(*out) for out in FRONT_OUTS]
        + [
            pltpu.SemaphoreType.DMA((copies,)),
            pltpu.SemaphoreType.DMA((copies,)),
            pltpu.SemaphoreType.DMA((FRONT_FETCHES,)),
            pltpu.SemaphoreType.DMA((len(FRONT_OUTS),)),
            pltpu.VMEM((2 * BLOCK, D), BF16),
            pltpu.VMEM((6 * H, BLOCK), jnp.int32),
            pltpu.VMEM((6 * H, BLOCK), jnp.int32),
            pltpu.VMEM((2, BLOCK, 6 * H), jnp.int32),
            pltpu.VMEM((SLOT, D), BF16),
            pltpu.VMEM((2, BLOCK, WIDE), F32),
            pltpu.VMEM((2, 10, BLOCK, SLOT), BF16),
            pltpu.VMEM((10, BLOCK, SLOT), BF16),
            pltpu.VMEM((2, BLOCK, SLOT), BF16),
        ],
        compiler_params=pltpu.CompilerParams(
            collective_id=0, has_side_effects=True, vmem_limit_bytes=VMEM_BYTES
        ),
    )(mem_len, *small, *large)


ARRANGED = (
    ((BLOCK, D), BF16),
    ((BLOCK, D), F32),
    ((8,), F32),
    ((8,), F32),
    ((8, H * DH), F32),
    ((8, H * DH), F32),
    ((8, H * DH), F32),
    ((H * DH,), F32),
    ((H * DH,), F32),
    ((8, H * E), F32),
    ((8, H * E * DH), F32),
    ((8, H * E), F32),
    ((8, H * E * DH), F32),
    ((8,), F32),
    ((8,), F32),
    ((8, FF), F32),
    ((32,), F32),
    ((32, D), F32),
    ((8,), F32),
    ((2, H, E), jnp.int32),
)


def arrange_kernel(result_in, tokens_in, small, down_in, up, out, value, keys, rest, *outs):
    (
        result,
        grad_tokens,
        attn_gain,
        attn_bias,
        grad_query,
        grad_key,
        grad_rel,
        grad_bias_u,
        grad_bias_v,
        value_router,
        grad_value,
        out_router,
        grad_out,
        ffn_gain,
        ffn_bias,
        grad_up,
        up_bias,
        grad_down,
        down_bias,
        counts,
    ) = outs
    result[...] = result_in[...]
    grad_tokens[...] = tokens_in[...]
    grad_down[...] = down_in[...]
    grad_up[:, : FF // 2] = up[0]
    grad_up[:, FF // 2 :] = up[1]
    for head in range(H):
        core, pair = head % 2, head // 2
        for expert in range(E):
            slot = (pair * E + expert) * SLOT
            start = (head * E + expert) * DH
            grad_out[:, start : start + DH] = out[core, :, slot : slot + DH]
            grad_value[:, start : start + DH] = value[core, :, slot : slot + DH]
        start = head * DH
        for target, source, slot in ((grad_key, keys, 0), (grad_query, keys, 2 * SLOT), (grad_rel, rest, 0)):
            slot += pair * SLOT
            target[:, start : start + DH] = source[core, :, slot : slot + DH]
        for kind, target in enumerate((value_router, out_router)):
            at = 2 * SLOT + (2 * kind + pair) * E
            target[:, head * E : (head + 1) * E] = rest[core, :, at : at + E]
    device = lax.axis_index("dp") * 4 + lax.axis_index("seq")

    def share(target, first, size):
        per_row = SLOT // size
        row = small[pl.ds(first + device // per_row, 1), :]
        row = pltpu.roll(row, SLOT - device % per_row * size, 1)
        target[...] = row[:, :size].reshape(size)

    for number, target in enumerate((attn_gain, attn_bias, ffn_gain, ffn_bias, down_bias)):
        share(target, VECTOR_ROW + 8 * number, 8)
    share(up_bias, UP_BIAS_ROW, 32)
    for first, target in ((0, grad_bias_u), (H, grad_bias_v)):
        heads = [small[first + head : first + head + 1, :DH] for head in range(H)]
        target[...] = jnp.concatenate(heads, axis=1).reshape(H * DH)
    row = (small[COUNT_ROW : COUNT_ROW + 1, :] + 0.5).astype(jnp.int32)
    for kind in range(2):
        for head in range(H):
            at = (kind * H + head) * E
            counts[kind, head : head + 1, :] = row[:, at : at + E]


def arrange(*operands):
    return local_call(arrange_kernel, [struct(*out) for out in ARRANGED], vmem=len(operands))(*operands)


def angle_tables():
    frequency = jnp.exp(jnp.arange(D // 2, dtype=jnp.int32).astype(F32) * (-2.0 * math.log(10000.0) / D))
    coarse = (64 * (31 - jnp.arange(32, dtype=jnp.int32))).astype(F32)[:, None] * frequency
    fine = (63 - jnp.arange(64, dtype=jnp.int32)).astype(F32)[:, None] * frequency
    return jnp.sin(coarse), jnp.cos(coarse), jnp.sin(fine), jnp.cos(fine)


def body(
    tokens,
    memory,
    cotangent,
    mem_len,
    value_route,
    output_route,
    attn_norm_gain,
    attn_norm_bias,
    query_weight,
    key_weight,
    rel_weight,
    bias_u,
    bias_v,
    value_router,
    value_weight,
    out_router,
    out_weight,
    ffn_norm_gain,
    ffn_norm_bias,
    up_weight,
    up_bias,
    down_weight,
    down_bias,
):
    tokens, memory, cotangent = tokens[0], memory[0], cotangent[0]
    (
        tokens_pair,
        cot,
        wide,
        out_wide,
        normed,
        experts,
        gates,
        keys,
        values,
        queries,
        attended,
        probs,
        heads_own,
        heads_peer,
        mixed,
        out_part,
        out_part_in,
        sinus,
        counts,
    ) = front(
        mem_len,
        [
            attn_norm_gain,
            attn_norm_bias,
            value_route[0].transpose(0, 2, 3, 1),
            output_route[0].transpose(1, 2, 0),
            bias_u,
            bias_v,
            value_router.T,
            out_router.T,
            *angle_tables(),
        ],
        [memory, tokens, cotangent, value_weight.T, key_weight.T, query_weight.T, rel_weight.T, out_weight],
    )
    final_mine, final_theirs, norm_part, grad_up_bias, *first, resid, hidden, grad_up = feed(
        tokens_pair,
        out_part,
        out_part_in,
        cot,
        ffn_norm_gain,
        ffn_norm_bias,
        up_bias,
        down_bias,
        up_weight,
        down_weight,
    )
    pay, pay_in, bias_sums, grad_far, grad_resid, result, grad_logit, feed_sums, *early = back(
        norm_part,
        final_theirs,
        ffn_norm_gain,
        [
            grad_up,
            hidden,
            cot,
            resid,
            out_wide,
            gates,
            heads_own,
            heads_peer,
            mixed,
            probs,
            attended,
            values,
            keys,
            queries,
            normed,
            final_mine,
        ],
    )
    *early, grad_experts, grad_value = first + early
    grad_tokens, small_sum, grad_down, up_both, out_both, value_both, keys_both, rest_both = close(
        attn_norm_gain,
        feed_sums,
        grad_up_bias,
        bias_sums,
        counts,
        pay,
        pay_in,
        grad_logit,
        grad_far,
        early,
        [grad_value, normed, experts, gates, wide, grad_experts, sinus, memory, tokens, grad_resid],
    )
    outs = arrange(
        result, grad_tokens, small_sum, grad_down, up_both, out_both, value_both, keys_both, rest_both
    )
    outs = list(outs)
    outs[0], outs[1], outs[12] = outs[0][None], outs[1][None], outs[12].T
    return tuple(outs)


def solution(mesh):
    in_specs = (
        P("dp", "seq", None),
        P("dp", "seq", None),
        P("dp", "seq", None),
        P("dp"),
        P("dp", None, "seq", None, None),
        P("dp", "seq", None, None),
        P(),
        P(),
        P(),
        P(),
        P(),
        P(),
        P(),
        P(),
        P(),
        P(),
        P(),
        P(),
        P(),
        P(),
        P(),
        P(),
        P(),
    )
    out_specs = (
        P("dp", "seq", None),
        P("dp", "seq", None),
        P(("dp", "seq")),
        P(("dp", "seq")),
        P(("dp", "seq"), None),
        P(("dp", "seq"), None),
        P(("dp", "seq"), None),
        P(),
        P(),
        P(("dp", "seq"), None),
        P(("dp", "seq"), None),
        P(("dp", "seq"), None),
        P(None, ("dp", "seq")),
        P(("dp", "seq")),
        P(("dp", "seq")),
        P(("dp", "seq"), None),
        P(("dp", "seq")),
        P(("dp", "seq"), None),
        P(("dp", "seq")),
        P(),
    )
    return jax.shard_map(body, mesh=mesh, in_specs=in_specs, out_specs=out_specs, check_vma=False)
```

```python
from functools import partial
import math

import jax
import jax.numpy as jnp
from jax import lax
from jax.experimental import pallas as pl
from jax.experimental.pallas import tpu as pltpu
from jax.sharding import PartitionSpec as P

D = 1024
H = 4
DH = 112
E = 5
FF = 4096
LEN = 1024
SLOT = 128
BLOCK = 256
EXPERTS = 2 * E * SLOT
KEY_AT = EXPERTS
QUERY_AT = KEY_AT + 2 * SLOT
ROUTER_AT = QUERY_AT + 2 * SLOT
WIDE = ROUTER_AT + SLOT
SCALE = DH ** (-0.5)
MASKED = -1e30
EPS = 1e-05
BF16 = jnp.bfloat16
F32 = jnp.float32
VMEM_BYTES = 60 * 1024 * 1024
IN_VMEM = pl.BlockSpec(memory_space=pltpu.VMEM)
IN_SMEM = pl.BlockSpec(memory_space=pltpu.SMEM)
ANYWHERE = pl.BlockSpec(memory_space=pl.ANY)
MESH = pl.DeviceIdType.MESH


def dot(left, right, left_dim=1, right_dim=0):
    return lax.dot_general(
        left, right, (((left_dim,), (right_dim,)), ((), ())), preferred_element_type=F32
    )


def struct(shape, kind=BF16):
    return jax.ShapeDtypeStruct(shape, kind)


def local_call(kernel, out_shape, scratch_shapes=(), smem=0, vmem=0, **kw):
    return pl.pallas_call(
        kernel,
        out_shape=out_shape,
        in_specs=[IN_SMEM] * smem + [IN_VMEM] * vmem,
        out_specs=[IN_VMEM] * len(out_shape),
        scratch_shapes=scratch_shapes,
        compiler_params=pltpu.CompilerParams(vmem_limit_bytes=VMEM_BYTES),
        **kw,
    )


def centered(rows):
    center = rows - jnp.mean(rows, axis=1, keepdims=True)
    inverse = lax.rsqrt(jnp.mean(center * center, axis=1, keepdims=True) + EPS)
    return center * inverse, inverse


def norm_back(grad, scaled, inverse, gain):
    through = grad * gain
    return inverse * (
        through
        - jnp.mean(through, axis=1, keepdims=True)
        - scaled * jnp.mean(through * scaled, axis=1, keepdims=True)
    )


def as_row(vector):
    return vector[...].astype(F32).reshape(1, vector.shape[0])


def chosen_lanes(route, first, core, lane, start):
    chosen = None
    for pair in range(2):
        for number in range(2):
            column = first + 4 * pair + number
            one = jnp.where(core == 0, route[:, column : column + 1], route[:, column + 2 : column + 3])
            hit = lane == one + (start + E * pair)
            chosen = hit if chosen is None else chosen | hit
    return chosen


def spots_of(core, chip):
    return [
        chip * 512 + core * BLOCK,
        chip * 512 + (1 - core) * BLOCK,
        (1 - chip) * 512 + core * BLOCK,
        (1 - chip) * 512 + (1 - core) * BLOCK,
    ]


def rows_at(start):
    return pl.ds(pl.multiple_of(start, BLOCK), BLOCK)


def attend(block, mem_mask, own_mask, qu, qv, keys, values, far_rel, attended, probs):
    rows = pl.ds(block * BLOCK, BLOCK)
    width = LEN + (block + 1) * BLOCK
    first_far = 2 * LEN - width
    content = dot(qu[rows, :], keys[:width, :], 1, 1)
    far = dot(qv[rows, :], far_rel[first_far:, :], 1, 1)
    raw = content + pltpu.roll(far, width - BLOCK + 1, 1, stride=1, stride_axis=0)
    parts = [raw[:, :LEN] + mem_mask]
    if block > 0:
        parts.append(raw[:, LEN : width - BLOCK])
    parts.append(raw[:, width - BLOCK :] + own_mask)
    highest = parts[0].max(axis=1, keepdims=True)
    for part in parts[1:]:
        highest = jnp.maximum(highest, part.max(axis=1, keepdims=True))
    parts = [jnp.exp2((part - highest) * (SCALE * math.log2(math.e))) for part in parts]
    total = parts[0].sum(axis=1, keepdims=True)
    for part in parts[1:]:
        total += part.sum(axis=1, keepdims=True)
    share = 1.0 / total
    start = 0
    for part in parts:
        size = part.shape[1]
        probs[rows, start : start + size] = (part * share).astype(BF16)
        start += size
    attended[rows, :] = dot(probs[rows, :width], values[:width, :], 1, 0)


def two_heads(chip, own, peer):
    first = jnp.where(chip == 0, own.astype(F32), peer.astype(F32))
    second = jnp.where(chip == 0, peer.astype(F32), own.astype(F32))
    return first, second


def place():
    dp = lax.axis_index("dp")
    sq = lax.axis_index("seq")
    return dict(x=dp // 8, z=(dp // 2) % 4, y=(sq // 2) * 2 + dp % 2, core=sq % 2)


def device_of(at):
    return (at["x"] * 8 + at["z"] * 2 + at["y"] % 2, (at["y"] // 2) * 2 + at["core"])


def moved(at, axis, steps):
    other = dict(at)
    other[axis] = (at[axis] + steps) % 4
    return device_of(other)


PLAIN = (("x", 4), ("z", 4), ("ylo", 2), ("yhi", 2))
SPLIT = (("xhi", 2), ("z", 4), ("ylo", 2), ("yhi", 2), ("xlo", 2))


def part_of(name, where):
    return {"hi": where // 2, "lo": where % 2}.get(name[1:], where)


def chunk_of(ref, dims, axis, where):
    return ref.at[tuple(part_of(name, where) if name[0] == axis else slice(None) for name, _ in dims)]


def without(dims, axes):
    return tuple(dim for dim in dims if dim[0][0] not in axes)


def lead_shape(dims):
    return tuple(size for _, size in dims)


def halves(width):
    one = (width // 2 + 127) // 128 * 128
    return (0, one), (one, width - one)


def each_block(lead, size, step):
    if math.prod(lead) * size <= 64 * 1024:
        step(Ellipsis)
        return

    def run(number, carry):
        step(number)
        return carry

    lax.fori_loop(0, lead[0], run, 0)


class Links:
    def __init__(self, send_sem, recv_sem):
        self.send_sem, self.recv_sem, self.made, self.open = send_sem, recv_sem, [], {}

    def prepared(self, src, dst, device):
        slot = len(self.made)
        copy = pltpu.make_async_remote_copy(
            src_ref=src,
            dst_ref=dst,
            send_sem=self.send_sem.at[slot],
            recv_sem=self.recv_sem.at[slot],
            device_id=device,
            device_id_type=MESH,
        )
        self.made.append(copy)
        self.open[id(copy)] = copy
        return copy

    def settle(self, copies=None):
        for copy in list(self.open.values()) if copies is None else copies:
            copy.wait_send()
            del self.open[id(copy)]

    def send(self, src, dst, device):
        copy = self.prepared(src, dst, device)
        copy.start()
        return copy


def added(target, *terms):
    def add(index):
        total = terms[0][index].astype(F32)
        for term in terms[1:]:
            total += term[index].astype(F32)
        target[index] = total.astype(target.dtype)

    return add


class Stage:
    def __init__(self, links, at, ref, dims, axis, width, bufs, after):
        self.links, self.bufs, self.after = links, bufs, after
        self.left = lead_shape(without(dims, axis))
        self.cols = [pl.ds(*half) for half in halves(width)]
        self.sizes = [half[1] * bufs[0].shape[-2] for half in halves(width)]
        self.near = [chunk_of(ref, dims, axis, (at[axis] + steps) % 4) for steps in range(4)]
        self.ahead = [self.near[steps].at[..., self.cols[side]] for side, steps in ((0, 1), (1, 3))]
        self.far, self.close, self.summed = [], [], []
        for side, steps in ((0, 1), (1, 3)):
            device = moved(at, axis, steps)
            other = self.cols[1 - side]
            self.far.append(links.prepared(self.near[2].at[..., self.cols[side]], bufs[side], device))
            self.close.append(links.prepared(self.near[steps].at[..., other], bufs[2 + side], device))
            self.summed.append(links.prepared(bufs[side], bufs[4 + side], device))

    def launch_far(self):
        for copy in self.far:
            copy.start()

    def launch_near(self):
        for copy in self.close:
            copy.start()

    def forward(self):
        for side in range(2):
            self.far[side].wait_recv()
            each_block(self.left, self.sizes[side], added(self.bufs[side], self.bufs[side], self.ahead[side]))
            self.summed[side].start()

    def collect(self):
        for copy in self.close + self.summed:
            copy.wait_recv()
        for side in (0, 1):
            cols = self.cols[side]
            terms = self.near[0].at[..., cols], self.bufs[4 + side], self.bufs[3 - side]
            each_block(self.left, self.sizes[side], added(self.after.at[..., cols], *terms))

    def settle(self):
        self.links.settle(self.far + self.close + self.summed)


class DirectStage:
    def __init__(self, links, at, ref, dims, axis, width, bufs, after):
        self.bufs, self.after = bufs, after
        self.left = lead_shape(without(dims, axis))
        self.size = width * bufs[0].shape[-2]
        self.near = [chunk_of(ref, dims, axis, (at[axis] + steps) % 4) for steps in range(4)]
        self.copies = [
            links.prepared(self.near[steps], bufs[steps - 1], moved(at, axis, steps)) for steps in (1, 2, 3)
        ]

    def launch_far(self):
        for copy in self.copies:
            copy.start()

    def launch_near(self):
        pass

    def forward(self):
        pass

    def collect(self):
        for copy in self.copies:
            copy.wait_recv()
        each_block(self.left, self.size, added(self.after, self.near[0], *self.bufs))


def direct_scratch(dims, axis, rows, width):
    return [pltpu.VMEM(lead_shape(without(dims, axis)) + (rows, width), BF16)] * 3


def stage_scratch(dims, axis, rows, width):
    left = lead_shape(without(dims, axis))
    (_, one), (_, two) = halves(width)
    return [pltpu.VMEM(left + (rows, size), BF16) for size in (one, two, two, one, one, two)]


def launch(stages):
    for stage in stages:
        stage.launch_far()
    for stage in stages:
        stage.launch_near()


def greet(devices):
    barrier = pltpu.get_barrier_semaphore()
    for device in devices:
        pl.semaphore_signal(barrier, inc=1, device_id=device, device_id_type=MESH)


UP, DOWN, OUT, VALUE, KEYS, REST = range(6)
LAYOUTS = (PLAIN, SPLIT, PLAIN, PLAIN, PLAIN, PLAIN)
SHAPES = ((16, FF // 2), (32, D), (16, EXPERTS), (16, EXPERTS), (16, 4 * SLOT), (16, 3 * SLOT))
UP_FIRST = ((UP, 0, 256, "xyz"), (UP, 256, 256, "zxy"), (UP, 512, 256, "yzx"))
UP_PIECES = ((UP, 768, 384, "xyz"), (UP, 1152, 384, "zxy"), (UP, 1536, 512, "yzx"))
DOWN_PIECES = ((DOWN, 0, 512, "xyz"), (DOWN, 512, 512, "zxy"))
OUT_PIECES = ((OUT, 0, 512, "xzy"), (OUT, 512, 512, "zyx"), (OUT, 1024, 256, "yzx"))
VALUE_PIECES = ((VALUE, 0, 512, "xyz"), (VALUE, 512, 512, "zxy"), (VALUE, 1024, 256, "yzx"))
KEYS_PIECES = ((KEYS, 0, 256, "xyz"), (KEYS, 256, 256, "zxy"))
REST_PIECES = ((REST, 0, 384, "yzx"),)
BACK_PIECES = UP_PIECES + DOWN_PIECES + OUT_PIECES
EARLY = UP_FIRST + BACK_PIECES
LATE = VALUE_PIECES + KEYS_PIECES + REST_PIECES


def dims_after(piece, phases):
    return without(LAYOUTS[piece[0]], piece[3][:phases])


def after_shape(piece, phases):
    return lead_shape(dims_after(piece, phases)) + (SHAPES[piece[0]][0], piece[2])


def is_direct(piece, phase):
    return phase == 2 or phase == 1 and piece in LATE


def phase_scratch(piece, phase):
    made = direct_scratch if is_direct(piece, phase) else stage_scratch
    return made(dims_after(piece, phase), piece[3][phase], SHAPES[piece[0]][0], piece[2])


def copies_of(piece, phase):
    return 3 if is_direct(piece, phase) else 6


def stage_for(links, at, piece, phase, ref, take, after):
    made = DirectStage if is_direct(piece, phase) else Stage
    bufs = take(3 if is_direct(piece, phase) else 6)
    return made(links, at, ref, dims_after(piece, phase), piece[3][phase], piece[2], bufs, after)


def full_shape(array):
    return lead_shape(LAYOUTS[array]) + SHAPES[array]


def columns_of(ref, piece):
    return ref.at[..., pl.ds(piece[1], piece[2])]


class Fetches:
    def __init__(self, sems):
        self.sems, self.copies = sems, []

    def start(self, src, dst):
        copy = pltpu.make_async_copy(src, dst, self.sems.at[len(self.copies)])
        copy.start()
        self.copies.append(copy)
        return copy


def wait_for(*copies):
    for copy in copies:
        copy.wait()


def forward(stages):
    for stage in stages:
        stage.forward()


def collect(stages):
    for stage in stages:
        stage.collect()


def others_of(at):
    sibling = dict(at)
    sibling["core"] = 1 - at["core"]
    return device_of(sibling), moved(at, "y", 2)


STEP = 256
STEPS = FF // 2 // STEP


def feed_kernel(*refs):
    refs = list(refs)
    take = lambda count: [refs.pop(0) for _ in range(count)]
    rows, part_mine, part_theirs, cot, gain, shift, up_bias, down_bias = take(8)
    up_given, down_given = take(2)
    final_mine, final_theirs, grad_part, grad_up_bias = take(4)
    afters = take(len(UP_FIRST))
    outs = take(3)
    resid, hidden, grad_up, write_sem = take(4)
    send_sem, recv_sem, fetch_sem, up, down, low, low_turned, grad_all, bias_row = take(9)
    before_a, before_b, above_a, above_b = take(4)
    fetches, writes = Fetches(fetch_sem), Fetches(write_sem)
    links = Links(send_sem, recv_sem)
    at = place()
    first = at["core"] * (FF // 2)

    def own(step):
        return pl.ds(step * STEP, STEP)

    for step in range(STEPS):
        there = pl.ds(pl.multiple_of(first + step * STEP, STEP), STEP)
        fetches.start(up_given.at[:, there], up.at[:, own(step)])
        fetches.start(down_given.at[there, :], down.at[own(step), :])
    devices = [moved(at, axis, steps) for axis in "xyz" for steps in (1, 3)]
    greet(devices)
    for side in range(2):
        here = slice(side * BLOCK, (side + 1) * BLOCK)
        total = rows[here, :].astype(F32) + (part_mine[here, :].astype(F32) + part_theirs[here, :].astype(F32))
        resid[here, :] = total
        scaled, _ = centered(total)
        low[here, :] = (scaled * as_row(gain) + as_row(shift)).astype(BF16)
    writes.start(resid, outs[0])
    low_turned[...] = low[...].T
    bias_row[...] = as_row(up_bias)

    def ahead(step, before, above):
        bias = bias_row[:, pl.ds(pl.multiple_of(first + step * STEP, STEP), STEP)]
        before[...] = dot(low[...], up[:, own(step)]) + bias
        above[...] = dot(cot[...], down[own(step), :], 1, 1)

    def weigh(step):
        block = dot(low_turned[...], grad_all[:, own(step)]).astype(BF16)
        grad_up[..., own(step)] = block.reshape(lead_shape(PLAIN) + (16, STEP))

    def activate(step, before, above):
        value = before[...]
        below = 0.5 * (1.0 + lax.erf(value * (0.5**0.5)))
        hidden[:, own(step)] = (value * below).astype(BF16)
        slope = below + value * (jnp.exp(-0.5 * value * value) * ((2.0 * math.pi) ** -0.5))
        grad_low = (above[...] * slope).astype(BF16)
        grad_all[:, own(step)] = grad_low
        grad_up_bias[:, own(step)] = jnp.sum(grad_low.astype(F32), axis=0, keepdims=True)

    stages = []
    for piece, after in zip(UP_FIRST, afters):
        stages.append(stage_for(links, at, piece, 0, columns_of(grad_up, piece), take, after))
    pairs = (before_a, above_a), (before_b, above_b)
    wait_for(*fetches.copies[:2])
    ahead(0, *pairs[0])
    for step in range(STEPS):
        if step + 1 < STEPS:
            wait_for(*fetches.copies[2 * step + 2 : 2 * step + 4])
            ahead(step + 1, *pairs[(step + 1) % 2])
        activate(step, *pairs[step % 2])
        if step > 0:
            weigh(step - 1)
        if step == 1:
            pl.semaphore_wait(pltpu.get_barrier_semaphore(), len(devices))
        if 1 <= step <= len(stages):
            launch(stages[step - 1 : step])
        if 4 <= step < 4 + len(stages):
            forward(stages[step - 4 : step - 3])
    weigh(STEPS - 1)
    writes.start(hidden, outs[1])
    writes.start(grad_up, outs[2])
    grad_part[...] = dot(grad_all[...], up[...], 1, 1).astype(BF16)
    final_mine[...] = resid[:BLOCK, :] + dot(hidden[:BLOCK, :], down[...]) + as_row(down_bias)
    final_theirs[...] = dot(hidden[BLOCK:, :], down[...]).astype(BF16)
    collect(stages)
    wait_for(*writes.copies)
    links.settle()


def feed(rows, part_mine, part_theirs, cot, gain, shift, up_bias, down_bias, up, down):
    pair = (2 * BLOCK, D)
    outs = [struct((BLOCK, D), F32), struct((BLOCK, D)), struct(pair), struct((1, FF // 2), F32)]
    outs += [struct(after_shape(piece, 1)) for piece in UP_FIRST]
    scratch = []
    for piece in UP_FIRST:
        scratch += phase_scratch(piece, 0)
    written = [struct(pair, F32), struct((2 * BLOCK, FF // 2)), struct(full_shape(UP))]
    return pl.pallas_call(
        feed_kernel,
        out_shape=outs + written,
        in_specs=[IN_VMEM] * 8 + [ANYWHERE] * 2,
        out_specs=[IN_VMEM] * len(outs) + [ANYWHERE] * len(written),
        scratch_shapes=[pltpu.VMEM(out.shape, out.dtype) for out in written]
        + [
            pltpu.SemaphoreType.DMA((len(written),)),
            pltpu.SemaphoreType.DMA((6 * len(UP_FIRST),)),
            pltpu.SemaphoreType.DMA((6 * len(UP_FIRST),)),
            pltpu.SemaphoreType.DMA((2 * STEPS,)),
            pltpu.VMEM((D, FF // 2), BF16),
            pltpu.VMEM((FF // 2, D), BF16),
            pltpu.VMEM(pair, BF16),
            pltpu.VMEM((D, 2 * BLOCK), BF16),
            pltpu.VMEM((2 * BLOCK, FF // 2), BF16),
            pltpu.VMEM((1, FF), F32),
        ]
        + [pltpu.VMEM((2 * BLOCK, STEP), F32)] * 4
        + scratch,
        compiler_params=pltpu.CompilerParams(
            collective_id=3, has_side_effects=True, vmem_limit_bytes=VMEM_BYTES
        ),
    )(rows, part_mine, part_theirs, cot, gain, shift, up_bias, down_bias, up, down)


KEY_BLOCKS = 2 * LEN // BLOCK


def rows_seeing(block):
    return pl.ds(max(0, block - 4) * BLOCK, LEN - max(0, block - 4) * BLOCK)


def back_kernel(*refs):
    refs = list(refs)
    take = lambda count: [refs.pop(0) for _ in range(count)]
    grad_part, final_theirs, gain = take(3)
    far_away = take(16)
    pay, pay_in, sums, grad_far, grad_resid, result, grad_logit, feed_sums = take(8)
    afters = take(len(BACK_PIECES))
    written = take(2)
    send_sem, recv_sem, fetch_sem, write_sem = take(4)
    writes = Fetches(write_sem)
    local = take(16)
    grads = {UP: local[0]}
    hidden, cot, resid, out_wide, gates, heads_own, heads_peer, mixed, probs, attended, values, keys, queries, normed, final_mine = local[1:]
    qu, qv, far_rel = (queries.at[pl.ds(start, size)] for start, size in ((0, LEN), (LEN, LEN), (2 * LEN, 2 * LEN)))
    part_in, final_in, given, given_in, grad_low, grad_mixed = take(6)
    grad_out, grad_u, grad_query, grad_keys, grad_values, far_sum, grad_experts = take(7)
    grads.update(zip((DOWN, OUT), take(2)))
    grads[VALUE] = grads[UP].at[..., pl.ds(0, EXPERTS)]
    links, fetches = Links(send_sem, recv_sem), Fetches(fetch_sem)
    loads = [fetches.start(src, dst) for src, dst in zip(far_away, local)]
    up_load = loads.pop(0)
    at = place()
    core, chip = at["core"], at["y"] // 2
    sibling, peer = others_of(at)
    devices = [moved(at, axis, steps) for axis in "xyz" for steps in (1, 2, 3)] + [sibling]
    greet(devices)
    pl.semaphore_wait(pltpu.get_barrier_semaphore(), len(devices))
    parts = [
        links.send(grad_part.at[pl.ds((1 - side) * BLOCK, BLOCK)], part_in.at[pl.ds(side * BLOCK, BLOCK)], sibling)
        for side in range(2)
    ]
    final_copy = links.send(final_theirs, final_in, sibling)

    unused = list(afters)

    def go(pieces):
        stages = []
        for piece in pieces:
            source = columns_of(grads[piece[0]], piece)
            stages.append(stage_for(links, at, piece, 0, source, take, unused.pop(0)))
        launch(stages)
        return stages

    up_load.wait()
    up_stages = go(UP_PIECES)

    def fill(array, left, right, start, width):
        block = dot(left[...], right[:, start : start + width], 0, 0).astype(BF16)
        grads[array][..., pl.ds(start, width)] = block.reshape(lead_shape(LAYOUTS[array]) + (SHAPES[array][0], width))

    wait_for(*loads[:2])
    down_stages = []
    for piece in DOWN_PIECES:
        fill(DOWN, hidden, cot, piece[1], piece[2])
        if piece[3][0] != "y":
            down_stages += go([piece])
    loads[2].wait()
    for copy in parts:
        copy.wait_recv()
    for side in range(2):
        here = slice(side * BLOCK, (side + 1) * BLOCK)
        scaled, inverse = centered(resid[here, :])
        grad = grad_part[here, :].astype(F32) + part_in[here, :].astype(F32)
        above = cot[here, :].astype(F32)
        total = above + norm_back(grad, scaled, inverse, as_row(gain))
        grad_low[here, :] = total.astype(BF16)
        if side == 0:
            grad_resid[...] = total
            feed_sums[0:1, :] = jnp.sum(grad * scaled, axis=0, keepdims=True)
            feed_sums[1:2, :] = jnp.sum(grad, axis=0, keepdims=True)
            feed_sums[2:3, :] = jnp.sum(above, axis=0, keepdims=True)
    wait_for(*loads[3:5])
    grad_mixed[...] = dot(grad_low[...], out_wide[...], 1, 1)
    for side in range(2):
        here = slice(side * BLOCK, (side + 1) * BLOCK)
        gate = gates[(2 + side) * BLOCK : (3 + side) * BLOCK, :]
        totals = []
        for pair in range(2):
            total = jnp.zeros((BLOCK, SLOT), F32)
            for expert in range(E):
                slot = pair * E + expert
                weight = gate[:, 2 * E + slot : 2 * E + slot + 1]
                total += weight * grad_mixed[here, slot * SLOT : (slot + 1) * SLOT]
            totals.append(total)
        given[0, side] = jnp.where(chip == 0, totals[0], totals[1]).astype(BF16)
        given[1, side] = jnp.where(chip == 0, totals[1], totals[0]).astype(BF16)
    arrived = links.send(given.at[1], given_in, peer)
    down_stages += go(DOWN_PIECES[2:])
    forward(up_stages)
    wait_for(*loads[5:8])
    out_stages = []
    for piece in OUT_PIECES:
        fill(OUT, grad_low, mixed, piece[1], piece[2])
        out_stages += go([piece])
    places = spots_of(core, chip)
    for side in range(2):
        grad_out[rows_at(places[side]), :] = given[0, side]
    wait_for(*loads[8:10])
    arrived.wait_recv()
    for side in range(2):
        grad_out[rows_at(places[2 + side]), :] = given_in[side]
    moving = []

    def give(first, held, base):
        for side in range(2):
            pay[first + side] = held[rows_at(places[side] + base), :]
            src = held.at[rows_at(places[2 + side] + base)]
            moving.append(links.send(src, pay_in.at[first + side], peer))

    for block in range(KEY_BLOCKS):
        cols, rows = pl.ds(block * BLOCK, BLOCK), rows_seeing(block)
        grad_values[cols, :] = dot(probs[rows, cols], grad_out[rows, :], 0, 0).astype(BF16)
    give(4, grad_values, 0)
    give(6, grad_values, LEN)
    value_moves = list(moving)
    lane = lax.broadcasted_iota(jnp.int32, (BLOCK, SLOT), 1)
    for side in range(2):
        here = slice(side * BLOCK, (side + 1) * BLOCK)
        gate = gates[(2 + side) * BLOCK : (3 + side) * BLOCK, :]
        heads = two_heads(chip, heads_own[side], heads_peer[side])
        total = jnp.zeros((BLOCK, SLOT), F32)
        for slot in range(2 * E):
            part = grad_mixed[here, slot * SLOT : (slot + 1) * SLOT] * heads[slot // E]
            total += jnp.where(lane == 2 * E + slot, jnp.sum(part, axis=1, keepdims=True), 0.0)
        grad_logit[here, :] = (total * gate * (1.0 - gate)).astype(BF16)
    forward(down_stages)
    wait_for(*loads[10:13])
    blocks = LEN // BLOCK
    sum_u = jnp.zeros((1, SLOT), F32)

    def score_rows(block):
        rows = pl.ds(block * BLOCK, BLOCK)
        width = LEN + (block + 1) * BLOCK
        above = grad_out[rows, :]
        grad_probs = dot(above, values[:width, :], 1, 1)
        inner = jnp.sum(above.astype(F32) * attended[rows, :], axis=1, keepdims=True)
        scores = (probs[rows, :width].astype(F32) * ((grad_probs - inner) * SCALE)).astype(BF16)
        probs[rows, :width] = scores
        part = dot(scores, keys[:width, :])
        grad_u[rows, :] = part
        return jnp.sum(part, axis=0, keepdims=True)

    for block in (0, 1):
        sum_u += score_rows(block)
    forward(out_stages)
    for block in (2, 3):
        sum_u += score_rows(block)
    for block in range(KEY_BLOCKS):
        cols, rows = pl.ds(block * BLOCK, BLOCK), rows_seeing(block)
        grad_keys[cols, :] = dot(probs[rows, cols], qu[rows, :], 0, 0).astype(BF16)
    give(0, grad_keys, 0)
    give(2, grad_keys, LEN)
    far_sum[...] = jnp.zeros_like(far_sum)
    down = lax.broadcasted_iota(jnp.int32, (BLOCK, BLOCK), 0)
    across = lax.broadcasted_iota(jnp.int32, (BLOCK, BLOCK), 1)
    flip = (down + across == BLOCK - 1).astype(F32).astype(BF16)
    sum_v = jnp.zeros((1, SLOT), F32)
    for block in range(blocks):
        rows = pl.ds(block * BLOCK, BLOCK)
        width = LEN + (block + 1) * BLOCK
        first_far = 2 * LEN - width
        far = pltpu.roll(dot(flip, probs[rows, :width]), 0, 1, stride=1, stride_axis=0).astype(BF16)
        turned = dot(flip, far).astype(BF16)
        part = dot(turned, far_rel[first_far:, :])
        far_sum[first_far:, :] += dot(turned, qv[rows, :], 0, 0)
        grad_query[rows, :] = (grad_u[rows, :] + part).astype(BF16)
        sum_v += jnp.sum(part, axis=0, keepdims=True)
    give(8, grad_query, 0)
    sums[0:1, :] = sum_u
    sums[1:2, :] = sum_v
    grad_far[...] = far_sum[...].astype(BF16)
    for copy in value_moves:
        copy.wait_recv()
    for block in range(4):
        rows = slice(block * BLOCK, (block + 1) * BLOCK)
        heads = two_heads(chip, pay[4 + block], pay_in[4 + block])
        for slot in range(2 * E):
            weight = gates[rows, slot : slot + 1]
            grad_experts[rows, slot * SLOT : (slot + 1) * SLOT] = (weight * heads[slot // E]).astype(BF16)
    writes.start(grad_experts, written[0])
    loads[13].wait()
    collect(up_stages)
    for stage in up_stages:
        stage.settle()
    for piece in VALUE_PIECES:
        fill(VALUE, normed, grad_experts, piece[1], piece[2])
    writes.start(grads[VALUE], written[1])
    loads[14].wait()
    final_copy.wait_recv()
    result[...] = (final_mine[...] + final_in[...].astype(F32)).astype(BF16)
    collect(down_stages)
    collect(out_stages)
    for copy in moving[4:]:
        copy.wait_recv()
    wait_for(*writes.copies)
    links.settle()


def back(grad_part, final_theirs, gain, later):
    scratch = []
    for piece in BACK_PIECES:
        scratch += phase_scratch(piece, 0)
    copies = 2 + 1 + 1 + 10 + 6 * len(BACK_PIECES)
    seq = (2 * LEN, SLOT)
    rows = (2 * BLOCK, D)
    outs = [struct((10, BLOCK, SLOT)), struct((10, BLOCK, SLOT)), struct((2, SLOT), F32), struct(seq)]
    outs += [struct((BLOCK, D), F32), struct((BLOCK, D)), struct((2 * BLOCK, SLOT)), struct((8, D), F32)]
    outs += [struct(after_shape(piece, 1)) for piece in BACK_PIECES]
    return pl.pallas_call(
        back_kernel,
        out_shape=outs + [struct((4 * BLOCK, EXPERTS)), struct(full_shape(VALUE))],
        in_specs=[IN_VMEM] * 3 + [ANYWHERE] * len(later),
        out_specs=[IN_VMEM] * len(outs) + [ANYWHERE] * 2,
        scratch_shapes=[
            pltpu.SemaphoreType.DMA((copies,)),
            pltpu.SemaphoreType.DMA((copies,)),
            pltpu.SemaphoreType.DMA((len(later),)),
            pltpu.SemaphoreType.DMA((2,)),
        ]
        + [pltpu.VMEM(operand.shape, operand.dtype) for operand in later]
        + [
            pltpu.VMEM(rows, BF16),
            pltpu.VMEM((BLOCK, D), BF16),
            pltpu.VMEM((2, 2, BLOCK, SLOT), BF16),
            pltpu.VMEM((2, BLOCK, SLOT), BF16),
            pltpu.VMEM(rows, BF16),
            pltpu.VMEM((2 * BLOCK, EXPERTS), F32),
            pltpu.VMEM((LEN, SLOT), BF16),
            pltpu.VMEM((LEN, SLOT), F32),
            pltpu.VMEM((LEN, SLOT), BF16),
            pltpu.VMEM(seq, BF16),
            pltpu.VMEM(seq, BF16),
            pltpu.VMEM(seq, F32),
            pltpu.VMEM((4 * BLOCK, EXPERTS), BF16),
        ]
        + [pltpu.VMEM(full_shape(array), BF16) for array in (DOWN, OUT)]
        + scratch,
        compiler_params=pltpu.CompilerParams(
            collective_id=1, has_side_effects=True, vmem_limit_bytes=VMEM_BYTES
        ),
    )(grad_part, final_theirs, gain, *later)


COUNT_ROW = 2 * H
VECTOR_ROW = 16
UP_BIAS_ROW = VECTOR_ROW + 5 * 8
SMALL_ROWS = UP_BIAS_ROW + FF // SLOT


def lay(target, first, vector):
    for row in range(vector.shape[1] // SLOT):
        target[first + row : first + row + 1, :] = vector[:, row * SLOT : (row + 1) * SLOT]


def close_kernel(*refs):
    refs = list(refs)
    take = lambda count: [refs.pop(0) for _ in range(count)]
    gain, feed_sums, grad_up_bias, bias_sums, counts, pay, pay_in, grad_logit, grad_far = take(9)
    far_away = take(10 + len(EARLY))
    grad_tokens, small_out, down_out = take(3)
    both = dict(zip((UP, OUT, VALUE, KEYS, REST), take(5)))
    send_sem, recv_sem, own_sem, fetch_sem = take(4)
    local = take(10 + len(EARLY))
    grads = {VALUE: local[0]}
    early = local[10:]
    normed, experts, gates, wide, grad_experts, sinus, memory, tokens, grad_resid = local[1:10]
    part, part_in, half_bias, grad_keys, grad_routers = take(5)
    grads.update(zip((KEYS, REST), take(2)))
    totals = dict(zip((UP, DOWN, OUT, VALUE, KEYS, REST), take(6)))
    slots = take(4)
    links, fetches = Links(send_sem, recv_sem), Fetches(fetch_sem)
    loads = [fetches.start(src, dst) for src, dst in zip(far_away, local)]
    value_load = loads.pop(0)
    at = place()
    core, chip = at["core"], at["y"] // 2
    sibling, _ = others_of(at)
    high, low = at["x"] // 2, at["x"] % 2
    stays = (high == low) & (low == core)
    ahead, behind = dict(at), dict(at)
    ahead["x"], ahead["core"] = 2 * core + high, low
    behind["x"], behind["core"] = 2 * low + core, high
    ahead, behind = device_of(ahead), device_of(behind)
    devices = [moved(at, axis, steps) for axis in "xyz" for steps in (1, 2, 3)] + [sibling]
    greet(devices)

    def greet_more():
        greet([ahead, behind])
        pl.semaphore_wait(pltpu.get_barrier_semaphore(), len(devices) + 2)

    pl.when(jnp.logical_not(stays))(greet_more)
    pl.when(stays)(lambda: pl.semaphore_wait(pltpu.get_barrier_semaphore(), len(devices)))

    def begin(jobs):
        stages, later = [], []
        for piece, phase, ref in jobs:
            after = take(1)[0] if phase < 2 else totals[piece[0]].at[:, pl.ds(piece[1], piece[2])]
            stages.append(stage_for(links, at, piece, phase, ref, take, after))
            if phase < 2:
                later.append((piece, phase + 1, after))
        launch(stages)
        return stages, later

    def spread(number, value):
        axis = "xyz"[number]
        here = slots[number].at[at[axis]]
        here[...] = value
        return [links.send(here, here, moved(at, axis, steps)) for steps in (1, 2, 3)]

    def gathered(number, copies):
        for copy in copies:
            copy.wait_recv()
        one = slots[number]
        return (one[0] + one[1]) + (one[2] + one[3])

    def fill(array, right, start):
        width = right.shape[1]
        block = dot(normed[...], right[...], 0, 0).astype(BF16)
        grads[array][..., pl.ds(start, width)] = block.reshape(lead_shape(PLAIN) + (16, width))

    value_load.wait()
    value_stages, value_jobs = begin([(piece, 0, columns_of(grads[VALUE], piece)) for piece in VALUE_PIECES])
    for block in range(4):
        rows = slice(block * BLOCK, (block + 1) * BLOCK)
        key_heads = two_heads(chip, pay[block], pay_in[block])
        if block >= 2:
            query_heads = two_heads(chip, pay[6 + block], pay_in[6 + block])
        for pair in range(2):
            grad_keys[rows, pair * SLOT : (pair + 1) * SLOT] = key_heads[pair].astype(BF16)
            query = query_heads[pair].astype(BF16) if block >= 2 else jnp.zeros((BLOCK, SLOT), BF16)
            grad_keys[rows, (2 + pair) * SLOT : (3 + pair) * SLOT] = query
    loads[0].wait()
    fill(KEYS, grad_keys, 0)
    key_stages, key_jobs = begin([(piece, 0, columns_of(grads[KEYS], piece)) for piece in KEYS_PIECES])
    wait_for(*loads[1:3])
    lane = lax.broadcasted_iota(jnp.int32, (BLOCK, SLOT), 1)
    for block in range(4):
        rows = slice(block * BLOCK, (block + 1) * BLOCK)
        gate = gates[rows, :]
        value_heads = two_heads(chip, pay[4 + block], pay_in[4 + block])
        total = jnp.zeros((BLOCK, SLOT), F32)
        for slot in range(2 * E):
            expert = experts[rows, slot * SLOT : (slot + 1) * SLOT].astype(F32)
            inner = jnp.sum(value_heads[slot // E] * expert, axis=1, keepdims=True)
            total += jnp.where(lane == slot, inner, 0.0)
        total = total * gate * (1.0 - gate)
        if block >= 2:
            total += grad_logit[(block - 2) * BLOCK : (block - 1) * BLOCK, :].astype(F32)
        grad_routers[rows, :] = total.astype(BF16)
    fill(REST, grad_routers, 2 * SLOT)
    loads[5].wait()
    rel = dot(sinus[...], grad_far[...], 0, 0).astype(BF16).reshape(lead_shape(PLAIN) + (16, SLOT))
    blank = jnp.zeros((), BF16)
    grads[REST][..., :SLOT] = jnp.where(chip == 0, rel, blank)
    grads[REST][..., SLOT : 2 * SLOT] = jnp.where(chip == 1, rel, blank)
    rest_stages, rest_jobs = begin([(piece, 0, columns_of(grads[REST], piece)) for piece in REST_PIECES])
    forward(value_stages)
    wait_for(*loads[9:])
    early_stages, early_jobs = begin([(piece, 1, ref) for piece, ref in zip(EARLY, early)])
    wait_for(*loads[3:5])
    halves_in = []
    for block in (1, 3, 0, 2):
        rows = slice(block * BLOCK, (block + 1) * BLOCK)
        total = dot(grad_experts[rows, :], wide[:EXPERTS, :]) + dot(grad_keys[rows, :], wide[KEY_AT:ROUTER_AT, :])
        part[block] = (total + dot(grad_routers[rows, :], wide[ROUTER_AT:, :])).astype(BF16)
        if block % 2 == 1:
            halves_in.append(links.send(part.at[block], part_in.at[block // 2], sibling))
        if block == 3:
            forward(key_stages)
    forward(rest_stages)
    collect(value_stages)
    value_stages, value_jobs = begin(value_jobs)
    collect(key_stages)
    key_stages, key_jobs = begin(key_jobs)
    wait_for(*loads[6:9])
    for copy in halves_in:
        copy.wait_recv()
    gain_sum = jnp.zeros((1, D), F32)
    bias_sum = jnp.zeros((1, D), F32)
    for side, rows in enumerate((memory, tokens)):
        scaled, inverse = centered(rows[...].astype(F32))
        grad = part[2 * side].astype(F32) + part_in[side].astype(F32)
        gain_sum += jnp.sum(grad * scaled, axis=0, keepdims=True)
        bias_sum += jnp.sum(grad, axis=0, keepdims=True)
        if side == 1:
            grad_tokens[...] = grad_resid[...] + norm_back(grad, scaled, inverse, as_row(gain))
    small = small_out
    small[:COUNT_ROW, :] = jnp.zeros((COUNT_ROW, SLOT), F32)
    small[COUNT_ROW:VECTOR_ROW, :] = counts[...]
    for number in range(2):
        small[pl.ds(H * number + 2 * chip + core, 1), :] = bias_sums[number : number + 1, :]
    lay(small, VECTOR_ROW, gain_sum)
    lay(small, VECTOR_ROW + 8, bias_sum)
    for number in range(3):
        lay(small, VECTOR_ROW + 16 + 8 * number, feed_sums[number : number + 1, :])
    small[UP_BIAS_ROW:, :] = jnp.zeros((FF // SLOT, SLOT), F32)
    lay(half_bias, 0, grad_up_bias[...])
    half = FF // 2 // SLOT
    small[pl.ds(pl.multiple_of(UP_BIAS_ROW + core * half, 8), half), :] = half_bias[...]
    copies = spread(0, small[...])
    forward(early_stages)
    collect(rest_stages)
    rest_stages, rest_jobs = begin(rest_jobs)
    collect(value_stages)
    value_stages, value_jobs = begin(value_jobs)
    collect(key_stages)
    key_stages, key_jobs = begin(key_jobs)
    copies = spread(1, gathered(0, copies))
    collect(early_stages)
    early_stages, early_jobs = begin(early_jobs)
    collect(rest_stages)
    rest_stages, rest_jobs = begin(rest_jobs)
    copies = spread(2, gathered(1, copies))
    collect(early_stages)
    last = []
    away = links.prepared(totals[DOWN], down_out, ahead)
    here = pltpu.make_async_copy(totals[DOWN], down_out, own_sem)
    pl.when(jnp.logical_not(stays))(away.start)
    pl.when(stays)(here.start)

    def exchange(arrays):
        for array in arrays:
            other = pl.ds(pl.multiple_of((1 - core) * 8, 8), 8)
            last.append(links.send(totals[array].at[other], both[array].at[core], sibling))
            both[array][core] = totals[array][pl.ds(pl.multiple_of(core * 8, 8), 8), :]

    exchange((UP, OUT))
    collect(value_stages)
    collect(key_stages)
    exchange((VALUE, KEYS))
    collect(rest_stages)
    exchange((REST,))
    pair = slots[3]
    pair[core] = gathered(2, copies)
    last.append(links.send(pair.at[core], pair.at[core], sibling))
    for copy in last:
        copy.wait_recv()
    small_out[...] = pair[0] + pair[1]
    pl.when(jnp.logical_not(stays))(away.wait)
    pl.when(stays)(here.wait)
    for copy in links.made:
        if copy is not away:
            copy.wait_send()


def close(gain, feed_sums, grad_up_bias, bias_sums, counts, pay, pay_in, grad_logit, grad_far, later):
    scratch = []
    copies = 2 + 9 + 1 + 1 + 5

    def round_of(pieces, phase):
        nonlocal copies
        for piece in pieces:
            if phase < 2:
                scratch.append(pltpu.VMEM(after_shape(piece, phase + 1), BF16))
            scratch.extend(phase_scratch(piece, phase))
            copies += copies_of(piece, phase)

    round_of(VALUE_PIECES, 0)
    round_of(KEYS_PIECES, 0)
    round_of(REST_PIECES, 0)
    round_of(EARLY, 1)
    round_of(VALUE_PIECES + KEYS_PIECES, 1)
    round_of(REST_PIECES, 1)
    round_of(VALUE_PIECES + KEYS_PIECES, 2)
    round_of(EARLY, 2)
    round_of(REST_PIECES, 2)
    outs = [struct((BLOCK, D), F32), struct((SMALL_ROWS, SLOT), F32), struct(SHAPES[DOWN], F32)]
    outs += [struct((2, 8, SHAPES[array][1]), F32) for array in (UP, OUT, VALUE, KEYS, REST)]
    return pl.pallas_call(
        close_kernel,
        out_shape=outs,
        in_specs=[IN_VMEM] * 9 + [ANYWHERE] * len(later),
        out_specs=[IN_VMEM] * len(outs),
        scratch_shapes=[
            pltpu.SemaphoreType.DMA((copies,)),
            pltpu.SemaphoreType.DMA((copies,)),
            pltpu.SemaphoreType.DMA,
            pltpu.SemaphoreType.DMA((len(later),)),
        ]
        + [pltpu.VMEM(operand.shape, operand.dtype) for operand in later]
        + [
            pltpu.VMEM((4, BLOCK, D), BF16),
            pltpu.VMEM((2, BLOCK, D), BF16),
            pltpu.VMEM((FF // 2 // SLOT, SLOT), F32),
            pltpu.VMEM((4 * BLOCK, 4 * SLOT), BF16),
            pltpu.VMEM((4 * BLOCK, SLOT), BF16),
        ]
        + [pltpu.VMEM(full_shape(array), BF16) for array in (KEYS, REST)]
        + [pltpu.VMEM(SHAPES[array], F32) for array in (UP, DOWN, OUT, VALUE, KEYS, REST)]
        + [pltpu.VMEM((4, SMALL_ROWS, SLOT), F32)] * 3
        + [pltpu.VMEM((2, SMALL_ROWS, SLOT), F32)]
        + scratch,
        compiler_params=pltpu.CompilerParams(
            collective_id=2, has_side_effects=True, vmem_limit_bytes=VMEM_BYTES
        ),
    )(gain, feed_sums, grad_up_bias, bias_sums, counts, pay, pay_in, grad_logit, grad_far, *later)


FRONT_OUTS = (
    ((2 * BLOCK, D), BF16),
    ((2 * BLOCK, D), BF16),
    ((WIDE, D), BF16),
    ((EXPERTS, D), BF16),
    ((4 * BLOCK, D), BF16),
    ((4 * BLOCK, EXPERTS), BF16),
    ((4 * BLOCK, SLOT), F32),
    ((2 * LEN, SLOT), BF16),
    ((2 * LEN, SLOT), BF16),
    ((4 * LEN, SLOT), BF16),
    ((LEN, SLOT), F32),
    ((LEN, 2 * LEN), BF16),
    ((2, BLOCK, SLOT), BF16),
    ((2, BLOCK, SLOT), BF16),
    ((2 * BLOCK, EXPERTS), BF16),
    ((2 * BLOCK, D), BF16),
    ((2 * BLOCK, D), BF16),
    ((2 * LEN, D), BF16),
    ((8, SLOT), F32),
)
FRONT_FETCHES = 3 + 2 * E * 2 + 2 * 2 + 1


def front_kernel(*refs):
    refs = list(refs)
    take = lambda count: [refs.pop(0) for _ in range(count)]
    (mem_len,) = take(1)
    gain, shift, value_route, out_route, bias_u, bias_v, value_router, out_router, sin_coarse, cos_coarse, sin_fine, cos_fine = take(12)
    memory, tokens, cotangent, value_weight, key_weight, query_weight, rel_weight, out_weight = take(8)
    outs = take(len(FRONT_OUTS))
    kept = take(len(FRONT_OUTS))
    tok, cot, wide, out_wide, normed, experts, gates, keys, values, queries, attended, probs, heads_own, heads_peer, mixed, part, part_in, sinus, counts = kept
    send_sem, recv_sem, fetch_sem, out_sem = take(4)
    mem, routes, routes_in, turned, rel, full, pay, pay_in, back = take(9)
    links, fetches, writes = Links(send_sem, recv_sem), Fetches(fetch_sem), Fetches(out_sem)
    at = place()
    core, chip = at["core"], at["y"] // 2
    peer = moved(at, "y", 2)
    sibling = dict(at)
    sibling["core"] = 1 - core
    sibling = device_of(sibling)
    mine, theirs = pl.ds(0, BLOCK), pl.ds(BLOCK, BLOCK)
    row_loads = [
        fetches.start(memory, mem.at[mine]),
        fetches.start(tokens, tok.at[mine]),
        fetches.start(cotangent, cot.at[mine]),
    ]

    def slots_from(target, slot, source, start):
        src = source.at[pl.ds(pl.multiple_of(start, 16), DH)]
        return fetches.start(src, target.at[pl.ds(slot, DH)])

    wide_loads, out_loads = [], []
    for pair in range(2):
        head = 2 * pair + core
        for expert in range(E):
            slot = (pair * E + expert) * SLOT
            wide_loads.append(slots_from(wide, slot, value_weight, (head * E + expert) * DH))
        wide_loads.append(slots_from(wide, KEY_AT + pair * SLOT, key_weight, head * DH))
        wide_loads.append(slots_from(wide, QUERY_AT + pair * SLOT, query_weight, head * DH))
    rel_load = slots_from(rel, 0, rel_weight, (2 * chip + core) * DH)
    for pair in range(2):
        head = 2 * pair + core
        for expert in range(E):
            slot = (pair * E + expert) * SLOT
            out_loads.append(slots_from(out_wide, slot, out_weight, (head * E + expert) * DH))
    for number in range(H):
        for kind in range(2):
            routes[8 * kind + 2 * number : 8 * kind + 2 * number + 2, :] = value_route[kind, number]
        routes[16 + 2 * number : 18 + 2 * number, :] = out_route[number]
    greet([sibling, peer])
    pl.semaphore_wait(pltpu.get_barrier_semaphore(), 2)
    mem_copy = links.send(memory, mem.at[theirs], sibling)
    tok_copy = links.send(tokens, tok.at[theirs], sibling)
    route_copy = links.send(routes, routes_in, sibling)
    cot_copy = links.send(cotangent, cot.at[theirs], sibling)
    blank = jnp.zeros((SLOT - DH, D), BF16)
    for slot in range(DH, EXPERTS, SLOT):
        out_wide[slot : slot + SLOT - DH, :] = blank
    for slot in range(DH, ROUTER_AT, SLOT):
        wide[slot : slot + SLOT - DH, :] = blank
    rel[DH:, :] = blank
    routers = []
    for router in (value_router, out_router):
        for pair in range(2):
            one = router[2 * pair * E : (2 * pair + 1) * E, :].astype(F32)
            two = router[(2 * pair + 1) * E : (2 * pair + 2) * E, :].astype(F32)
            routers.append(jnp.where(core == 0, one, two))
    routers.append(jnp.zeros((SLOT - 4 * E, D), F32))
    wide[ROUTER_AT:, :] = jnp.concatenate(routers, axis=0).astype(BF16)
    lane = lax.broadcasted_iota(jnp.int32, (BLOCK, SLOT), 1)
    turned[0] = routes[...].astype(F32).T.astype(jnp.int32)
    slot_of = lax.broadcasted_iota(jnp.int32, (2 * H, SLOT), 1) - lax.broadcasted_iota(jnp.int32, (2 * H, SLOT), 0) // 2 * E
    counted = jnp.zeros((1, SLOT), F32)
    for first in (0, 8, 16):
        for expert in range(E):
            named = (routes[first : first + 2 * H, :] == expert).astype(F32)
            number = jnp.sum(named, axis=1, keepdims=True)
            at_slot = slot_of == expert + (H * E if first == 16 else 0)
            counted += jnp.sum(jnp.where(at_slot, number, 0.0), axis=0, keepdims=True)
    counts[...] = jnp.zeros_like(counts)
    counts[0:1, :] = counted
    wait_for(*row_loads[:2])

    def normalize(block):
        rows = slice(block * BLOCK, (block + 1) * BLOCK)
        given = (mem, tok)[block // 2][(block % 2) * BLOCK : (block % 2 + 1) * BLOCK, :]
        scaled, _ = centered(given.astype(F32))
        normed[rows, :] = (scaled * as_row(gain) + as_row(shift)).astype(BF16)

    moving = []

    def project(block, buffer):
        rows = slice(block * BLOCK, (block + 1) * BLOCK)
        space = full.at[buffer]
        space[...] = dot(normed[rows, :], wide[...], 1, 1)
        experts[rows, :] = space[:, :EXPERTS].astype(BF16)
        named = turned[block % 2]
        token = block // 2
        chosen = chosen_lanes(named, 2 * H * token, core, lane, 0) & (lane < 2 * E)
        if token:
            chosen = chosen | chosen_lanes(named, 4 * H, core, lane, 2 * E)
        gate = jnp.where(chosen, jax.nn.sigmoid(space[:, ROUTER_AT:WIDE]), 0.0)
        gates[rows, :] = gate
        for pair in range(2):
            total = jnp.zeros((BLOCK, SLOT), F32)
            for expert in range(E):
                slot = pair * E + expert
                total += gate[:, slot : slot + 1] * space[:, slot * SLOT : (slot + 1) * SLOT]
            pay[pair, block] = space[:, KEY_AT + pair * SLOT : KEY_AT + (pair + 1) * SLOT].astype(BF16)
            pay[pair, 4 + block] = total.astype(BF16)
            if token:
                pay[pair, 6 + block] = space[:, QUERY_AT + pair * SLOT : QUERY_AT + (pair + 1) * SLOT].astype(BF16)
        for segment in (block, 4 + block) + ((6 + block,) if token else ()):
            moving.append(links.send(pay.at[1 - chip, segment], pay_in.at[segment], peer))

    normalize(0)
    normalize(2)
    wait_for(*wide_loads)
    project(0, 0)
    project(2, 1)
    mem_copy.wait_recv()
    normalize(1)
    tok_copy.wait_recv()
    normalize(3)
    route_copy.wait_recv()
    turned[1] = routes_in[...].astype(F32).T.astype(jnp.int32)
    project(1, 0)
    project(3, 1)
    for number in (0, 2, 4, 5, 6):
        writes.start(kept[number], outs[number])
    sin_b, cos_b = sin_fine[...], cos_fine[...]
    for number in range(32):
        sin_a, cos_a = sin_coarse[number : number + 1, :], cos_coarse[number : number + 1, :]
        rows = slice(64 * number, 64 * (number + 1))
        sinus[rows, : D // 2] = (sin_a * cos_b + cos_a * sin_b).astype(BF16)
        sinus[rows, D // 2 :] = (cos_a * cos_b - sin_a * sin_b).astype(BF16)
    writes.start(kept[17], outs[17])
    writes.start(kept[18], outs[18])
    rel_load.wait()
    far_rel = queries.at[pl.ds(2 * LEN, 2 * LEN)]
    far_rel[...] = dot(sinus[...], rel[...], 1, 1).astype(BF16)
    places = spots_of(core, chip)
    head = 2 * chip + core

    def own_head(bias):
        row = bias[...].astype(F32).reshape(1, H * DH)
        total = jnp.zeros((1, DH), F32)
        for number in range(H):
            total += jnp.where(head == number, row[:, number * DH : (number + 1) * DH], 0.0)
        return jnp.concatenate([total, jnp.zeros((1, SLOT - DH), F32)], axis=1)

    head_u, head_v = own_head(bias_u), own_head(bias_v)
    qu, qv = queries.at[pl.ds(0, LEN)], queries.at[pl.ds(LEN, LEN)]

    def assemble(number, segment_of):
        side = number % 2
        start = places[number]
        keys[rows_at(start), :] = segment_of(side)
        keys[rows_at(start + LEN), :] = segment_of(2 + side)
        values[rows_at(start), :] = segment_of(4 + side)
        values[rows_at(start + LEN), :] = segment_of(6 + side)
        query = segment_of(8 + side).astype(F32)
        qu[rows_at(start), :] = (query + head_u).astype(BF16)
        qv[rows_at(start), :] = (query + head_v).astype(BF16)

    for number in range(2):
        assemble(number, lambda segment: pay[chip, segment])
    for copy in moving:
        copy.wait_recv()
    for number in range(2, 4):
        assemble(number, lambda segment: pay_in[segment])
    for number in (7, 8, 9):
        writes.start(kept[number], outs[number])
    mem_at = lax.broadcasted_iota(jnp.int32, (1, LEN), 1)
    mem_mask = jnp.where(mem_at >= LEN - mem_len[0], 0.0, MASKED)
    down = lax.broadcasted_iota(jnp.int32, (BLOCK, BLOCK), 0)
    across = lax.broadcasted_iota(jnp.int32, (BLOCK, BLOCK), 1)
    own_mask = jnp.where(across <= down, 0.0, MASKED)
    for block in range(LEN // BLOCK):
        attend(block, mem_mask, own_mask, qu, qv, keys, values, far_rel, attended, probs)
    for side in range(2):
        heads_own[side] = attended[rows_at(places[side]), :].astype(BF16)
        back[side] = attended[rows_at(places[2 + side]), :].astype(BF16)
    returned = links.send(back, heads_peer, peer)
    for number in (10, 11, 12):
        writes.start(kept[number], outs[number])
    wait_for(*out_loads)
    writes.start(kept[3], outs[3])
    returned.wait_recv()
    writes.start(kept[13], outs[13])
    sent = []
    for side in range(2):
        heads = two_heads(chip, heads_own[side], heads_peer[side])
        rows = slice(side * BLOCK, (side + 1) * BLOCK)
        gate = gates[(2 + side) * BLOCK : (3 + side) * BLOCK, :]
        for slot in range(2 * E):
            weight = gate[:, 2 * E + slot : 2 * E + slot + 1]
            mixed[rows, slot * SLOT : (slot + 1) * SLOT] = (weight * heads[slot // E]).astype(BF16)
        part[rows, :] = dot(mixed[rows, :], out_wide[...]).astype(BF16)
        other = pl.ds((1 - side) * BLOCK, BLOCK)
        sent.append(links.send(part.at[pl.ds(side * BLOCK, BLOCK)], part_in.at[other], sibling))
    writes.start(kept[14], outs[14])
    writes.start(kept[15], outs[15])
    row_loads[2].wait()
    cot_copy.wait_recv()
    writes.start(kept[1], outs[1])
    for copy in sent:
        copy.wait_recv()
    writes.start(kept[16], outs[16])
    wait_for(*writes.copies)
    for copy in links.made:
        copy.wait_send()


def front(mem_len, small, large):
    copies = 4 + 10 + 1 + 2
    return pl.pallas_call(
        front_kernel,
        out_shape=[struct(*out) for out in FRONT_OUTS],
        in_specs=[IN_SMEM] + [IN_VMEM] * len(small) + [ANYWHERE] * len(large),
        out_specs=[ANYWHERE] * len(FRONT_OUTS),
        scratch_shapes=[pltpu.VMEM(*out) for out in FRONT_OUTS]
        + [
            pltpu.SemaphoreType.DMA((copies,)),
            pltpu.SemaphoreType.DMA((copies,)),
            pltpu.SemaphoreType.DMA((FRONT_FETCHES,)),
            pltpu.SemaphoreType.DMA((len(FRONT_OUTS),)),
            pltpu.VMEM((2 * BLOCK, D), BF16),
            pltpu.VMEM((6 * H, BLOCK), jnp.int32),
            pltpu.VMEM((6 * H, BLOCK), jnp.int32),
            pltpu.VMEM((2, BLOCK, 6 * H), jnp.int32),
            pltpu.VMEM((SLOT, D), BF16),
            pltpu.VMEM((2, BLOCK, WIDE), F32),
            pltpu.VMEM((2, 10, BLOCK, SLOT), BF16),
            pltpu.VMEM((10, BLOCK, SLOT), BF16),
            pltpu.VMEM((2, BLOCK, SLOT), BF16),
        ],
        compiler_params=pltpu.CompilerParams(
            collective_id=0, has_side_effects=True, vmem_limit_bytes=VMEM_BYTES
        ),
    )(mem_len, *small, *large)


ARRANGED = (
    ((BLOCK, D), BF16),
    ((BLOCK, D), F32),
    ((8,), F32),
    ((8,), F32),
    ((8, H * DH), F32),
    ((8, H * DH), F32),
    ((8, H * DH), F32),
    ((H * DH,), F32),
    ((H * DH,), F32),
    ((8, H * E), F32),
    ((8, H * E * DH), F32),
    ((8, H * E), F32),
    ((8, H * E * DH), F32),
    ((8,), F32),
    ((8,), F32),
    ((8, FF), F32),
    ((32,), F32),
    ((32, D), F32),
    ((8,), F32),
    ((2, H, E), jnp.int32),
)


def arrange_kernel(result_in, tokens_in, small, down_in, up, out, value, keys, rest, *outs):
    (
        result,
        grad_tokens,
        attn_gain,
        attn_bias,
        grad_query,
        grad_key,
        grad_rel,
        grad_bias_u,
        grad_bias_v,
        value_router,
        grad_value,
        out_router,
        grad_out,
        ffn_gain,
        ffn_bias,
        grad_up,
        up_bias,
        grad_down,
        down_bias,
        counts,
    ) = outs
    result[...] = result_in[...]
    grad_tokens[...] = tokens_in[...]
    grad_down[...] = down_in[...]
    grad_up[:, : FF // 2] = up[0]
    grad_up[:, FF // 2 :] = up[1]
    for head in range(H):
        core, pair = head % 2, head // 2
        for expert in range(E):
            slot = (pair * E + expert) * SLOT
            start = (head * E + expert) * DH
            grad_out[:, start : start + DH] = out[core, :, slot : slot + DH]
            grad_value[:, start : start + DH] = value[core, :, slot : slot + DH]
        start = head * DH
        for target, source, slot in ((grad_key, keys, 0), (grad_query, keys, 2 * SLOT), (grad_rel, rest, 0)):
            slot += pair * SLOT
            target[:, start : start + DH] = source[core, :, slot : slot + DH]
        for kind, target in enumerate((value_router, out_router)):
            at = 2 * SLOT + (2 * kind + pair) * E
            target[:, head * E : (head + 1) * E] = rest[core, :, at : at + E]
    device = lax.axis_index("dp") * 4 + lax.axis_index("seq")

    def share(target, first, size):
        per_row = SLOT // size
        row = small[pl.ds(first + device // per_row, 1), :]
        row = pltpu.roll(row, SLOT - device % per_row * size, 1)
        target[...] = row[:, :size].reshape(size)

    for number, target in enumerate((attn_gain, attn_bias, ffn_gain, ffn_bias, down_bias)):
        share(target, VECTOR_ROW + 8 * number, 8)
    share(up_bias, UP_BIAS_ROW, 32)
    for first, target in ((0, grad_bias_u), (H, grad_bias_v)):
        heads = [small[first + head : first + head + 1, :DH] for head in range(H)]
        target[...] = jnp.concatenate(heads, axis=1).reshape(H * DH)
    row = (small[COUNT_ROW : COUNT_ROW + 1, :] + 0.5).astype(jnp.int32)
    for kind in range(2):
        for head in range(H):
            at = (kind * H + head) * E
            counts[kind, head : head + 1, :] = row[:, at : at + E]


def arrange(*operands):
    return local_call(arrange_kernel, [struct(*out) for out in ARRANGED], vmem=len(operands))(*operands)


def angle_tables():
    frequency = jnp.exp(jnp.arange(D // 2, dtype=jnp.int32).astype(F32) * (-2.0 * math.log(10000.0) / D))
    coarse = (64 * (31 - jnp.arange(32, dtype=jnp.int32))).astype(F32)[:, None] * frequency
    fine = (63 - jnp.arange(64, dtype=jnp.int32)).astype(F32)[:, None] * frequency
    return jnp.sin(coarse), jnp.cos(coarse), jnp.sin(fine), jnp.cos(fine)


def body(
    tokens,
    memory,
    cotangent,
    mem_len,
    value_route,
    output_route,
    attn_norm_gain,
    attn_norm_bias,
    query_weight,
    key_weight,
    rel_weight,
    bias_u,
    bias_v,
    value_router,
    value_weight,
    out_router,
    out_weight,
    ffn_norm_gain,
    ffn_norm_bias,
    up_weight,
    up_bias,
    down_weight,
    down_bias,
):
    tokens, memory, cotangent = tokens[0], memory[0], cotangent[0]
    (
        tokens_pair,
        cot,
        wide,
        out_wide,
        normed,
        experts,
        gates,
        keys,
        values,
        queries,
        attended,
        probs,
        heads_own,
        heads_peer,
        mixed,
        out_part,
        out_part_in,
        sinus,
        counts,
    ) = front(
        mem_len,
        [
            attn_norm_gain,
            attn_norm_bias,
            value_route[0].transpose(0, 2, 3, 1),
            output_route[0].transpose(1, 2, 0),
            bias_u,
            bias_v,
            value_router.T,
            out_router.T,
            *angle_tables(),
        ],
        [memory, tokens, cotangent, value_weight.T, key_weight.T, query_weight.T, rel_weight.T, out_weight],
    )
    final_mine, final_theirs, norm_part, grad_up_bias, *first, resid, hidden, grad_up = feed(
        tokens_pair,
        out_part,
        out_part_in,
        cot,
        ffn_norm_gain,
        ffn_norm_bias,
        up_bias,
        down_bias,
        up_weight,
        down_weight,
    )
    pay, pay_in, bias_sums, grad_far, grad_resid, result, grad_logit, feed_sums, *early = back(
        norm_part,
        final_theirs,
        ffn_norm_gain,
        [
            grad_up,
            hidden,
            cot,
            resid,
            out_wide,
            gates,
            heads_own,
            heads_peer,
            mixed,
            probs,
            attended,
            values,
            keys,
            queries,
            normed,
            final_mine,
        ],
    )
    *early, grad_experts, grad_value = first + early
    grad_tokens, small_sum, grad_down, up_both, out_both, value_both, keys_both, rest_both = close(
        attn_norm_gain,
        feed_sums,
        grad_up_bias,
        bias_sums,
        counts,
        pay,
        pay_in,
        grad_logit,
        grad_far,
        [grad_value, normed, experts, gates, wide, grad_experts, sinus, memory, tokens, grad_resid, *early],
    )
    outs = arrange(
        result, grad_tokens, small_sum, grad_down, up_both, out_both, value_both, keys_both, rest_both
    )
    outs = list(outs)
    outs[0], outs[1], outs[12] = outs[0][None], outs[1][None], outs[12].T
    return tuple(outs)


def solution(mesh):
    in_specs = (
        P("dp", "seq", None),
        P("dp", "seq", None),
        P("dp", "seq", None),
        P("dp"),
        P("dp", None, "seq", None, None),
        P("dp", "seq", None, None),
        P(),
        P(),
        P(),
        P(),
        P(),
        P(),
        P(),
        P(),
        P(),
        P(),
        P(),
        P(),
        P(),
        P(),
        P(),
        P(),
        P(),
    )
    out_specs = (
        P("dp", "seq", None),
        P("dp", "seq", None),
        P(("dp", "seq")),
        P(("dp", "seq")),
        P(("dp", "seq"), None),
        P(("dp", "seq"), None),
        P(("dp", "seq"), None),
        P(),
        P(),
        P(("dp", "seq"), None),
        P(("dp", "seq"), None),
        P(("dp", "seq"), None),
        P(None, ("dp", "seq")),
        P(("dp", "seq")),
        P(("dp", "seq")),
        P(("dp", "seq"), None),
        P(("dp", "seq")),
        P(("dp", "seq"), None),
        P(("dp", "seq")),
        P(),
    )
    return jax.shard_map(body, mesh=mesh, in_specs=in_specs, out_specs=out_specs, check_vma=False)
```
